32 devices in a mesh: crops: 2 (over y), row: 4 (over z), col: 2 (over x), seq: 2 (over core).
Axes of the slice: x: 2, y: 2, z: 4, core: 2. Of those that a mesh axis runs over, the one named last changes fastest.
Arguments:
- homolog_embedding: bfloat16 [512, 64, 256], P(('crops', 'seq'), ('col', 'row')), parts along dimension 0, may hold values from -6 to 6
- homolog_cell_occupancy: int32 [512, 64], P(('crops', 'seq'), ('col', 'row')), parts along dimension 0, may hold values from 0 to 1, as said below
- peptide_occupancy: int32 [128], P(('crops', 'col', 'row')), parts along dimension 0, may hold values from 0 to 1
- standardize_multiplier: float32 [256], replicated, may hold values from 0.5 to 1.5
- standardize_addend: float32 [256], replicated, may hold values from -3 to 3
- lhs_linear_map: bfloat16 [256, 32], replicated, may hold values from -0.375 to 0.375
- lhs_linear_constant: float32 [32], replicated, may hold values from -3 to 3
- rhs_linear_map: bfloat16 [256, 32], replicated, may hold values from -0.375 to 0.375
- rhs_linear_constant: float32 [32], replicated, may hold values from -3 to 3
- closing_linear_map: bfloat16 [1024, 128], replicated, may hold values from -0.375 to 0.375
- closing_linear_constant: float32 [128], replicated, may hold values from -40 to 40
Outputs:
- pair_update: bfloat16 [128, 64, 128], P(('crops', 'row'), ('col', 'seq')), parts along dimension 0
The draws below stay inside these ranges and needn't reach their ends.
There are 2 independent parts, one for each index of `crops`. The reference program is written for one: setup_inputs(seed, part) draws one part's arguments, and reference() takes and returns one part's arrays. A program takes and returns all parts, laid end to end along the dimension named above; an argument that names none is the same for every part. Nothing has to cross between parts.
Inputs may be any that keep to these rules, and one draw needn't show every extreme that they name: `homolog_cell_occupancy`: sequence 0 is present at every residue.
All inputs are finite; a program needn't handle non-finite values.
Results may differ from the reference program's by a relative error of at most 0.003.
Values may be sent and summed in bfloat16 or wider, within the bound.
No kernel may reach another device: no remote copies, remote signals or barrier semaphores. Data moves between devices by JAX's collectives and lax.ppermute only.
A program may use at most 128 MiB of HBM per device.

```python
import math
import jax
import jax.numpy as jnp
from jax import lax

SIGNAL_SPAN = 256
HIDDEN_SPAN = 32
CZ = 128
HOMOLOG_TOTAL = 256
WINDOW_SPAN = 64


def draw_homolog_cell_occupancy(key, part):
    key = jax.random.fold_in(key, 11)
    quantile_marks = jax.random.randint(key, (HOMOLOG_TOTAL, WINDOW_SPAN), 0, 1000)
    homolog_position = jnp.arange(HOMOLOG_TOTAL, dtype=jnp.int32)[:, None]
    cutoff_level = 900 - 600 * homolog_position // max(HOMOLOG_TOTAL - 1, 1)
    present = (quantile_marks < cutoff_level).astype(jnp.int32)
    present = jnp.where(homolog_position == 0, 1, present)
    return present.astype(jnp.int32)


def draw_peptide_occupancy(key, part):
    key = jax.random.fold_in(key, 23)
    order_key = jax.random.fold_in(key, 1)
    level_key = jax.random.fold_in(key, 2)
    ranking = jax.random.permutation(order_key, WINDOW_SPAN).astype(jnp.int32)
    marks = jax.random.randint(level_key, (WINDOW_SPAN,), 0, 1000)
    present = jnp.where(ranking == 0, 0, jnp.where(ranking == WINDOW_SPAN - 1, 1, (marks >= 250).astype(jnp.int32)))
    return present.astype(jnp.int32)


def block_levels(rng, dims, pieces, least, top_value):
    level = 1.0
    for axis_at, parts in pieces:
        heights = jax.random.uniform(jax.random.fold_in(jax.random.fold_in(rng, 6), axis_at), (parts,), jnp.float32, least / len(pieces), top_value / len(pieces))
        level = level * jnp.repeat(jnp.exp(heights), dims[axis_at] // parts).reshape((-1,) + (1,) * (len(dims) - 1 - axis_at))
    return level


def normal_values(rng, extent, scale, most, cuts=(), kind=jnp.bfloat16):
    array = jax.random.normal(rng, extent, jnp.float32) * scale
    if len(cuts) > 0:
        array = block_levels(rng, extent, cuts, -0.22, 0.18) * array
    return jnp.clip(array, min=-most, max=most).astype(kind)


def setup_inputs(seed: int = 0, part: int = 0) -> dict:
    key_list = jax.random.split(jax.random.key(seed), 12)
    part_splits = jax.random.split(jax.random.fold_in(key_list[11], part), 12)
    return {
        "homolog_embedding": normal_values(part_splits[0], (HOMOLOG_TOTAL, WINDOW_SPAN, SIGNAL_SPAN), 1.0, 6.0, ((0, 2), (1, 8))),
        "homolog_cell_occupancy": draw_homolog_cell_occupancy(jax.random.fold_in(jax.random.fold_in(key_list[11], part), 71), part),
        "peptide_occupancy": draw_peptide_occupancy(jax.random.fold_in(jax.random.fold_in(key_list[11], part), 71), part),
        "standardize_multiplier": jnp.clip(jax.random.uniform(key_list[3], (SIGNAL_SPAN,), jnp.float32, 0.5, 1.5), 0.5, 1.5),
        "standardize_addend": normal_values(key_list[4], (SIGNAL_SPAN,), 0.5, 3.0, (), jnp.float32),
        "lhs_linear_map": normal_values(key_list[5], (SIGNAL_SPAN, HIDDEN_SPAN), SIGNAL_SPAN ** -0.5, 0.375),
        "lhs_linear_constant": normal_values(key_list[6], (HIDDEN_SPAN,), 0.5, 3.0, (), jnp.float32),
        "rhs_linear_map": normal_values(key_list[7], (SIGNAL_SPAN, HIDDEN_SPAN), SIGNAL_SPAN ** -0.5, 0.375),
        "rhs_linear_constant": normal_values(key_list[8], (HIDDEN_SPAN,), 0.5, 3.0, (), jnp.float32),
        "closing_linear_map": normal_values(key_list[9], (HIDDEN_SPAN * HIDDEN_SPAN, CZ), (HIDDEN_SPAN * 8) ** -0.5, 0.375),
        "closing_linear_constant": normal_values(key_list[10], (CZ,), 8.0, 40.0, (), jnp.float32),
    }


def project_side(normed, occupied_indicator, weight, bias):
    seq_count, res_count, width = normed.shape
    report_text = jnp.dot(normed.reshape(seq_count * res_count, width), weight, preferred_element_type=jnp.float32)
    report_text = (report_text + bias).reshape(seq_count, res_count, -1) * occupied_indicator[:, :, None]
    return report_text.astype(jnp.bfloat16)

def reference(homolog_embedding, homolog_cell_occupancy, peptide_occupancy, standardize_multiplier, standardize_addend, lhs_linear_map, lhs_linear_constant, rhs_linear_map, rhs_linear_constant, closing_linear_map, closing_linear_constant):
    occupied_indicator = (homolog_cell_occupancy * peptide_occupancy[None, :]).astype(jnp.float32)
    report_text = homolog_embedding.astype(jnp.float32)
    average = lax.optimization_barrier(jnp.mean(report_text, axis=-1, keepdims=True))
    spread = lax.optimization_barrier(jnp.mean(jnp.square(report_text - average), axis=-1, keepdims=True))
    normed = ((report_text - average) * lax.rsqrt(spread + 1e-05) * standardize_multiplier + standardize_addend).astype(jnp.bfloat16)
    left = project_side(normed, occupied_indicator, lhs_linear_map, lhs_linear_constant)
    right = project_side(normed, occupied_indicator, rhs_linear_map, rhs_linear_constant)
    counts = jnp.dot(occupied_indicator.T, occupied_indicator, precision=lax.Precision.HIGHEST)
    weight_f32 = closing_linear_map.astype(jnp.float32)
    right_f32 = right.astype(jnp.float32)
    res_count = left.shape[1]
    block_rows = math.gcd(res_count, 8)

    def project_block(first_row):
        left_block = lax.dynamic_slice_in_dim(left, first_row, block_rows, 1).astype(jnp.float32)
        outer_prod = jnp.einsum('sic,sjd->ijcd', left_block, right_f32)
        flattened = outer_prod.reshape(block_rows * res_count, -1)
        result = jnp.dot(flattened, weight_f32, precision=lax.Precision.HIGHEST)
        return result.reshape(block_rows, res_count, -1)
    starts = (jnp.arange(res_count // block_rows) * block_rows).astype(jnp.int32)
    projected = lax.map(project_block, starts).reshape(res_count, res_count, -1)
    return ((projected + closing_linear_constant) / jnp.maximum(counts, 1.0)[:, :, None]).astype(jnp.bfloat16)
```

```python
import math

import jax
import jax.numpy as jnp
from jax import lax
from jax.experimental import pallas as pl
from jax.experimental.pallas import tpu as pltpu
from jax.sharding import PartitionSpec as P

GROUP = ("row", "col", "seq")
NT = (((1,), (1,)), ((), ()))
MASK_ROWS = 16


def from_root(x, axis, root):
    mine = lax.axis_index(axis) == root
    return lax.psum(jnp.where(mine, x, jnp.zeros_like(x)), axis)


def project_side(normed, occupied_indicator, weight, bias):
    seq_count, res_count, width = normed.shape
    report_text = jnp.dot(
        normed.reshape(seq_count * res_count, width), weight, preferred_element_type=jnp.float32
    )
    report_text = (report_text + bias).reshape(seq_count, res_count, -1) * occupied_indicator[
        :, :, None
    ]
    return report_text.astype(jnp.bfloat16)


def pair_rows(left, right, closing_linear_map):
    row_count = left.shape[1]
    col_count = right.shape[1]
    block_rows = math.gcd(row_count, max(1, 512 // col_count))
    weight_f32 = closing_linear_map.astype(jnp.float32)

    def project_block(first_row):
        left_block = lax.dynamic_slice_in_dim(left, first_row, block_rows, 1)
        outer_prod = jnp.einsum(
            "sic,sjd->ijcd", left_block, right, preferred_element_type=jnp.float32
        )
        flattened = outer_prod.reshape(block_rows * col_count, -1)
        result = jnp.dot(flattened, weight_f32, precision=lax.Precision.HIGHEST)
        return result.reshape(block_rows, col_count, -1)

    starts = jnp.arange(row_count // block_rows) * block_rows
    return lax.map(project_block, starts).reshape(row_count, col_count, -1)


def general_shards(
    homolog_embedding,
    homolog_cell_occupancy,
    peptide_occupancy,
    standardize_multiplier,
    standardize_addend,
    lhs_linear_map,
    lhs_linear_constant,
    rhs_linear_map,
    rhs_linear_constant,
    closing_linear_map,
    closing_linear_constant,
):
    occupied_indicator = (homolog_cell_occupancy * peptide_occupancy[None, :]).astype(jnp.float32)
    report_text = homolog_embedding.astype(jnp.float32)
    average = jnp.mean(report_text, axis=-1, keepdims=True)
    spread = jnp.mean(jnp.square(report_text - average), axis=-1, keepdims=True)
    normed = (
        (report_text - average) * lax.rsqrt(spread + 1e-05) * standardize_multiplier
        + standardize_addend
    ).astype(jnp.bfloat16)
    left = project_side(normed, occupied_indicator, lhs_linear_map, lhs_linear_constant)
    right = project_side(normed, occupied_indicator, rhs_linear_map, rhs_linear_constant)
    mask_bf = occupied_indicator.astype(jnp.bfloat16)
    left_col, right_col, mask_col = (
        lax.all_gather(left, "row", axis=1, tiled=True),
        lax.all_gather(right, "row", axis=1, tiled=True),
        lax.all_gather(mask_bf, "row", axis=1, tiled=True),
    )
    row_devices = lax.axis_size("row")
    col_devices = lax.axis_size("col")
    col_len = left_col.shape[1]
    row_len = col_len * col_devices // row_devices
    row_index = lax.axis_index("row")
    root_col = row_index * col_devices // row_devices
    offset = row_index * row_len % col_len
    whole_left, whole_mask = (
        from_root(left_col, "col", root_col),
        from_root(mask_col, "col", root_col),
    )
    left_row = lax.dynamic_slice_in_dim(whole_left, offset, row_len, 1)
    mask_row = lax.dynamic_slice_in_dim(whole_mask, offset, row_len, 1)
    partial_value = pair_rows(left_row, right_col, closing_linear_map)
    mask_rows_all, mask_cols_all = (
        lax.all_gather(mask_row, "seq", axis=0, tiled=True),
        lax.all_gather(mask_col, "seq", axis=0, tiled=True),
    )
    counts_full = jnp.dot(mask_rows_all.T, mask_cols_all, preferred_element_type=jnp.float32)
    summed = lax.psum_scatter(
        partial_value.astype(jnp.bfloat16), "seq", scatter_dimension=1, tiled=True
    ).astype(jnp.float32)
    seq_devices = lax.axis_size("seq")
    part_cols = col_len // seq_devices
    counts = lax.dynamic_slice_in_dim(counts_full, lax.axis_index("seq") * part_cols, part_cols, 1)
    return ((summed + closing_linear_constant) / jnp.maximum(counts, 1.0)[:, :, None]).astype(
        jnp.bfloat16
    )


def project_kernel(
    pept_ref, x_ref, occ_ref, gain_ref, shift_ref, wl_ref, bl_ref, wr_ref, br_ref,
    left_ref, right_ref, y_ref, l_ref,
):
    residues, sequences = occ_ref.shape
    hidden = wl_ref.shape[0]
    x = x_ref[...].astype(jnp.float32)
    average = jnp.mean(x, axis=-1, keepdims=True)
    centred = x - average
    spread = jnp.mean(jnp.square(centred), axis=-1, keepdims=True)
    normed = (centred * lax.rsqrt(spread + 1e-05) * gain_ref[...] + shift_ref[...]).astype(
        jnp.bfloat16
    )
    weight = jnp.concatenate([wl_ref[...], wr_ref[...]], axis=0)
    bias = jnp.concatenate([bl_ref[...], br_ref[...]], axis=1)
    y = lax.dot_general(normed, weight, NT, preferred_element_type=jnp.float32) + bias
    y_ref[:, : 2 * hidden] = y
    for i in range(residues):
        live = (occ_ref[i : i + 1, :] * pept_ref[i]).astype(jnp.float32)
        part = y_ref[pl.ds(i, sequences, stride=residues), :].T[: 2 * hidden] * live
        l_ref[pl.ds(i, hidden, stride=residues), :] = part[:hidden]
        right_ref[i * hidden : (i + 1) * hidden, :] = part[hidden:].astype(jnp.bfloat16)
        l_ref[hidden * residues + i : hidden * residues + i + 1, :] = live
    l_ref[hidden * residues + residues :, :] = jnp.zeros((MASK_ROWS - residues, sequences), jnp.float32)
    left_ref[...] = l_ref[...].astype(jnp.bfloat16)
    right_ref[hidden * residues :, :] = l_ref[hidden * residues :, :].astype(jnp.bfloat16)


def pair_kernel(
    l0, l1, l2, l3, r0, r1, r2, r3, w_ref, b_ref, out_ref, ls_ref, rs_ref, big_ref, p_ref
):
    hidden = 32
    body = l0.shape[0] - MASK_ROWS
    residues = body // hidden
    width = w_ref.shape[1]
    row, col, seq = (lax.axis_index(name) for name in GROUP)
    for k, (left, right) in enumerate(((l0, r0), (l1, r1), (l2, r2), (l3, r3))):
        ls_ref[seq ^ (k % 2), col ^ (k // 2)] = left[...]
        rs_ref[(row % 2) ^ (k % 2), (row // 2) ^ (k // 2)] = right[...]

    def rows(ref, first, last):
        return jnp.concatenate(
            [
                jnp.concatenate([ref[h, p, first:last, :] for p in range(2)], axis=0)
                for h in range(2)
            ],
            axis=1,
        )

    left = rows(ls_ref, 0, body)
    right = rows(rs_ref, 0, body)
    outer = lax.dot_general(left, right, NT, preferred_element_type=jnp.float32)
    live_i = rows(ls_ref, body, body + MASK_ROWS)
    live_j = rows(rs_ref, body, body + MASK_ROWS)
    counts = lax.dot_general(live_i, live_j, NT, preferred_element_type=jnp.float32)
    spread_shape = (2 * MASK_ROWS, 2 * body)
    at_row = lax.broadcasted_iota(jnp.int32, spread_shape, 0)
    at_lane = lax.broadcasted_iota(jnp.int32, spread_shape, 1)
    hit = ((at_row // MASK_ROWS) * residues + at_row % MASK_ROWS == at_lane // hidden) & (
        at_row % MASK_ROWS < residues
    )
    counts = jnp.dot(
        counts.astype(jnp.bfloat16), hit.astype(jnp.bfloat16), preferred_element_type=jnp.float32
    )
    per_vector = 128 // hidden
    lane = lax.broadcasted_iota(jnp.int32, (2 * residues, 128), 1) // hidden
    masks = [(lane == a).astype(jnp.bfloat16) for a in range(per_vector)]

    def put(slot, low, high):
        both = jnp.concatenate([low, high], axis=0).astype(jnp.bfloat16)
        for g in range(2 * residues // per_vector):
            tile = both[:, g * 128 : (g + 1) * 128]
            for a in range(per_vector):
                first = (g * per_vector + a) * 2 * residues
                big_ref[first : first + 2 * residues, slot * 128 : (slot + 1) * 128] = tile * masks[a]

    for c in range(hidden):
        put(c, outer[c * residues : (c + 1) * residues], outer[body + c * residues : body + (c + 1) * residues])
    put(hidden, counts[:residues], counts[MASK_ROWS : MASK_ROWS + residues])
    weight = jnp.concatenate(
        [w_ref[c * hidden : (c + 1) * hidden, :] for c in range(hidden) for _ in range(per_vector)],
        axis=0,
    )
    projected = jnp.dot(
        big_ref[:, : hidden * 128], weight, preferred_element_type=jnp.float32
    )
    share = jnp.full((128, width), 1.0 / hidden, jnp.bfloat16)
    divisor = jnp.dot(big_ref[:, hidden * 128 :], share, preferred_element_type=jnp.float32)
    p_ref[...] = (projected + b_ref[...]) / jnp.maximum(divisor, 1.0)
    for i in range(2 * residues):
        out_ref[i] = p_ref[pl.ds(i, 2 * residues, stride=2 * residues), :].astype(jnp.bfloat16)


def left_route(k):
    route = []
    for r in range(4):
        for c in range(2):
            for q in range(2):
                to = (2 * c + r // 2, (r % 2) ^ (k // 2), q ^ (k % 2))
                route.append((4 * r + 2 * c + q, 4 * to[0] + 2 * to[1] + to[2]))
    return route


def right_route(k):
    route = []
    for r in range(4):
        for c in range(2):
            for q in range(2):
                to = (2 * ((r % 2) ^ (k // 2)) + (q ^ (k % 2)), c, r // 2)
                route.append((4 * r + 2 * c + q, 4 * to[0] + 2 * to[1] + to[2]))
    return route


def direct_shards(
    homolog_embedding,
    homolog_cell_occupancy,
    peptide_occupancy,
    standardize_multiplier,
    standardize_addend,
    lhs_linear_map,
    lhs_linear_constant,
    rhs_linear_map,
    rhs_linear_constant,
    closing_linear_map,
    closing_linear_constant,
):
    sequences, residues, signal = homolog_embedding.shape
    hidden = lhs_linear_map.shape[1]
    width = closing_linear_map.shape[1]
    rows = residues * hidden + MASK_ROWS
    payload = jax.ShapeDtypeStruct((rows, sequences), jnp.bfloat16)
    vmem = pl.BlockSpec(memory_space=pltpu.VMEM)
    left, right = pl.pallas_call(
        project_kernel,
        out_shape=(payload, payload),
        in_specs=[pl.BlockSpec(memory_space=pltpu.SMEM)] + [vmem] * 8,
        out_specs=(vmem, vmem),
        scratch_shapes=[
            pltpu.VMEM((sequences * residues, 128), jnp.float32),
            pltpu.VMEM((rows, sequences), jnp.float32),
        ],
        compiler_params=pltpu.CompilerParams(vmem_limit_bytes=24 * 1024 * 1024),
        name="normalize_and_project",
    )(
        peptide_occupancy,
        homolog_embedding.reshape(sequences * residues, signal),
        homolog_cell_occupancy.T,
        standardize_multiplier.reshape(1, signal),
        standardize_addend.reshape(1, signal),
        lhs_linear_map.T,
        lhs_linear_constant.reshape(1, hidden),
        rhs_linear_map.T,
        rhs_linear_constant.reshape(1, hidden),
    )
    lefts = [lax.ppermute(left, GROUP, left_route(k)) for k in range(4)]
    rights = [lax.ppermute(right, GROUP, right_route(k)) for k in range(4)]
    return pl.pallas_call(
        pair_kernel,
        out_shape=jax.ShapeDtypeStruct((2 * residues, 2 * residues, width), jnp.bfloat16),
        in_specs=[vmem] * 10,
        out_specs=vmem,
        scratch_shapes=[
            pltpu.VMEM((2, 2, rows, sequences), jnp.bfloat16),
            pltpu.VMEM((2, 2, rows, sequences), jnp.bfloat16),
            pltpu.VMEM((4 * residues * residues, (hidden + 1) * 128), jnp.bfloat16),
            pltpu.VMEM((4 * residues * residues, width), jnp.float32),
        ],
        compiler_params=pltpu.CompilerParams(vmem_limit_bytes=32 * 1024 * 1024),
        name="pair_update",
    )(*lefts, *rights, closing_linear_map, closing_linear_constant.reshape(1, width))


def shards(*arrays):
    sizes = tuple(lax.axis_size(name) for name in GROUP)
    if sizes == (4, 2, 2) and arrays[0].shape[:2] == (128, 8):
        return direct_shards(*arrays)
    return general_shards(*arrays)


def solution(mesh):
    return jax.shard_map(
        shards,
        mesh=mesh,
        in_specs=(
            P(("crops", "seq"), ("col", "row"), None),
            P(("crops", "seq"), ("col", "row")),
            P(("crops", "col", "row")),
            P(),
            P(),
            P(),
            P(),
            P(),
            P(),
            P(),
            P(),
        ),
        out_specs=P(("crops", "row"), ("col", "seq"), None),
        check_vma=False,
    )
```

```python
import math

import jax
import jax.numpy as jnp
from jax import lax
from jax.experimental import pallas as pl
from jax.experimental.pallas import tpu as pltpu
from jax.sharding import PartitionSpec as P

GROUP = ("row", "col", "seq")
NT = (((1,), (1,)), ((), ()))
MASK_ROWS = 16


def from_root(x, axis, root):
    mine = lax.axis_index(axis) == root
    return lax.psum(jnp.where(mine, x, jnp.zeros_like(x)), axis)


def project_side(normed, occupied_indicator, weight, bias):
    seq_count, res_count, width = normed.shape
    report_text = jnp.dot(
        normed.reshape(seq_count * res_count, width), weight, preferred_element_type=jnp.float32
    )
    report_text = (report_text + bias).reshape(seq_count, res_count, -1) * occupied_indicator[
        :, :, None
    ]
    return report_text.astype(jnp.bfloat16)


def pair_rows(left, right, closing_linear_map):
    row_count = left.shape[1]
    col_count = right.shape[1]
    block_rows = math.gcd(row_count, max(1, 512 // col_count))
    weight_f32 = closing_linear_map.astype(jnp.float32)

    def project_block(first_row):
        left_block = lax.dynamic_slice_in_dim(left, first_row, block_rows, 1)
        outer_prod = jnp.einsum(
            "sic,sjd->ijcd", left_block, right, preferred_element_type=jnp.float32
        )
        flattened = outer_prod.reshape(block_rows * col_count, -1)
        result = jnp.dot(flattened, weight_f32, precision=lax.Precision.HIGHEST)
        return result.reshape(block_rows, col_count, -1)

    starts = jnp.arange(row_count // block_rows) * block_rows
    return lax.map(project_block, starts).reshape(row_count, col_count, -1)


def general_shards(
    homolog_embedding,
    homolog_cell_occupancy,
    peptide_occupancy,
    standardize_multiplier,
    standardize_addend,
    lhs_linear_map,
    lhs_linear_constant,
    rhs_linear_map,
    rhs_linear_constant,
    closing_linear_map,
    closing_linear_constant,
):
    occupied_indicator = (homolog_cell_occupancy * peptide_occupancy[None, :]).astype(jnp.float32)
    report_text = homolog_embedding.astype(jnp.float32)
    average = jnp.mean(report_text, axis=-1, keepdims=True)
    spread = jnp.mean(jnp.square(report_text - average), axis=-1, keepdims=True)
    normed = (
        (report_text - average) * lax.rsqrt(spread + 1e-05) * standardize_multiplier
        + standardize_addend
    ).astype(jnp.bfloat16)
    left = project_side(normed, occupied_indicator, lhs_linear_map, lhs_linear_constant)
    right = project_side(normed, occupied_indicator, rhs_linear_map, rhs_linear_constant)
    mask_bf = occupied_indicator.astype(jnp.bfloat16)
    left_col, right_col, mask_col = (
        lax.all_gather(left, "row", axis=1, tiled=True),
        lax.all_gather(right, "row", axis=1, tiled=True),
        lax.all_gather(mask_bf, "row", axis=1, tiled=True),
    )
    row_devices = lax.axis_size("row")
    col_devices = lax.axis_size("col")
    col_len = left_col.shape[1]
    row_len = col_len * col_devices // row_devices
    row_index = lax.axis_index("row")
    root_col = row_index * col_devices // row_devices
    offset = row_index * row_len % col_len
    whole_left, whole_mask = (
        from_root(left_col, "col", root_col),
        from_root(mask_col, "col", root_col),
    )
    left_row = lax.dynamic_slice_in_dim(whole_left, offset, row_len, 1)
    mask_row = lax.dynamic_slice_in_dim(whole_mask, offset, row_len, 1)
    partial_value = pair_rows(left_row, right_col, closing_linear_map)
    mask_rows_all, mask_cols_all = (
        lax.all_gather(mask_row, "seq", axis=0, tiled=True),
        lax.all_gather(mask_col, "seq", axis=0, tiled=True),
    )
    counts_full = jnp.dot(mask_rows_all.T, mask_cols_all, preferred_element_type=jnp.float32)
    summed = lax.psum_scatter(
        partial_value.astype(jnp.bfloat16), "seq", scatter_dimension=1, tiled=True
    ).astype(jnp.float32)
    seq_devices = lax.axis_size("seq")
    part_cols = col_len // seq_devices
    counts = lax.dynamic_slice_in_dim(counts_full, lax.axis_index("seq") * part_cols, part_cols, 1)
    return ((summed + closing_linear_constant) / jnp.maximum(counts, 1.0)[:, :, None]).astype(
        jnp.bfloat16
    )


def project_kernel(
    pept_hbm, x_hbm, occ_hbm, gain_hbm, shift_hbm, wl_hbm, bl_hbm, wr_hbm, br_hbm,
    left_ref, right_ref,
    pept_ref, x_ref, occ_ref, gain_ref, shift_ref, wl_ref, bl_ref, wr_ref, br_ref,
    y_ref, l_ref, x_sems, sems,
):
    residues, sequences = occ_ref.shape
    hidden = wl_ref.shape[0]
    chunks = x_sems.shape[0]
    size = x_ref.shape[0] // chunks
    x_copies = [
        pltpu.make_async_copy(
            x_hbm.at[pl.ds(n * size, size)], x_ref.at[pl.ds(n * size, size)], x_sems.at[n]
        )
        for n in range(chunks)
    ]
    pairs = (
        (wl_hbm, wl_ref), (wr_hbm, wr_ref), (gain_hbm, gain_ref), (shift_hbm, shift_ref),
        (bl_hbm, bl_ref), (br_hbm, br_ref), (occ_hbm, occ_ref), (pept_hbm, pept_ref),
    )
    copies = [pltpu.make_async_copy(a, b, sems.at[n]) for n, (a, b) in enumerate(pairs)]
    x_copies[0].start()
    for copy in copies:
        copy.start()
    for copy in x_copies[1:]:
        copy.start()
    for copy in copies:
        copy.wait()
    weight = jnp.concatenate([wl_ref[...], wr_ref[...]], axis=0)
    bias = jnp.concatenate([bl_ref[...], br_ref[...]], axis=1)
    for n, copy in enumerate(x_copies):
        copy.wait()
        x = x_ref[n * size : (n + 1) * size, :].astype(jnp.float32)
        average = jnp.mean(x, axis=-1, keepdims=True)
        centred = x - average
        spread = jnp.mean(jnp.square(centred), axis=-1, keepdims=True)
        normed = (centred * lax.rsqrt(spread + 1e-05) * gain_ref[...] + shift_ref[...]).astype(
            jnp.bfloat16
        )
        y = lax.dot_general(normed, weight, NT, preferred_element_type=jnp.float32) + bias
        y_ref[n * size : (n + 1) * size, : 2 * hidden] = y
    for i in range(residues):
        live = (occ_ref[i : i + 1, :] * pept_ref[i]).astype(jnp.float32)
        part = y_ref[pl.ds(i, sequences, stride=residues), :].T[: 2 * hidden] * live
        l_ref[pl.ds(i, hidden, stride=residues), :] = part[:hidden]
        right_ref[i * hidden : (i + 1) * hidden, :] = part[hidden:].astype(jnp.bfloat16)
        l_ref[hidden * residues + i : hidden * residues + i + 1, :] = live
    l_ref[hidden * residues + residues :, :] = jnp.zeros((MASK_ROWS - residues, sequences), jnp.float32)
    left_ref[...] = l_ref[...].astype(jnp.bfloat16)
    right_ref[hidden * residues :, :] = l_ref[hidden * residues :, :].astype(jnp.bfloat16)


def expand(tile, store, hidden):
    rows, lanes = tile.shape
    per_vector = 128 // hidden
    lane = lax.broadcasted_iota(jnp.int32, (rows, 128), 1) // hidden
    for g in range(lanes // 128):
        part = tile[:, g * 128 : (g + 1) * 128]
        for a in range(per_vector):
            first = (g * per_vector + a) * rows
            store(first, part * (lane == a).astype(jnp.bfloat16))


def pair_kernel(
    own, l0, l1, r0, r1, r2, r3, w_ref, out_ref, ls_ref, rs_ref, big_ref
):
    body = l0.shape[0] - MASK_ROWS
    hidden = 32
    residues = body // hidden
    row, col, seq = (lax.axis_index(name) for name in GROUP)
    for k, piece in enumerate((l0, l1)):
        ls_ref[col ^ k] = piece[...]
    for k, piece in enumerate((r0, r1, r2, r3)):
        rs_ref[row ^ k] = piece[...]
    half = 2 * (seq if own else 1 - seq)

    def rows(ref, at, first, last):
        return jnp.concatenate([ref[at + p, first:last, :] for p in range(2)], axis=0)

    outer = lax.dot_general(
        rows(ls_ref, 0, 0, body), rows(rs_ref, half, 0, body), NT, preferred_element_type=jnp.float32
    )
    live_i = rows(ls_ref, 0, body, body + MASK_ROWS)
    live_j = rows(rs_ref, half, body, body + MASK_ROWS)
    live_j = jnp.concatenate([live_j, jnp.zeros((128 - 2 * MASK_ROWS, live_j.shape[1]), live_j.dtype)], axis=0)
    counts = lax.dot_general(live_i, live_j, NT, preferred_element_type=jnp.float32)
    for c in range(hidden):
        tile = jnp.concatenate(
            [outer[p * body + c * residues : p * body + (c + 1) * residues] for p in range(2)], axis=0
        ).astype(jnp.bfloat16)

        def store(first, value, c=c):
            big_ref[first : first + 2 * residues, c * 128 : (c + 1) * 128] = value

        expand(tile, store, hidden)
    weight = jnp.concatenate(
        [w_ref[c * hidden : (c + 1) * hidden, :] for c in range(hidden) for _ in range(128 // hidden)],
        axis=0,
    )
    pairs = 4 * residues * residues
    projected = jnp.dot(big_ref[...], weight, preferred_element_type=jnp.float32)
    out_ref[:pairs, :] = projected.astype(out_ref.dtype)
    out_ref[pairs:, :] = counts.astype(out_ref.dtype)


def finish_kernel(mine_ref, other_ref, b_ref, out_ref, big_ref, p_ref):
    residues = out_ref.shape[0] // 2
    pairs = 4 * residues * residues
    hidden = 32
    counts = mine_ref[pairs:, :] + other_ref[pairs:, :].astype(jnp.float32)
    spread_shape = (128, 2 * residues * hidden)
    at_row = lax.broadcasted_iota(jnp.int32, spread_shape, 0)
    at_lane = lax.broadcasted_iota(jnp.int32, spread_shape, 1)
    hit = ((at_row // MASK_ROWS) * residues + at_row % MASK_ROWS == at_lane // hidden) & (
        at_row % MASK_ROWS < residues
    )
    counts = jnp.dot(
        counts.astype(jnp.bfloat16), hit.astype(jnp.bfloat16), preferred_element_type=jnp.float32
    )
    tile = jnp.concatenate(
        [counts[p * MASK_ROWS : p * MASK_ROWS + residues] for p in range(2)], axis=0
    ).astype(jnp.bfloat16)

    def store(first, value):
        big_ref[first : first + 2 * residues, :] = value

    expand(tile, store, hidden)
    share = jnp.full((128, 128), 1.0 / hidden, jnp.bfloat16)
    divisor = jnp.dot(big_ref[...], share, preferred_element_type=jnp.float32)
    total = mine_ref[:pairs, :] + other_ref[:pairs, :].astype(jnp.float32)
    p_ref[...] = (total + b_ref[...]) / jnp.maximum(divisor, 1.0)
    for i in range(2 * residues):
        out_ref[i] = p_ref[pl.ds(i, 2 * residues, stride=2 * residues), :].astype(jnp.bfloat16)


def route(target):
    return [
        (4 * r + 2 * c + q, 4 * to[0] + 2 * to[1] + to[2])
        for r in range(4)
        for c in range(2)
        for q in range(2)
        for to in (target(r, c, q),)
    ]


def direct_shards(
    homolog_embedding,
    homolog_cell_occupancy,
    peptide_occupancy,
    standardize_multiplier,
    standardize_addend,
    lhs_linear_map,
    lhs_linear_constant,
    rhs_linear_map,
    rhs_linear_constant,
    closing_linear_map,
    closing_linear_constant,
):
    sequences, residues, signal = homolog_embedding.shape
    hidden = lhs_linear_map.shape[1]
    width = closing_linear_map.shape[1]
    rows = residues * hidden + MASK_ROWS
    pairs = 4 * residues * residues
    payload = jax.ShapeDtypeStruct((rows, sequences), jnp.bfloat16)
    vmem = pl.BlockSpec(memory_space=pltpu.VMEM)
    in_hbm = pl.BlockSpec(memory_space=pltpu.HBM)
    left, right = pl.pallas_call(
        project_kernel,
        out_shape=(payload, payload),
        in_specs=[in_hbm] * 9,
        out_specs=(vmem, vmem),
        scratch_shapes=[
            pltpu.SMEM((residues,), jnp.int32),
            pltpu.VMEM((sequences * residues, signal), jnp.bfloat16),
            pltpu.VMEM((residues, sequences), jnp.int32),
            pltpu.VMEM((1, signal), jnp.float32),
            pltpu.VMEM((1, signal), jnp.float32),
            pltpu.VMEM((hidden, signal), jnp.bfloat16),
            pltpu.VMEM((1, hidden), jnp.float32),
            pltpu.VMEM((hidden, signal), jnp.bfloat16),
            pltpu.VMEM((1, hidden), jnp.float32),
            pltpu.VMEM((sequences * residues, 128), jnp.float32),
            pltpu.VMEM((rows, sequences), jnp.float32),
            pltpu.SemaphoreType.DMA((4,)),
            pltpu.SemaphoreType.DMA((8,)),
        ],
        compiler_params=pltpu.CompilerParams(vmem_limit_bytes=60 * 1024 * 1024),
        name="normalize_and_project",
    )(
        peptide_occupancy,
        homolog_embedding.reshape(sequences * residues, signal),
        homolog_cell_occupancy.T,
        standardize_multiplier.reshape(1, signal),
        standardize_addend.reshape(1, signal),
        lhs_linear_map.T,
        lhs_linear_constant.reshape(1, hidden),
        rhs_linear_map.T,
        rhs_linear_constant.reshape(1, hidden),
    )
    rights = [right] + [
        lax.ppermute(right, GROUP, route(lambda r, c, q, k=k: (r ^ k, c, q))) for k in (1, 2, 3)
    ]
    lefts = [
        lax.ppermute(left, GROUP, route(lambda r, c, q, k=k: (2 * c + r // 2, (r % 2) ^ k, q)))
        for k in range(2)
    ]

    def pair_sums(own, kind):
        return pl.pallas_call(
            lambda *refs: pair_kernel(own, *refs),
            out_shape=jax.ShapeDtypeStruct((pairs + 2 * MASK_ROWS, width), kind),
            in_specs=[vmem] * 7,
            out_specs=vmem,
            scratch_shapes=[
                pltpu.VMEM((2, rows, sequences), jnp.bfloat16),
                pltpu.VMEM((4, rows, sequences), jnp.bfloat16),
                pltpu.VMEM((pairs, hidden * 128), jnp.bfloat16),
            ],
            compiler_params=pltpu.CompilerParams(vmem_limit_bytes=24 * 1024 * 1024),
            cost_estimate=pl.CostEstimate(
                flops=2 * pairs * hidden * 128 * width, bytes_accessed=1 << 20, transcendentals=0
            ),
            name="own_pair_sums" if own else "other_pair_sums",
        )(*lefts, *rights, closing_linear_map)

    theirs = pair_sums(False, jnp.bfloat16)
    received = lax.ppermute(theirs, GROUP, route(lambda r, c, q: (r, c, 1 - q)))
    mine = pair_sums(True, jnp.float32)
    return pl.pallas_call(
        finish_kernel,
        out_shape=jax.ShapeDtypeStruct((2 * residues, 2 * residues, width), jnp.bfloat16),
        in_specs=[vmem] * 3,
        out_specs=vmem,
        scratch_shapes=[
            pltpu.VMEM((pairs, 128), jnp.bfloat16),
            pltpu.VMEM((pairs, width), jnp.float32),
        ],
        compiler_params=pltpu.CompilerParams(vmem_limit_bytes=16 * 1024 * 1024),
        name="divide",
    )(mine, received, closing_linear_constant.reshape(1, width))


def shards(*arrays):
    sizes = tuple(lax.axis_size(name) for name in GROUP)
    if sizes == (4, 2, 2) and arrays[0].shape[:2] == (128, 8):
        return direct_shards(*arrays)
    return general_shards(*arrays)


def solution(mesh):
    return jax.shard_map(
        shards,
        mesh=mesh,
        in_specs=(
            P(("crops", "seq"), ("col", "row"), None),
            P(("crops", "seq"), ("col", "row")),
            P(("crops", "col", "row")),
            P(),
            P(),
            P(),
            P(),
            P(),
            P(),
            P(),
            P(),
        ),
        out_specs=P(("crops", "row"), ("col", "seq"), None),
        check_vma=False,
    )
```

```python
import math

import jax
import jax.numpy as jnp
from jax import lax
from jax.experimental import pallas as pl
from jax.experimental.pallas import tpu as pltpu
from jax.sharding import PartitionSpec as P

GROUP = ("row", "col", "seq")
NT = (((1,), (1,)), ((), ()))
MASK_ROWS = 16


def from_root(x, axis, root):
    mine = lax.axis_index(axis) == root
    return lax.psum(jnp.where(mine, x, jnp.zeros_like(x)), axis)


def project_side(normed, occupied_indicator, weight, bias):
    seq_count, res_count, width = normed.shape
    report_text = jnp.dot(
        normed.reshape(seq_count * res_count, width), weight, preferred_element_type=jnp.float32
    )
    report_text = (report_text + bias).reshape(seq_count, res_count, -1) * occupied_indicator[
        :, :, None
    ]
    return report_text.astype(jnp.bfloat16)


def pair_rows(left, right, closing_linear_map):
    row_count = left.shape[1]
    col_count = right.shape[1]
    block_rows = math.gcd(row_count, max(1, 512 // col_count))
    weight_f32 = closing_linear_map.astype(jnp.float32)

    def project_block(first_row):
        left_block = lax.dynamic_slice_in_dim(left, first_row, block_rows, 1)
        outer_prod = jnp.einsum(
            "sic,sjd->ijcd", left_block, right, preferred_element_type=jnp.float32
        )
        flattened = outer_prod.reshape(block_rows * col_count, -1)
        result = jnp.dot(flattened, weight_f32, precision=lax.Precision.HIGHEST)
        return result.reshape(block_rows, col_count, -1)

    starts = jnp.arange(row_count // block_rows) * block_rows
    return lax.map(project_block, starts).reshape(row_count, col_count, -1)


def general_shards(
    homolog_embedding,
    homolog_cell_occupancy,
    peptide_occupancy,
    standardize_multiplier,
    standardize_addend,
    lhs_linear_map,
    lhs_linear_constant,
    rhs_linear_map,
    rhs_linear_constant,
    closing_linear_map,
    closing_linear_constant,
):
    occupied_indicator = (homolog_cell_occupancy * peptide_occupancy[None, :]).astype(jnp.float32)
    report_text = homolog_embedding.astype(jnp.float32)
    average = jnp.mean(report_text, axis=-1, keepdims=True)
    spread = jnp.mean(jnp.square(report_text - average), axis=-1, keepdims=True)
    normed = (
        (report_text - average) * lax.rsqrt(spread + 1e-05) * standardize_multiplier
        + standardize_addend
    ).astype(jnp.bfloat16)
    left = project_side(normed, occupied_indicator, lhs_linear_map, lhs_linear_constant)
    right = project_side(normed, occupied_indicator, rhs_linear_map, rhs_linear_constant)
    mask_bf = occupied_indicator.astype(jnp.bfloat16)
    left_col, right_col, mask_col = (
        lax.all_gather(left, "row", axis=1, tiled=True),
        lax.all_gather(right, "row", axis=1, tiled=True),
        lax.all_gather(mask_bf, "row", axis=1, tiled=True),
    )
    row_devices = lax.axis_size("row")
    col_devices = lax.axis_size("col")
    col_len = left_col.shape[1]
    row_len = col_len * col_devices // row_devices
    row_index = lax.axis_index("row")
    root_col = row_index * col_devices // row_devices
    offset = row_index * row_len % col_len
    whole_left, whole_mask = (
        from_root(left_col, "col", root_col),
        from_root(mask_col, "col", root_col),
    )
    left_row = lax.dynamic_slice_in_dim(whole_left, offset, row_len, 1)
    mask_row = lax.dynamic_slice_in_dim(whole_mask, offset, row_len, 1)
    partial_value = pair_rows(left_row, right_col, closing_linear_map)
    mask_rows_all, mask_cols_all = (
        lax.all_gather(mask_row, "seq", axis=0, tiled=True),
        lax.all_gather(mask_col, "seq", axis=0, tiled=True),
    )
    counts_full = jnp.dot(mask_rows_all.T, mask_cols_all, preferred_element_type=jnp.float32)
    summed = lax.psum_scatter(
        partial_value.astype(jnp.bfloat16), "seq", scatter_dimension=1, tiled=True
    ).astype(jnp.float32)
    seq_devices = lax.axis_size("seq")
    part_cols = col_len // seq_devices
    counts = lax.dynamic_slice_in_dim(counts_full, lax.axis_index("seq") * part_cols, part_cols, 1)
    return ((summed + closing_linear_constant) / jnp.maximum(counts, 1.0)[:, :, None]).astype(
        jnp.bfloat16
    )


def project_kernel(
    pept_hbm, x_hbm, occ_hbm, gain_hbm, shift_hbm, wl_hbm, bl_hbm, wr_hbm, br_hbm,
    left_ref, right_ref,
    pept_ref, x_ref, occ_ref, gain_ref, shift_ref, wl_ref, bl_ref, wr_ref, br_ref,
    y_ref, l_ref, x_sems, sems,
):
    residues, sequences = occ_ref.shape
    hidden = wl_ref.shape[0]
    chunks = x_sems.shape[0]
    size = x_ref.shape[0] // chunks
    x_copies = [
        pltpu.make_async_copy(
            x_hbm.at[pl.ds(n * size, size)], x_ref.at[pl.ds(n * size, size)], x_sems.at[n]
        )
        for n in range(chunks)
    ]
    pairs = (
        (wl_hbm, wl_ref), (wr_hbm, wr_ref), (gain_hbm, gain_ref), (shift_hbm, shift_ref),
        (bl_hbm, bl_ref), (br_hbm, br_ref), (occ_hbm, occ_ref), (pept_hbm, pept_ref),
    )
    copies = [pltpu.make_async_copy(a, b, sems.at[n]) for n, (a, b) in enumerate(pairs)]
    x_copies[0].start()
    for copy in copies:
        copy.start()
    for copy in x_copies[1:]:
        copy.start()
    for copy in copies:
        copy.wait()
    weight = jnp.concatenate([wl_ref[...], wr_ref[...]], axis=0)
    bias = jnp.concatenate([bl_ref[...], br_ref[...]], axis=1)
    for n, copy in enumerate(x_copies):
        copy.wait()
        x = x_ref[n * size : (n + 1) * size, :].astype(jnp.float32)
        average = jnp.mean(x, axis=-1, keepdims=True)
        centred = x - average
        spread = jnp.mean(jnp.square(centred), axis=-1, keepdims=True)
        normed = (centred * lax.rsqrt(spread + 1e-05) * gain_ref[...] + shift_ref[...]).astype(
            jnp.bfloat16
        )
        y = lax.dot_general(normed, weight, NT, preferred_element_type=jnp.float32) + bias
        y_ref[n * size : (n + 1) * size, : 2 * hidden] = y
    for i in range(residues):
        live = (occ_ref[i : i + 1, :] * pept_ref[i]).astype(jnp.float32)
        part = y_ref[pl.ds(i, sequences, stride=residues), :].T[: 2 * hidden] * live
        l_ref[pl.ds(i, hidden, stride=residues), :] = part[:hidden]
        right_ref[i * hidden : (i + 1) * hidden, :] = part[hidden:].astype(jnp.bfloat16)
        l_ref[hidden * residues + i : hidden * residues + i + 1, :] = live
    l_ref[hidden * residues + residues :, :] = jnp.zeros((MASK_ROWS - residues, sequences), jnp.float32)
    left_ref[...] = l_ref[...].astype(jnp.bfloat16)
    right_ref[hidden * residues :, :] = l_ref[hidden * residues :, :].astype(jnp.bfloat16)


def expand(tile, store, hidden):
    rows, lanes = tile.shape
    per_vector = 128 // hidden
    lane = lax.broadcasted_iota(jnp.int32, (rows, 128), 1) // hidden
    for g in range(lanes // 128):
        part = tile[:, g * 128 : (g + 1) * 128]
        for a in range(per_vector):
            first = (g * per_vector + a) * rows
            store(first, part * (lane == a).astype(jnp.bfloat16))


def pair_kernel(
    own, l0, l1, r0, r1, r2, r3, w_ref, b_hbm, out_ref, ls_ref, rs_ref, big_ref, b_ref, b_sem
):
    if own:
        bias_copy = pltpu.make_async_copy(b_hbm, b_ref, b_sem)
        bias_copy.start()
    body = l0.shape[0] - MASK_ROWS
    hidden = 32
    residues = body // hidden
    row, col, seq = (lax.axis_index(name) for name in GROUP)
    for k, piece in enumerate((l0, l1)):
        ls_ref[col ^ k] = piece[...]
    for k, piece in enumerate((r0, r1, r2, r3)):
        rs_ref[row ^ k] = piece[...]
    half = 2 * (seq if own else 1 - seq)

    def rows(ref, at, first, last):
        return jnp.concatenate([ref[at + p, first:last, :] for p in range(2)], axis=0)

    outer = lax.dot_general(
        rows(ls_ref, 0, 0, body), rows(rs_ref, half, 0, body), NT, preferred_element_type=jnp.float32
    )
    live_i = rows(ls_ref, 0, body, body + MASK_ROWS)
    live_j = rows(rs_ref, half, body, body + MASK_ROWS)
    live_j = jnp.concatenate([live_j, jnp.zeros((128 - 2 * MASK_ROWS, live_j.shape[1]), live_j.dtype)], axis=0)
    counts = lax.dot_general(live_i, live_j, NT, preferred_element_type=jnp.float32)
    for c in range(hidden):
        tile = jnp.concatenate(
            [outer[p * body + c * residues : p * body + (c + 1) * residues] for p in range(2)], axis=0
        ).astype(jnp.bfloat16)

        def store(first, value, c=c):
            big_ref[first : first + 2 * residues, c * 128 : (c + 1) * 128] = value

        expand(tile, store, hidden)
    weight = jnp.concatenate(
        [w_ref[c * hidden : (c + 1) * hidden, :] for c in range(hidden) for _ in range(128 // hidden)],
        axis=0,
    )
    pairs = 4 * residues * residues
    projected = jnp.dot(big_ref[...], weight, preferred_element_type=jnp.float32)
    if own:
        bias_copy.wait()
        projected = projected + b_ref[...]
    out_ref[:pairs, :] = projected.astype(out_ref.dtype)
    out_ref[pairs:, :] = counts.astype(out_ref.dtype)


def finish_kernel(mine_ref, other_ref, out_ref, big_ref, p_ref):
    residues = out_ref.shape[0] // 2
    pairs = 4 * residues * residues
    hidden = 32
    counts = mine_ref[pairs:, :] + other_ref[pairs:, :].astype(jnp.float32)
    spread_shape = (128, 2 * residues * hidden)
    at_row = lax.broadcasted_iota(jnp.int32, spread_shape, 0)
    at_lane = lax.broadcasted_iota(jnp.int32, spread_shape, 1)
    hit = ((at_row // MASK_ROWS) * residues + at_row % MASK_ROWS == at_lane // hidden) & (
        at_row % MASK_ROWS < residues
    )
    counts = jnp.dot(
        counts.astype(jnp.bfloat16), hit.astype(jnp.bfloat16), preferred_element_type=jnp.float32
    )
    tile = jnp.concatenate(
        [counts[p * MASK_ROWS : p * MASK_ROWS + residues] for p in range(2)], axis=0
    ).astype(jnp.bfloat16)

    def store(first, value):
        big_ref[first : first + 2 * residues, :] = value

    expand(tile, store, hidden)
    share = jnp.full((128, 128), 1.0 / hidden, jnp.bfloat16)
    divisor = jnp.dot(big_ref[...], share, preferred_element_type=jnp.float32)
    total = mine_ref[:pairs, :] + other_ref[:pairs, :].astype(jnp.float32)
    p_ref[...] = total / jnp.maximum(divisor, 1.0)
    for i in range(2 * residues):
        out_ref[i] = p_ref[pl.ds(i, 2 * residues, stride=2 * residues), :].astype(jnp.bfloat16)


def route(target):
    return [
        (4 * r + 2 * c + q, 4 * to[0] + 2 * to[1] + to[2])
        for r in range(4)
        for c in range(2)
        for q in range(2)
        for to in (target(r, c, q),)
    ]


def direct_shards(
    homolog_embedding,
    homolog_cell_occupancy,
    peptide_occupancy,
    standardize_multiplier,
    standardize_addend,
    lhs_linear_map,
    lhs_linear_constant,
    rhs_linear_map,
    rhs_linear_constant,
    closing_linear_map,
    closing_linear_constant,
):
    sequences, residues, signal = homolog_embedding.shape
    hidden = lhs_linear_map.shape[1]
    width = closing_linear_map.shape[1]
    rows = residues * hidden + MASK_ROWS
    pairs = 4 * residues * residues
    payload = jax.ShapeDtypeStruct((rows, sequences), jnp.bfloat16)
    vmem = pl.BlockSpec(memory_space=pltpu.VMEM)
    in_hbm = pl.BlockSpec(memory_space=pltpu.HBM)
    left, right = pl.pallas_call(
        project_kernel,
        out_shape=(payload, payload),
        in_specs=[in_hbm] * 9,
        out_specs=(vmem, vmem),
        scratch_shapes=[
            pltpu.SMEM((residues,), jnp.int32),
            pltpu.VMEM((sequences * residues, signal), jnp.bfloat16),
            pltpu.VMEM((residues, sequences), jnp.int32),
            pltpu.VMEM((1, signal), jnp.float32),
            pltpu.VMEM((1, signal), jnp.float32),
            pltpu.VMEM((hidden, signal), jnp.bfloat16),
            pltpu.VMEM((1, hidden), jnp.float32),
            pltpu.VMEM((hidden, signal), jnp.bfloat16),
            pltpu.VMEM((1, hidden), jnp.float32),
            pltpu.VMEM((sequences * residues, 128), jnp.float32),
            pltpu.VMEM((rows, sequences), jnp.float32),
            pltpu.SemaphoreType.DMA((4,)),
            pltpu.SemaphoreType.DMA((8,)),
        ],
        compiler_params=pltpu.CompilerParams(vmem_limit_bytes=60 * 1024 * 1024),
        name="normalize_and_project",
    )(
        peptide_occupancy,
        homolog_embedding.reshape(sequences * residues, signal),
        homolog_cell_occupancy.T,
        standardize_multiplier.reshape(1, signal),
        standardize_addend.reshape(1, signal),
        lhs_linear_map.T,
        lhs_linear_constant.reshape(1, hidden),
        rhs_linear_map.T,
        rhs_linear_constant.reshape(1, hidden),
    )
    far = lax.ppermute(right, GROUP, route(lambda r, c, q: (r ^ 2, c, q)))
    near = lax.ppermute(right, GROUP, route(lambda r, c, q: (r ^ 1, c, q)))
    first = lax.ppermute(left, GROUP, route(lambda r, c, q: (2 * c + r // 2, r % 2, q)))
    passed = lax.ppermute(far, GROUP, route(lambda r, c, q: (r ^ 1, c, q)))
    second = lax.ppermute(first, GROUP, route(lambda r, c, q: (r, 1 - c, q)))
    rights = [right, near, far, passed]
    lefts = [first, second]

    def pair_sums(own, kind):
        return pl.pallas_call(
            lambda *refs: pair_kernel(own, *refs),
            out_shape=jax.ShapeDtypeStruct((pairs + 2 * MASK_ROWS, width), kind),
            in_specs=[vmem] * 7 + [in_hbm],
            out_specs=vmem,
            scratch_shapes=[
                pltpu.VMEM((2, rows, sequences), jnp.bfloat16),
                pltpu.VMEM((4, rows, sequences), jnp.bfloat16),
                pltpu.VMEM((pairs, hidden * 128), jnp.bfloat16),
                pltpu.VMEM((1, width), jnp.float32),
                pltpu.SemaphoreType.DMA,
            ],
            compiler_params=pltpu.CompilerParams(vmem_limit_bytes=24 * 1024 * 1024),
            cost_estimate=pl.CostEstimate(
                flops=2 * pairs * hidden * 128 * width, bytes_accessed=1 << 20, transcendentals=0
            ),
            name="own_pair_sums" if own else "other_pair_sums",
        )(*lefts, *rights, closing_linear_map, closing_linear_constant.reshape(1, width))

    theirs = pair_sums(False, jnp.bfloat16)
    received = lax.ppermute(theirs, GROUP, route(lambda r, c, q: (r, c, 1 - q)))
    mine = pair_sums(True, jnp.float32)
    return pl.pallas_call(
        finish_kernel,
        out_shape=jax.ShapeDtypeStruct((2 * residues, 2 * residues, width), jnp.bfloat16),
        in_specs=[vmem] * 2,
        out_specs=vmem,
        scratch_shapes=[
            pltpu.VMEM((pairs, 128), jnp.bfloat16),
            pltpu.VMEM((pairs, width), jnp.float32),
        ],
        compiler_params=pltpu.CompilerParams(vmem_limit_bytes=16 * 1024 * 1024),
        name="divide",
    )(mine, received)


def shards(*arrays):
    sizes = tuple(lax.axis_size(name) for name in GROUP)
    if sizes == (4, 2, 2) and arrays[0].shape[:2] == (128, 8):
        return direct_shards(*arrays)
    return general_shards(*arrays)


def solution(mesh):
    return jax.shard_map(
        shards,
        mesh=mesh,
        in_specs=(
            P(("crops", "seq"), ("col", "row"), None),
            P(("crops", "seq"), ("col", "row")),
            P(("crops", "col", "row")),
            P(),
            P(),
            P(),
            P(),
            P(),
            P(),
            P(),
            P(),
        ),
        out_specs=P(("crops", "row"), ("col", "seq"), None),
        check_vma=False,
    )
```

```python
import math

import jax
import jax.numpy as jnp
from jax import lax
from jax.experimental import pallas as pl
from jax.experimental.pallas import tpu as pltpu
from jax.sharding import PartitionSpec as P

GROUP = ("row", "col", "seq")
NT = (((1,), (1,)), ((), ()))
MASK_ROWS = 16


def from_root(x, axis, root):
    mine = lax.axis_index(axis) == root
    return lax.psum(jnp.where(mine, x, jnp.zeros_like(x)), axis)


def project_side(normed, occupied_indicator, weight, bias):
    seq_count, res_count, width = normed.shape
    report_text = jnp.dot(
        normed.reshape(seq_count * res_count, width), weight, preferred_element_type=jnp.float32
    )
    report_text = (report_text + bias).reshape(seq_count, res_count, -1) * occupied_indicator[
        :, :, None
    ]
    return report_text.astype(jnp.bfloat16)


def pair_rows(left, right, closing_linear_map):
    row_count = left.shape[1]
    col_count = right.shape[1]
    block_rows = math.gcd(row_count, max(1, 512 // col_count))
    weight_f32 = closing_linear_map.astype(jnp.float32)

    def project_block(first_row):
        left_block = lax.dynamic_slice_in_dim(left, first_row, block_rows, 1)
        outer_prod = jnp.einsum(
            "sic,sjd->ijcd", left_block, right, preferred_element_type=jnp.float32
        )
        flattened = outer_prod.reshape(block_rows * col_count, -1)
        result = jnp.dot(flattened, weight_f32, precision=lax.Precision.HIGHEST)
        return result.reshape(block_rows, col_count, -1)

    starts = jnp.arange(row_count // block_rows) * block_rows
    return lax.map(project_block, starts).reshape(row_count, col_count, -1)


def general_shards(
    homolog_embedding,
    homolog_cell_occupancy,
    peptide_occupancy,
    standardize_multiplier,
    standardize_addend,
    lhs_linear_map,
    lhs_linear_constant,
    rhs_linear_map,
    rhs_linear_constant,
    closing_linear_map,
    closing_linear_constant,
):
    occupied_indicator = (homolog_cell_occupancy * peptide_occupancy[None, :]).astype(jnp.float32)
    report_text = homolog_embedding.astype(jnp.float32)
    average = jnp.mean(report_text, axis=-1, keepdims=True)
    spread = jnp.mean(jnp.square(report_text - average), axis=-1, keepdims=True)
    normed = (
        (report_text - average) * lax.rsqrt(spread + 1e-05) * standardize_multiplier
        + standardize_addend
    ).astype(jnp.bfloat16)
    left = project_side(normed, occupied_indicator, lhs_linear_map, lhs_linear_constant)
    right = project_side(normed, occupied_indicator, rhs_linear_map, rhs_linear_constant)
    mask_bf = occupied_indicator.astype(jnp.bfloat16)
    left_col, right_col, mask_col = (
        lax.all_gather(left, "row", axis=1, tiled=True),
        lax.all_gather(right, "row", axis=1, tiled=True),
        lax.all_gather(mask_bf, "row", axis=1, tiled=True),
    )
    row_devices = lax.axis_size("row")
    col_devices = lax.axis_size("col")
    col_len = left_col.shape[1]
    row_len = col_len * col_devices // row_devices
    row_index = lax.axis_index("row")
    root_col = row_index * col_devices // row_devices
    offset = row_index * row_len % col_len
    whole_left, whole_mask = (
        from_root(left_col, "col", root_col),
        from_root(mask_col, "col", root_col),
    )
    left_row = lax.dynamic_slice_in_dim(whole_left, offset, row_len, 1)
    mask_row = lax.dynamic_slice_in_dim(whole_mask, offset, row_len, 1)
    partial_value = pair_rows(left_row, right_col, closing_linear_map)
    mask_rows_all, mask_cols_all = (
        lax.all_gather(mask_row, "seq", axis=0, tiled=True),
        lax.all_gather(mask_col, "seq", axis=0, tiled=True),
    )
    counts_full = jnp.dot(mask_rows_all.T, mask_cols_all, preferred_element_type=jnp.float32)
    summed = lax.psum_scatter(
        partial_value.astype(jnp.bfloat16), "seq", scatter_dimension=1, tiled=True
    ).astype(jnp.float32)
    seq_devices = lax.axis_size("seq")
    part_cols = col_len // seq_devices
    counts = lax.dynamic_slice_in_dim(counts_full, lax.axis_index("seq") * part_cols, part_cols, 1)
    return ((summed + closing_linear_constant) / jnp.maximum(counts, 1.0)[:, :, None]).astype(
        jnp.bfloat16
    )


def project_kernel(
    pept_hbm, x_hbm, occ_hbm, gain_hbm, shift_hbm, wl_hbm, bl_hbm, wr_hbm, br_hbm,
    left_ref, right_ref,
    pept_ref, x_ref, occ_ref, gain_ref, shift_ref, wl_ref, bl_ref, wr_ref, br_ref,
    y_ref, l_ref, x_sems, sems,
):
    residues, sequences = occ_ref.shape
    hidden = wl_ref.shape[0]
    chunks = x_sems.shape[0]
    size = x_ref.shape[0] // chunks
    x_copies = [
        pltpu.make_async_copy(
            x_hbm.at[pl.ds(n * size, size)], x_ref.at[pl.ds(n * size, size)], x_sems.at[n]
        )
        for n in range(chunks)
    ]
    pairs = (
        (wl_hbm, wl_ref), (wr_hbm, wr_ref), (gain_hbm, gain_ref), (shift_hbm, shift_ref),
        (bl_hbm, bl_ref), (br_hbm, br_ref), (occ_hbm, occ_ref), (pept_hbm, pept_ref),
    )
    copies = [pltpu.make_async_copy(a, b, sems.at[n]) for n, (a, b) in enumerate(pairs)]
    x_copies[0].start()
    for copy in copies:
        copy.start()
    for copy in x_copies[1:]:
        copy.start()
    for copy in copies:
        copy.wait()
    weight = jnp.concatenate([wl_ref[...], wr_ref[...]], axis=0)
    bias = jnp.concatenate([bl_ref[...], br_ref[...]], axis=1)
    for n, copy in enumerate(x_copies):
        copy.wait()
        x = x_ref[n * size : (n + 1) * size, :].astype(jnp.float32)
        average = jnp.mean(x, axis=-1, keepdims=True)
        centred = x - average
        spread = jnp.mean(jnp.square(centred), axis=-1, keepdims=True)
        normed = (centred * lax.rsqrt(spread + 1e-05) * gain_ref[...] + shift_ref[...]).astype(
            jnp.bfloat16
        )
        y = lax.dot_general(normed, weight, NT, preferred_element_type=jnp.float32) + bias
        y_ref[n * size : (n + 1) * size, : 2 * hidden] = y
    for i in range(residues):
        live = (occ_ref[i : i + 1, :] * pept_ref[i]).astype(jnp.float32)
        part = y_ref[pl.ds(i, sequences, stride=residues), :].T[: 2 * hidden] * live
        l_ref[pl.ds(i, hidden, stride=residues), :] = part[:hidden]
        right_ref[i * hidden : (i + 1) * hidden, :] = part[hidden:].astype(jnp.bfloat16)
        l_ref[hidden * residues + i : hidden * residues + i + 1, :] = live
    l_ref[hidden * residues + residues :, :] = jnp.zeros((MASK_ROWS - residues, sequences), jnp.float32)
    left_ref[...] = l_ref[...].astype(jnp.bfloat16)
    right_ref[hidden * residues :, :] = l_ref[hidden * residues :, :].astype(jnp.bfloat16)


def expand(tile, store, hidden):
    rows, lanes = tile.shape
    per_vector = 128 // hidden
    lane = lax.broadcasted_iota(jnp.int32, (rows, 128), 1) // hidden
    for g in range(lanes // 128):
        part = tile[:, g * 128 : (g + 1) * 128]
        for a in range(per_vector):
            first = (g * per_vector + a) * rows
            store(first, part * (lane == a).astype(jnp.bfloat16))


def keep_kernel(right_ref, w_ref, b_ref, right_out, w_out, b_out):
    hidden = 32
    right_out[...] = right_ref[...]
    b_out[...] = b_ref[...]
    for c in range(hidden):
        block = w_ref[c * hidden : (c + 1) * hidden, :]
        for a in range(128 // hidden):
            w_out[c * 128 + a * hidden : c * 128 + (a + 1) * hidden, :] = block


def pair_kernel(
    own, l0, l1, r0, r1, r2, r3, w_ref, b_ref, out_ref, ls_ref, rs_ref, big_ref
):
    body = l0.shape[0] - MASK_ROWS
    hidden = 32
    residues = body // hidden
    row, col, seq = (lax.axis_index(name) for name in GROUP)
    for k, piece in enumerate((l0, l1)):
        ls_ref[col ^ k] = piece[...]
    for k, piece in enumerate((r0, r1, r2, r3)):
        rs_ref[row ^ k] = piece[...]
    half = 2 * (seq if own else 1 - seq)

    def rows(ref, at, first, last):
        return jnp.concatenate([ref[at + p, first:last, :] for p in range(2)], axis=0)

    outer = lax.dot_general(
        rows(ls_ref, 0, 0, body), rows(rs_ref, half, 0, body), NT, preferred_element_type=jnp.float32
    )
    live_i = rows(ls_ref, 0, body, body + MASK_ROWS)
    live_j = rows(rs_ref, half, body, body + MASK_ROWS)
    live_j = jnp.concatenate([live_j, jnp.zeros((128 - 2 * MASK_ROWS, live_j.shape[1]), live_j.dtype)], axis=0)
    counts = lax.dot_general(live_i, live_j, NT, preferred_element_type=jnp.float32)
    for c in range(hidden):
        tile = jnp.concatenate(
            [outer[p * body + c * residues : p * body + (c + 1) * residues] for p in range(2)], axis=0
        ).astype(jnp.bfloat16)

        def store(first, value, c=c):
            big_ref[first : first + 2 * residues, c * 128 : (c + 1) * 128] = value

        expand(tile, store, hidden)
    pairs = 4 * residues * residues
    projected = jnp.dot(big_ref[...], w_ref[...], preferred_element_type=jnp.float32)
    if own:
        projected = projected + b_ref[...]
    out_ref[:pairs, :] = projected.astype(out_ref.dtype)
    out_ref[pairs:, :] = counts.astype(out_ref.dtype)


def finish_kernel(mine_ref, other_ref, out_ref, big_ref, p_ref):
    residues = out_ref.shape[0] // 2
    pairs = 4 * residues * residues
    hidden = 32
    counts = mine_ref[pairs:, :] + other_ref[pairs:, :].astype(jnp.float32)
    spread_shape = (128, 2 * residues * hidden)
    at_row = lax.broadcasted_iota(jnp.int32, spread_shape, 0)
    at_lane = lax.broadcasted_iota(jnp.int32, spread_shape, 1)
    hit = ((at_row // MASK_ROWS) * residues + at_row % MASK_ROWS == at_lane // hidden) & (
        at_row % MASK_ROWS < residues
    )
    counts = jnp.dot(
        counts.astype(jnp.bfloat16), hit.astype(jnp.bfloat16), preferred_element_type=jnp.float32
    )
    tile = jnp.concatenate(
        [counts[p * MASK_ROWS : p * MASK_ROWS + residues] for p in range(2)], axis=0
    ).astype(jnp.bfloat16)

    def store(first, value):
        big_ref[first : first + 2 * residues, :] = value

    expand(tile, store, hidden)
    share = jnp.full((128, 128), 1.0 / hidden, jnp.bfloat16)
    divisor = jnp.dot(big_ref[...], share, preferred_element_type=jnp.float32)
    total = mine_ref[:pairs, :] + other_ref[:pairs, :].astype(jnp.float32)
    p_ref[...] = total / jnp.maximum(divisor, 1.0)
    for i in range(2 * residues):
        out_ref[i] = p_ref[pl.ds(i, 2 * residues, stride=2 * residues), :].astype(jnp.bfloat16)


def route(target):
    return [
        (4 * r + 2 * c + q, 4 * to[0] + 2 * to[1] + to[2])
        for r in range(4)
        for c in range(2)
        for q in range(2)
        for to in (target(r, c, q),)
    ]


def direct_shards(
    homolog_embedding,
    homolog_cell_occupancy,
    peptide_occupancy,
    standardize_multiplier,
    standardize_addend,
    lhs_linear_map,
    lhs_linear_constant,
    rhs_linear_map,
    rhs_linear_constant,
    closing_linear_map,
    closing_linear_constant,
):
    sequences, residues, signal = homolog_embedding.shape
    hidden = lhs_linear_map.shape[1]
    width = closing_linear_map.shape[1]
    rows = residues * hidden + MASK_ROWS
    pairs = 4 * residues * residues
    payload = jax.ShapeDtypeStruct((rows, sequences), jnp.bfloat16)
    vmem = pl.BlockSpec(memory_space=pltpu.VMEM)
    in_hbm = pl.BlockSpec(memory_space=pltpu.HBM)
    left, right = pl.pallas_call(
        project_kernel,
        out_shape=(payload, payload),
        in_specs=[in_hbm] * 9,
        out_specs=(vmem, vmem),
        scratch_shapes=[
            pltpu.SMEM((residues,), jnp.int32),
            pltpu.VMEM((sequences * residues, signal), jnp.bfloat16),
            pltpu.VMEM((residues, sequences), jnp.int32),
            pltpu.VMEM((1, signal), jnp.float32),
            pltpu.VMEM((1, signal), jnp.float32),
            pltpu.VMEM((hidden, signal), jnp.bfloat16),
            pltpu.VMEM((1, hidden), jnp.float32),
            pltpu.VMEM((hidden, signal), jnp.bfloat16),
            pltpu.VMEM((1, hidden), jnp.float32),
            pltpu.VMEM((sequences * residues, 128), jnp.float32),
            pltpu.VMEM((rows, sequences), jnp.float32),
            pltpu.SemaphoreType.DMA((4,)),
            pltpu.SemaphoreType.DMA((8,)),
        ],
        compiler_params=pltpu.CompilerParams(vmem_limit_bytes=60 * 1024 * 1024),
        name="normalize_and_project",
    )(
        peptide_occupancy,
        homolog_embedding.reshape(sequences * residues, signal),
        homolog_cell_occupancy.T,
        standardize_multiplier.reshape(1, signal),
        standardize_addend.reshape(1, signal),
        lhs_linear_map.T,
        lhs_linear_constant.reshape(1, hidden),
        rhs_linear_map.T,
        rhs_linear_constant.reshape(1, hidden),
    )
    far = lax.ppermute(right, GROUP, route(lambda r, c, q: (r ^ 2, c, q)))
    near = lax.ppermute(right, GROUP, route(lambda r, c, q: (r ^ 1, c, q)))
    first = lax.ppermute(left, GROUP, route(lambda r, c, q: (2 * c + r // 2, r % 2, q)))
    passed = lax.ppermute(far, GROUP, route(lambda r, c, q: (r ^ 1, c, q)))
    second = lax.ppermute(first, GROUP, route(lambda r, c, q: (r, 1 - c, q)))
    kept, weight, bias = pl.pallas_call(
        keep_kernel,
        out_shape=(
            payload,
            jax.ShapeDtypeStruct((hidden * 128, width), jnp.bfloat16),
            jax.ShapeDtypeStruct((1, width), jnp.float32),
        ),
        in_specs=[vmem] * 3,
        out_specs=(vmem,) * 3,
        compiler_params=pltpu.CompilerParams(vmem_limit_bytes=16 * 1024 * 1024),
        cost_estimate=pl.CostEstimate(flops=0, bytes_accessed=1 << 22, transcendentals=0),
        name="keep",
    )(right, closing_linear_map, closing_linear_constant.reshape(1, width))
    rights = [kept, near, far, passed]
    lefts = [first, second]

    def pair_sums(own, kind):
        return pl.pallas_call(
            lambda *refs: pair_kernel(own, *refs),
            out_shape=jax.ShapeDtypeStruct((pairs + 2 * MASK_ROWS, width), kind),
            in_specs=[vmem] * 8,
            out_specs=vmem,
            scratch_shapes=[
                pltpu.VMEM((2, rows, sequences), jnp.bfloat16),
                pltpu.VMEM((4, rows, sequences), jnp.bfloat16),
                pltpu.VMEM((pairs, hidden * 128), jnp.bfloat16),
            ],
            compiler_params=pltpu.CompilerParams(vmem_limit_bytes=24 * 1024 * 1024),
            cost_estimate=pl.CostEstimate(
                flops=2 * pairs * hidden * 128 * width, bytes_accessed=1 << 20, transcendentals=0
            ),
            name="own_pair_sums" if own else "other_pair_sums",
        )(*lefts, *rights, weight, bias)

    theirs = pair_sums(False, jnp.bfloat16)
    received = lax.ppermute(theirs, GROUP, route(lambda r, c, q: (r, c, 1 - q)))
    mine = pair_sums(True, jnp.float32)
    return pl.pallas_call(
        finish_kernel,
        out_shape=jax.ShapeDtypeStruct((2 * residues, 2 * residues, width), jnp.bfloat16),
        in_specs=[vmem] * 2,
        out_specs=vmem,
        scratch_shapes=[
            pltpu.VMEM((pairs, 128), jnp.bfloat16),
            pltpu.VMEM((pairs, width), jnp.float32),
        ],
        compiler_params=pltpu.CompilerParams(vmem_limit_bytes=16 * 1024 * 1024),
        name="divide",
    )(mine, received)


def shards(*arrays):
    sizes = tuple(lax.axis_size(name) for name in GROUP)
    if sizes == (4, 2, 2) and arrays[0].shape[:2] == (128, 8):
        return direct_shards(*arrays)
    return general_shards(*arrays)


def solution(mesh):
    return jax.shard_map(
        shards,
        mesh=mesh,
        in_specs=(
            P(("crops", "seq"), ("col", "row"), None),
            P(("crops", "seq"), ("col", "row")),
            P(("crops", "col", "row")),
            P(),
            P(),
            P(),
            P(),
            P(),
            P(),
            P(),
            P(),
        ),
        out_specs=P(("crops", "row"), ("col", "seq"), None),
        check_vma=False,
    )
```

```python
import math

import jax
import jax.numpy as jnp
from jax import lax
from jax.experimental import pallas as pl
from jax.experimental.pallas import tpu as pltpu
from jax.sharding import PartitionSpec as P

GROUP = ("row", "col", "seq")
NT = (((1,), (1,)), ((), ()))
MASK_ROWS = 16


def from_root(x, axis, root):
    mine = lax.axis_index(axis) == root
    return lax.psum(jnp.where(mine, x, jnp.zeros_like(x)), axis)


def project_side(normed, occupied_indicator, weight, bias):
    seq_count, res_count, width = normed.shape
    report_text = jnp.dot(
        normed.reshape(seq_count * res_count, width), weight, preferred_element_type=jnp.float32
    )
    report_text = (report_text + bias).reshape(seq_count, res_count, -1) * occupied_indicator[
        :, :, None
    ]
    return report_text.astype(jnp.bfloat16)


def pair_rows(left, right, closing_linear_map):
    row_count = left.shape[1]
    col_count = right.shape[1]
    block_rows = math.gcd(row_count, max(1, 512 // col_count))
    weight_f32 = closing_linear_map.astype(jnp.float32)

    def project_block(first_row):
        left_block = lax.dynamic_slice_in_dim(left, first_row, block_rows, 1)
        outer_prod = jnp.einsum(
            "sic,sjd->ijcd", left_block, right, preferred_element_type=jnp.float32
        )
        flattened = outer_prod.reshape(block_rows * col_count, -1)
        result = jnp.dot(flattened, weight_f32, precision=lax.Precision.HIGHEST)
        return result.reshape(block_rows, col_count, -1)

    starts = jnp.arange(row_count // block_rows) * block_rows
    return lax.map(project_block, starts).reshape(row_count, col_count, -1)


def general_shards(
    homolog_embedding,
    homolog_cell_occupancy,
    peptide_occupancy,
    standardize_multiplier,
    standardize_addend,
    lhs_linear_map,
    lhs_linear_constant,
    rhs_linear_map,
    rhs_linear_constant,
    closing_linear_map,
    closing_linear_constant,
):
    occupied_indicator = (homolog_cell_occupancy * peptide_occupancy[None, :]).astype(jnp.float32)
    report_text = homolog_embedding.astype(jnp.float32)
    average = jnp.mean(report_text, axis=-1, keepdims=True)
    spread = jnp.mean(jnp.square(report_text - average), axis=-1, keepdims=True)
    normed = (
        (report_text - average) * lax.rsqrt(spread + 1e-05) * standardize_multiplier
        + standardize_addend
    ).astype(jnp.bfloat16)
    left = project_side(normed, occupied_indicator, lhs_linear_map, lhs_linear_constant)
    right = project_side(normed, occupied_indicator, rhs_linear_map, rhs_linear_constant)
    mask_bf = occupied_indicator.astype(jnp.bfloat16)
    left_col, right_col, mask_col = (
        lax.all_gather(left, "row", axis=1, tiled=True),
        lax.all_gather(right, "row", axis=1, tiled=True),
        lax.all_gather(mask_bf, "row", axis=1, tiled=True),
    )
    row_devices = lax.axis_size("row")
    col_devices = lax.axis_size("col")
    col_len = left_col.shape[1]
    row_len = col_len * col_devices // row_devices
    row_index = lax.axis_index("row")
    root_col = row_index * col_devices // row_devices
    offset = row_index * row_len % col_len
    whole_left, whole_mask = (
        from_root(left_col, "col", root_col),
        from_root(mask_col, "col", root_col),
    )
    left_row = lax.dynamic_slice_in_dim(whole_left, offset, row_len, 1)
    mask_row = lax.dynamic_slice_in_dim(whole_mask, offset, row_len, 1)
    partial_value = pair_rows(left_row, right_col, closing_linear_map)
    mask_rows_all, mask_cols_all = (
        lax.all_gather(mask_row, "seq", axis=0, tiled=True),
        lax.all_gather(mask_col, "seq", axis=0, tiled=True),
    )
    counts_full = jnp.dot(mask_rows_all.T, mask_cols_all, preferred_element_type=jnp.float32)
    summed = lax.psum_scatter(
        partial_value.astype(jnp.bfloat16), "seq", scatter_dimension=1, tiled=True
    ).astype(jnp.float32)
    seq_devices = lax.axis_size("seq")
    part_cols = col_len // seq_devices
    counts = lax.dynamic_slice_in_dim(counts_full, lax.axis_index("seq") * part_cols, part_cols, 1)
    return ((summed + closing_linear_constant) / jnp.maximum(counts, 1.0)[:, :, None]).astype(
        jnp.bfloat16
    )


def project_kernel(
    pept_hbm, x_hbm, occ_hbm, gain_hbm, shift_hbm, wl_hbm, bl_hbm, wr_hbm, br_hbm,
    left_ref, right_ref,
    pept_ref, x_ref, occ_ref, gain_ref, shift_ref, wl_ref, bl_ref, wr_ref, br_ref,
    y_ref, l_ref, x_sems, sems,
):
    residues, sequences = occ_ref.shape
    hidden = wl_ref.shape[0]
    chunks = x_sems.shape[0]
    size = x_ref.shape[0] // chunks
    x_copies = [
        pltpu.make_async_copy(
            x_hbm.at[pl.ds(n * size, size)], x_ref.at[pl.ds(n * size, size)], x_sems.at[n]
        )
        for n in range(chunks)
    ]
    pairs = (
        (wl_hbm, wl_ref), (wr_hbm, wr_ref), (gain_hbm, gain_ref), (shift_hbm, shift_ref),
        (bl_hbm, bl_ref), (br_hbm, br_ref), (occ_hbm, occ_ref), (pept_hbm, pept_ref),
    )
    copies = [pltpu.make_async_copy(a, b, sems.at[n]) for n, (a, b) in enumerate(pairs)]
    x_copies[0].start()
    for copy in copies:
        copy.start()
    for copy in x_copies[1:]:
        copy.start()
    for copy in copies:
        copy.wait()
    weight = jnp.concatenate([wl_ref[...], wr_ref[...]], axis=0)
    bias = jnp.concatenate([bl_ref[...], br_ref[...]], axis=1)
    for n, copy in enumerate(x_copies):
        copy.wait()
        x = x_ref[n * size : (n + 1) * size, :].astype(jnp.float32)
        average = jnp.mean(x, axis=-1, keepdims=True)
        centred = x - average
        spread = jnp.mean(jnp.square(centred), axis=-1, keepdims=True)
        normed = (centred * lax.rsqrt(spread + 1e-05) * gain_ref[...] + shift_ref[...]).astype(
            jnp.bfloat16
        )
        y = lax.dot_general(normed, weight, NT, preferred_element_type=jnp.float32) + bias
        y_ref[n * size : (n + 1) * size, : 2 * hidden] = y
    for i in range(residues):
        live = (occ_ref[i : i + 1, :] * pept_ref[i]).astype(jnp.float32)
        part = y_ref[pl.ds(i, sequences, stride=residues), :].T[: 2 * hidden] * live
        l_ref[pl.ds(i, hidden, stride=residues), :] = part[:hidden]
        mine = part[hidden:].astype(jnp.bfloat16)
        for n in range(right_ref.shape[0]):
            right_ref[n, i * hidden : (i + 1) * hidden, :] = mine
        l_ref[hidden * residues + i : hidden * residues + i + 1, :] = live
    l_ref[hidden * residues + residues :, :] = jnp.zeros((MASK_ROWS - residues, sequences), jnp.float32)
    left_ref[...] = l_ref[...].astype(jnp.bfloat16)
    masks = l_ref[hidden * residues :, :].astype(jnp.bfloat16)
    for n in range(right_ref.shape[0]):
        right_ref[n, hidden * residues :, :] = masks


def expand(tile, store, hidden):
    rows, lanes = tile.shape
    per_vector = 128 // hidden
    lane = lax.broadcasted_iota(jnp.int32, (rows, 128), 1) // hidden
    for g in range(lanes // 128):
        part = tile[:, g * 128 : (g + 1) * 128]
        for a in range(per_vector):
            first = (g * per_vector + a) * rows
            store(first, part * (lane == a).astype(jnp.bfloat16))


def keep_kernel(w_ref, b_ref, w_out, b_out):
    hidden = 32
    b_out[...] = b_ref[...]
    for c in range(hidden):
        block = w_ref[c * hidden : (c + 1) * hidden, :]
        for a in range(128 // hidden):
            w_out[c * 128 + a * hidden : c * 128 + (a + 1) * hidden, :] = block


def pair_kernel(
    own, l0, l1, rs_ref, w_ref, b_ref, out_ref, ls_ref, big_ref
):
    body = l0.shape[0] - MASK_ROWS
    hidden = 32
    residues = body // hidden
    col, seq = lax.axis_index("col"), lax.axis_index("seq")
    for k, piece in enumerate((l0, l1)):
        ls_ref[col ^ k] = piece[...]
    half = 2 * (seq if own else 1 - seq)

    def rows(ref, at, first, last):
        return jnp.concatenate([ref[at + p, first:last, :] for p in range(2)], axis=0)

    outer = lax.dot_general(
        rows(ls_ref, 0, 0, body), rows(rs_ref, half, 0, body), NT, preferred_element_type=jnp.float32
    )
    live_i = rows(ls_ref, 0, body, body + MASK_ROWS)
    live_j = rows(rs_ref, half, body, body + MASK_ROWS)
    live_j = jnp.concatenate([live_j, jnp.zeros((128 - 2 * MASK_ROWS, live_j.shape[1]), live_j.dtype)], axis=0)
    counts = lax.dot_general(live_i, live_j, NT, preferred_element_type=jnp.float32)
    for c in range(hidden):
        tile = jnp.concatenate(
            [outer[p * body + c * residues : p * body + (c + 1) * residues] for p in range(2)], axis=0
        ).astype(jnp.bfloat16)

        def store(first, value, c=c):
            big_ref[first : first + 2 * residues, c * 128 : (c + 1) * 128] = value

        expand(tile, store, hidden)
    pairs = 4 * residues * residues
    projected = jnp.dot(big_ref[...], w_ref[...], preferred_element_type=jnp.float32)
    if own:
        projected = projected + b_ref[...]
    out_ref[:pairs, :] = projected.astype(out_ref.dtype)
    out_ref[pairs:, :] = counts.astype(out_ref.dtype)


def finish_kernel(mine_ref, other_ref, out_ref, big_ref, p_ref):
    residues = out_ref.shape[0] // 2
    pairs = 4 * residues * residues
    hidden = 32
    counts = mine_ref[pairs:, :] + other_ref[pairs:, :].astype(jnp.float32)
    spread_shape = (128, 2 * residues * hidden)
    at_row = lax.broadcasted_iota(jnp.int32, spread_shape, 0)
    at_lane = lax.broadcasted_iota(jnp.int32, spread_shape, 1)
    hit = ((at_row // MASK_ROWS) * residues + at_row % MASK_ROWS == at_lane // hidden) & (
        at_row % MASK_ROWS < residues
    )
    counts = jnp.dot(
        counts.astype(jnp.bfloat16), hit.astype(jnp.bfloat16), preferred_element_type=jnp.float32
    )
    tile = jnp.concatenate(
        [counts[p * MASK_ROWS : p * MASK_ROWS + residues] for p in range(2)], axis=0
    ).astype(jnp.bfloat16)

    def store(first, value):
        big_ref[first : first + 2 * residues, :] = value

    expand(tile, store, hidden)
    share = jnp.full((128, 128), 1.0 / hidden, jnp.bfloat16)
    divisor = jnp.dot(big_ref[...], share, preferred_element_type=jnp.float32)
    total = mine_ref[:pairs, :] + other_ref[:pairs, :].astype(jnp.float32)
    p_ref[...] = total / jnp.maximum(divisor, 1.0)
    for i in range(2 * residues):
        out_ref[i] = p_ref[pl.ds(i, 2 * residues, stride=2 * residues), :].astype(jnp.bfloat16)


def route(target):
    return [
        (4 * r + 2 * c + q, 4 * to[0] + 2 * to[1] + to[2])
        for r in range(4)
        for c in range(2)
        for q in range(2)
        for to in (target(r, c, q),)
    ]


def direct_shards(
    homolog_embedding,
    homolog_cell_occupancy,
    peptide_occupancy,
    standardize_multiplier,
    standardize_addend,
    lhs_linear_map,
    lhs_linear_constant,
    rhs_linear_map,
    rhs_linear_constant,
    closing_linear_map,
    closing_linear_constant,
):
    sequences, residues, signal = homolog_embedding.shape
    hidden = lhs_linear_map.shape[1]
    width = closing_linear_map.shape[1]
    rows = residues * hidden + MASK_ROWS
    pairs = 4 * residues * residues
    payload = jax.ShapeDtypeStruct((rows, sequences), jnp.bfloat16)
    payloads = jax.ShapeDtypeStruct((lax.axis_size("row"), rows, sequences), jnp.bfloat16)
    vmem = pl.BlockSpec(memory_space=pltpu.VMEM)
    in_hbm = pl.BlockSpec(memory_space=pltpu.HBM)
    left, right = pl.pallas_call(
        project_kernel,
        out_shape=(payload, payloads),
        in_specs=[in_hbm] * 9,
        out_specs=(vmem, vmem),
        scratch_shapes=[
            pltpu.SMEM((residues,), jnp.int32),
            pltpu.VMEM((sequences * residues, signal), jnp.bfloat16),
            pltpu.VMEM((residues, sequences), jnp.int32),
            pltpu.VMEM((1, signal), jnp.float32),
            pltpu.VMEM((1, signal), jnp.float32),
            pltpu.VMEM((hidden, signal), jnp.bfloat16),
            pltpu.VMEM((1, hidden), jnp.float32),
            pltpu.VMEM((hidden, signal), jnp.bfloat16),
            pltpu.VMEM((1, hidden), jnp.float32),
            pltpu.VMEM((sequences * residues, 128), jnp.float32),
            pltpu.VMEM((rows, sequences), jnp.float32),
            pltpu.SemaphoreType.DMA((4,)),
            pltpu.SemaphoreType.DMA((8,)),
        ],
        compiler_params=pltpu.CompilerParams(vmem_limit_bytes=60 * 1024 * 1024),
        name="normalize_and_project",
    )(
        peptide_occupancy,
        homolog_embedding.reshape(sequences * residues, signal),
        homolog_cell_occupancy.T,
        standardize_multiplier.reshape(1, signal),
        standardize_addend.reshape(1, signal),
        lhs_linear_map.T,
        lhs_linear_constant.reshape(1, hidden),
        rhs_linear_map.T,
        rhs_linear_constant.reshape(1, hidden),
    )
    rights = lax.all_to_all(right, "row", 0, 0)
    first = lax.ppermute(left, GROUP, route(lambda r, c, q: (2 * c + r // 2, r % 2, q)))
    second = lax.ppermute(first, GROUP, route(lambda r, c, q: (r, 1 - c, q)))
    weight, bias = pl.pallas_call(
        keep_kernel,
        out_shape=(
            jax.ShapeDtypeStruct((hidden * 128, width), jnp.bfloat16),
            jax.ShapeDtypeStruct((1, width), jnp.float32),
        ),
        in_specs=[vmem] * 2,
        out_specs=(vmem,) * 2,
        compiler_params=pltpu.CompilerParams(vmem_limit_bytes=16 * 1024 * 1024),
        cost_estimate=pl.CostEstimate(flops=0, bytes_accessed=1 << 22, transcendentals=0),
        name="keep",
    )(closing_linear_map, closing_linear_constant.reshape(1, width))
    lefts = [first, second]

    def pair_sums(own, kind):
        return pl.pallas_call(
            lambda *refs: pair_kernel(own, *refs),
            out_shape=jax.ShapeDtypeStruct((pairs + 2 * MASK_ROWS, width), kind),
            in_specs=[vmem] * 5,
            out_specs=vmem,
            scratch_shapes=[
                pltpu.VMEM((2, rows, sequences), jnp.bfloat16),
                pltpu.VMEM((pairs, hidden * 128), jnp.bfloat16),
            ],
            compiler_params=pltpu.CompilerParams(vmem_limit_bytes=24 * 1024 * 1024),
            cost_estimate=pl.CostEstimate(
                flops=2 * pairs * hidden * 128 * width, bytes_accessed=1 << 20, transcendentals=0
            ),
            name="own_pair_sums" if own else "other_pair_sums",
        )(*lefts, rights, weight, bias)

    theirs = pair_sums(False, jnp.bfloat16)
    received = lax.ppermute(theirs, GROUP, route(lambda r, c, q: (r, c, 1 - q)))
    mine = pair_sums(True, jnp.float32)
    return pl.pallas_call(
        finish_kernel,
        out_shape=jax.ShapeDtypeStruct((2 * residues, 2 * residues, width), jnp.bfloat16),
        in_specs=[vmem] * 2,
        out_specs=vmem,
        scratch_shapes=[
            pltpu.VMEM((pairs, 128), jnp.bfloat16),
            pltpu.VMEM((pairs, width), jnp.float32),
        ],
        compiler_params=pltpu.CompilerParams(vmem_limit_bytes=16 * 1024 * 1024),
        name="divide",
    )(mine, received)


def shards(*arrays):
    sizes = tuple(lax.axis_size(name) for name in GROUP)
    if sizes == (4, 2, 2) and arrays[0].shape[:2] == (128, 8):
        return direct_shards(*arrays)
    return general_shards(*arrays)


def solution(mesh):
    return jax.shard_map(
        shards,
        mesh=mesh,
        in_specs=(
            P(("crops", "seq"), ("col", "row"), None),
            P(("crops", "seq"), ("col", "row")),
            P(("crops", "col", "row")),
            P(),
            P(),
            P(),
            P(),
            P(),
            P(),
            P(),
            P(),
        ),
        out_specs=P(("crops", "row"), ("col", "seq"), None),
        check_vma=False,
    )
```

```python
import math

import jax
import jax.numpy as jnp
from jax import lax
from jax.experimental import pallas as pl
from jax.experimental.pallas import tpu as pltpu
from jax.sharding import PartitionSpec as P

GROUP = ("row", "col", "seq")
NT = (((1,), (1,)), ((), ()))
MASK_ROWS = 16
WIDE = 2


def from_root(x, axis, root):
    mine = lax.axis_index(axis) == root
    return lax.psum(jnp.where(mine, x, jnp.zeros_like(x)), axis)


def project_side(normed, occupied_indicator, weight, bias):
    seq_count, res_count, width = normed.shape
    report_text = jnp.dot(
        normed.reshape(seq_count * res_count, width), weight, preferred_element_type=jnp.float32
    )
    report_text = (report_text + bias).reshape(seq_count, res_count, -1) * occupied_indicator[
        :, :, None
    ]
    return report_text.astype(jnp.bfloat16)


def pair_rows(left, right, closing_linear_map):
    row_count = left.shape[1]
    col_count = right.shape[1]
    block_rows = math.gcd(row_count, max(1, 512 // col_count))
    weight_f32 = closing_linear_map.astype(jnp.float32)

    def project_block(first_row):
        left_block = lax.dynamic_slice_in_dim(left, first_row, block_rows, 1)
        outer_prod = jnp.einsum(
            "sic,sjd->ijcd", left_block, right, preferred_element_type=jnp.float32
        )
        flattened = outer_prod.reshape(block_rows * col_count, -1)
        result = jnp.dot(flattened, weight_f32, precision=lax.Precision.HIGHEST)
        return result.reshape(block_rows, col_count, -1)

    starts = jnp.arange(row_count // block_rows) * block_rows
    return lax.map(project_block, starts).reshape(row_count, col_count, -1)


def general_shards(
    homolog_embedding,
    homolog_cell_occupancy,
    peptide_occupancy,
    standardize_multiplier,
    standardize_addend,
    lhs_linear_map,
    lhs_linear_constant,
    rhs_linear_map,
    rhs_linear_constant,
    closing_linear_map,
    closing_linear_constant,
):
    occupied_indicator = (homolog_cell_occupancy * peptide_occupancy[None, :]).astype(jnp.float32)
    report_text = homolog_embedding.astype(jnp.float32)
    average = jnp.mean(report_text, axis=-1, keepdims=True)
    spread = jnp.mean(jnp.square(report_text - average), axis=-1, keepdims=True)
    normed = (
        (report_text - average) * lax.rsqrt(spread + 1e-05) * standardize_multiplier
        + standardize_addend
    ).astype(jnp.bfloat16)
    left = project_side(normed, occupied_indicator, lhs_linear_map, lhs_linear_constant)
    right = project_side(normed, occupied_indicator, rhs_linear_map, rhs_linear_constant)
    mask_bf = occupied_indicator.astype(jnp.bfloat16)
    left_col, right_col, mask_col = (
        lax.all_gather(left, "row", axis=1, tiled=True),
        lax.all_gather(right, "row", axis=1, tiled=True),
        lax.all_gather(mask_bf, "row", axis=1, tiled=True),
    )
    row_devices = lax.axis_size("row")
    col_devices = lax.axis_size("col")
    col_len = left_col.shape[1]
    row_len = col_len * col_devices // row_devices
    row_index = lax.axis_index("row")
    root_col = row_index * col_devices // row_devices
    offset = row_index * row_len % col_len
    whole_left, whole_mask = (
        from_root(left_col, "col", root_col),
        from_root(mask_col, "col", root_col),
    )
    left_row = lax.dynamic_slice_in_dim(whole_left, offset, row_len, 1)
    mask_row = lax.dynamic_slice_in_dim(whole_mask, offset, row_len, 1)
    partial_value = pair_rows(left_row, right_col, closing_linear_map)
    mask_rows_all, mask_cols_all = (
        lax.all_gather(mask_row, "seq", axis=0, tiled=True),
        lax.all_gather(mask_col, "seq", axis=0, tiled=True),
    )
    counts_full = jnp.dot(mask_rows_all.T, mask_cols_all, preferred_element_type=jnp.float32)
    summed = lax.psum_scatter(
        partial_value.astype(jnp.bfloat16), "seq", scatter_dimension=1, tiled=True
    ).astype(jnp.float32)
    seq_devices = lax.axis_size("seq")
    part_cols = col_len // seq_devices
    counts = lax.dynamic_slice_in_dim(counts_full, lax.axis_index("seq") * part_cols, part_cols, 1)
    return ((summed + closing_linear_constant) / jnp.maximum(counts, 1.0)[:, :, None]).astype(
        jnp.bfloat16
    )


def project_kernel(
    pept_hbm, x_hbm, occ_hbm, gain_hbm, shift_hbm, wl_hbm, bl_hbm, wr_hbm, br_hbm,
    right_ref, left_ref,
    pept_ref, x_ref, occ_ref, gain_ref, shift_ref, wl_ref, bl_ref, wr_ref, br_ref,
    y_ref, l_ref, x_sems, sems,
):
    residues, sequences = occ_ref.shape
    hidden = wl_ref.shape[0]
    chunks = x_sems.shape[0]
    size = x_ref.shape[0] // chunks
    x_copies = [
        pltpu.make_async_copy(
            x_hbm.at[pl.ds(n * size, size)], x_ref.at[pl.ds(n * size, size)], x_sems.at[n]
        )
        for n in range(chunks)
    ]
    pairs = (
        (wl_hbm, wl_ref), (wr_hbm, wr_ref), (gain_hbm, gain_ref), (shift_hbm, shift_ref),
        (bl_hbm, bl_ref), (br_hbm, br_ref), (occ_hbm, occ_ref), (pept_hbm, pept_ref),
    )
    copies = [pltpu.make_async_copy(a, b, sems.at[n]) for n, (a, b) in enumerate(pairs)]
    x_copies[0].start()
    for copy in copies:
        copy.start()
    for copy in x_copies[1:]:
        copy.start()
    for copy in copies:
        copy.wait()
    weight = jnp.concatenate([wl_ref[...], wr_ref[...]], axis=0)
    bias = jnp.concatenate([bl_ref[...], br_ref[...]], axis=1)
    for n, copy in enumerate(x_copies):
        copy.wait()
        x = x_ref[n * size : (n + 1) * size, :].astype(jnp.float32)
        average = jnp.mean(x, axis=-1, keepdims=True)
        centred = x - average
        spread = jnp.mean(jnp.square(centred), axis=-1, keepdims=True)
        normed = (centred * lax.rsqrt(spread + 1e-05) * gain_ref[...] + shift_ref[...]).astype(
            jnp.bfloat16
        )
        y = lax.dot_general(normed, weight, NT, preferred_element_type=jnp.float32) + bias
        y_ref[n * size : (n + 1) * size, : 2 * hidden] = y
    for i in range(residues):
        live = (occ_ref[i : i + 1, :] * pept_ref[i]).astype(jnp.float32)
        part = y_ref[pl.ds(i, sequences, stride=residues), :].T[: 2 * hidden] * live
        l_ref[pl.ds(i, hidden, stride=residues), :] = part[:hidden]
        right_ref[i * hidden : (i + 1) * hidden, :] = part[hidden:].astype(jnp.bfloat16)
        l_ref[hidden * residues + i : hidden * residues + i + 1, :] = live
    l_ref[hidden * residues + residues :, :] = jnp.zeros((MASK_ROWS - residues, sequences), jnp.float32)
    left_ref[...] = l_ref[...].astype(jnp.bfloat16)
    right_ref[hidden * residues :, :] = l_ref[hidden * residues :, :].astype(jnp.bfloat16)


def expand(tile, store, hidden, wide):
    rows, lanes = tile.shape
    per_vector = 128 // hidden
    lane = lax.broadcasted_iota(jnp.int32, (rows, 128), 1) // (hidden * wide)
    for g in range(lanes // 128):
        part = tile[:, g * 128 : (g + 1) * 128]
        for a in range(per_vector // wide):
            first = (g * (per_vector // wide) + a) * rows
            store(first, part * (lane == a).astype(jnp.bfloat16))


def keep_kernel(right_ref, left_ref, w_ref, b_ref, right_out, left_out, w_out, b_out):
    hidden = 32
    right_out[...] = right_ref[...]
    left_out[...] = left_ref[...]
    b_out[...] = b_ref[...]
    width = b_ref.shape[1]
    zero = jnp.zeros((hidden, width), jnp.bfloat16)
    for c in range(hidden):
        block = w_ref[c * hidden : (c + 1) * hidden, :]
        for a in range(128 // hidden):
            for n in range(WIDE):
                w_out[c * 128 + a * hidden : c * 128 + (a + 1) * hidden, n * width : (n + 1) * width] = (
                    block if a % WIDE == n else zero
                )


def pair_kernel(
    own, r2, r3, l0, l1, r1, r0, w_ref, b_ref, out_ref, ls_ref, rs_ref, big_ref
):
    body = l0.shape[0] - MASK_ROWS
    hidden = 32
    residues = body // hidden
    row, col, seq = (lax.axis_index(name) for name in GROUP)
    for k, piece in enumerate((l0, l1)):
        ls_ref[col ^ k] = piece[...]
    for k, piece in enumerate((r0, r1, r2, r3)):
        rs_ref[row ^ k] = piece[...]
    half = 2 * (seq if own else 1 - seq)

    def rows(ref, at, first, last):
        return jnp.concatenate([ref[at + p, first:last, :] for p in range(2)], axis=0)

    outer = lax.dot_general(
        rows(ls_ref, 0, 0, body), rows(rs_ref, half, 0, body), NT, preferred_element_type=jnp.float32
    )
    live_i = rows(ls_ref, 0, body, body + MASK_ROWS)
    live_j = rows(rs_ref, half, body, body + MASK_ROWS)
    live_j = jnp.concatenate([live_j, jnp.zeros((128 - 2 * MASK_ROWS, live_j.shape[1]), live_j.dtype)], axis=0)
    counts = lax.dot_general(live_i, live_j, NT, preferred_element_type=jnp.float32)
    for c in range(hidden):
        tile = jnp.concatenate(
            [outer[p * body + c * residues : p * body + (c + 1) * residues] for p in range(2)], axis=0
        ).astype(jnp.bfloat16)

        def store(first, value, c=c):
            big_ref[first : first + 2 * residues, c * 128 : (c + 1) * 128] = value

        expand(tile, store, hidden, WIDE)
    pairs = 4 * residues * residues
    projected = jnp.dot(big_ref[...], w_ref[...], preferred_element_type=jnp.float32)
    width = b_ref.shape[1]
    size = 2 * residues
    for g in range(pairs // (size * WIDE)):
        for n in range(WIDE):
            part = projected[g * size : (g + 1) * size, n * width : (n + 1) * width]
            if own:
                part = part + b_ref[...]
            first = (g * WIDE + n) * size
            out_ref[first : first + size, :] = part.astype(out_ref.dtype)
    out_ref[pairs:, :] = counts.astype(out_ref.dtype)


def finish_kernel(mine_ref, other_ref, out_ref, big_ref, p_ref):
    residues = out_ref.shape[0] // 2
    pairs = 4 * residues * residues
    hidden = 32
    counts = mine_ref[pairs:, :] + other_ref[pairs:, :].astype(jnp.float32)
    spread_shape = (128, 2 * residues * hidden)
    at_row = lax.broadcasted_iota(jnp.int32, spread_shape, 0)
    at_lane = lax.broadcasted_iota(jnp.int32, spread_shape, 1)
    hit = ((at_row // MASK_ROWS) * residues + at_row % MASK_ROWS == at_lane // hidden) & (
        at_row % MASK_ROWS < residues
    )
    counts = jnp.dot(
        counts.astype(jnp.bfloat16), hit.astype(jnp.bfloat16), preferred_element_type=jnp.float32
    )
    tile = jnp.concatenate(
        [counts[p * MASK_ROWS : p * MASK_ROWS + residues] for p in range(2)], axis=0
    ).astype(jnp.bfloat16)

    def store(first, value):
        big_ref[first : first + 2 * residues, :] = value

    expand(tile, store, hidden, 1)
    share = jnp.full((128, 128), 1.0 / hidden, jnp.bfloat16)
    divisor = jnp.dot(big_ref[...], share, preferred_element_type=jnp.float32)
    total = mine_ref[:pairs, :] + other_ref[:pairs, :].astype(jnp.float32)
    p_ref[...] = total / jnp.maximum(divisor, 1.0)
    for i in range(2 * residues):
        out_ref[i] = p_ref[pl.ds(i, 2 * residues, stride=2 * residues), :].astype(jnp.bfloat16)


def route(target):
    return [
        (4 * r + 2 * c + q, 4 * to[0] + 2 * to[1] + to[2])
        for r in range(4)
        for c in range(2)
        for q in range(2)
        for to in (target(r, c, q),)
    ]


def direct_shards(
    homolog_embedding,
    homolog_cell_occupancy,
    peptide_occupancy,
    standardize_multiplier,
    standardize_addend,
    lhs_linear_map,
    lhs_linear_constant,
    rhs_linear_map,
    rhs_linear_constant,
    closing_linear_map,
    closing_linear_constant,
):
    sequences, residues, signal = homolog_embedding.shape
    hidden = lhs_linear_map.shape[1]
    width = closing_linear_map.shape[1]
    rows = residues * hidden + MASK_ROWS
    pairs = 4 * residues * residues
    payload = jax.ShapeDtypeStruct((rows, sequences), jnp.bfloat16)
    vmem = pl.BlockSpec(memory_space=pltpu.VMEM)
    in_hbm = pl.BlockSpec(memory_space=pltpu.HBM)
    right, left = pl.pallas_call(
        project_kernel,
        out_shape=(payload, payload),
        in_specs=[in_hbm] * 9,
        out_specs=(vmem, vmem),
        scratch_shapes=[
            pltpu.SMEM((residues,), jnp.int32),
            pltpu.VMEM((sequences * residues, signal), jnp.bfloat16),
            pltpu.VMEM((residues, sequences), jnp.int32),
            pltpu.VMEM((1, signal), jnp.float32),
            pltpu.VMEM((1, signal), jnp.float32),
            pltpu.VMEM((hidden, signal), jnp.bfloat16),
            pltpu.VMEM((1, hidden), jnp.float32),
            pltpu.VMEM((hidden, signal), jnp.bfloat16),
            pltpu.VMEM((1, hidden), jnp.float32),
            pltpu.VMEM((sequences * residues, 128), jnp.float32),
            pltpu.VMEM((rows, sequences), jnp.float32),
            pltpu.SemaphoreType.DMA((4,)),
            pltpu.SemaphoreType.DMA((8,)),
        ],
        compiler_params=pltpu.CompilerParams(vmem_limit_bytes=60 * 1024 * 1024),
        name="normalize_and_project",
    )(
        peptide_occupancy,
        homolog_embedding.reshape(sequences * residues, signal),
        homolog_cell_occupancy.T,
        standardize_multiplier.reshape(1, signal),
        standardize_addend.reshape(1, signal),
        lhs_linear_map.T,
        lhs_linear_constant.reshape(1, hidden),
        rhs_linear_map.T,
        rhs_linear_constant.reshape(1, hidden),
    )
    kept, left, weight, bias = pl.pallas_call(
        keep_kernel,
        out_shape=(
            payload,
            payload,
            jax.ShapeDtypeStruct((hidden * 128, WIDE * width), jnp.bfloat16),
            jax.ShapeDtypeStruct((1, width), jnp.float32),
        ),
        in_specs=[vmem] * 4,
        out_specs=(vmem,) * 4,
        compiler_params=pltpu.CompilerParams(vmem_limit_bytes=16 * 1024 * 1024),
        cost_estimate=pl.CostEstimate(flops=0, bytes_accessed=1 << 22, transcendentals=0),
        name="keep",
    )(right, left, closing_linear_map, closing_linear_constant.reshape(1, width))

    first = lax.ppermute(left, GROUP, route(lambda r, c, q: (2 * c + r // 2, r % 2, q)))
    second = lax.ppermute(first, GROUP, route(lambda r, c, q: (r, 1 - c, q)))
    far = lax.ppermute(right, GROUP, route(lambda r, c, q: (r ^ 2, c, q)))
    near = lax.ppermute(right, GROUP, route(lambda r, c, q: (r ^ 1, c, q)))
    passed = lax.ppermute(far, GROUP, route(lambda r, c, q: (r ^ 1, c, q)))

    def pair_sums(own, kind):
        return pl.pallas_call(
            lambda *refs: pair_kernel(own, *refs),
            out_shape=jax.ShapeDtypeStruct((pairs + 2 * MASK_ROWS, width), kind),
            in_specs=[vmem] * 8,
            out_specs=vmem,
            scratch_shapes=[
                pltpu.VMEM((2, rows, sequences), jnp.bfloat16),
                pltpu.VMEM((4, rows, sequences), jnp.bfloat16),
                pltpu.VMEM((pairs // WIDE, hidden * 128), jnp.bfloat16),
            ],
            compiler_params=pltpu.CompilerParams(vmem_limit_bytes=24 * 1024 * 1024),
            cost_estimate=pl.CostEstimate(
                flops=2 * pairs * hidden * 128 * width, bytes_accessed=1 << 20, transcendentals=0
            ),
            name="own_pair_sums" if own else "other_pair_sums",
        )(far, passed, first, second, near, kept, weight, bias)

    theirs = pair_sums(False, jnp.bfloat16)
    received = lax.ppermute(theirs, GROUP, route(lambda r, c, q: (r, c, 1 - q)))
    mine = pair_sums(True, jnp.float32)
    return pl.pallas_call(
        finish_kernel,
        out_shape=jax.ShapeDtypeStruct((2 * residues, 2 * residues, width), jnp.bfloat16),
        in_specs=[vmem] * 2,
        out_specs=vmem,
        scratch_shapes=[
            pltpu.VMEM((pairs, 128), jnp.bfloat16),
            pltpu.VMEM((pairs, width), jnp.float32),
        ],
        compiler_params=pltpu.CompilerParams(vmem_limit_bytes=16 * 1024 * 1024),
        name="divide",
    )(mine, received)


def shards(*arrays):
    sizes = tuple(lax.axis_size(name) for name in GROUP)
    if sizes == (4, 2, 2) and arrays[0].shape[:2] == (128, 8):
        return direct_shards(*arrays)
    return general_shards(*arrays)


def solution(mesh):
    return jax.shard_map(
        shards,
        mesh=mesh,
        in_specs=(
            P(("crops", "seq"), ("col", "row"), None),
            P(("crops", "seq"), ("col", "row")),
            P(("crops", "col", "row")),
            P(),
            P(),
            P(),
            P(),
            P(),
            P(),
            P(),
            P(),
        ),
        out_specs=P(("crops", "row"), ("col", "seq"), None),
        check_vma=False,
    )
```

```python
import math

import jax
import jax.numpy as jnp
from jax import lax
from jax.experimental import pallas as pl
from jax.experimental.pallas import tpu as pltpu
from jax.sharding import PartitionSpec as P

GROUP = ("row", "col", "seq")
NT = (((1,), (1,)), ((), ()))
MASK_ROWS = 16
WIDE = 2


def from_root(x, axis, root):
    mine = lax.axis_index(axis) == root
    return lax.psum(jnp.where(mine, x, jnp.zeros_like(x)), axis)


def project_side(normed, occupied_indicator, weight, bias):
    seq_count, res_count, width = normed.shape
    report_text = jnp.dot(
        normed.reshape(seq_count * res_count, width), weight, preferred_element_type=jnp.float32
    )
    report_text = (report_text + bias).reshape(seq_count, res_count, -1) * occupied_indicator[
        :, :, None
    ]
    return report_text.astype(jnp.bfloat16)


def pair_rows(left, right, closing_linear_map):
    row_count = left.shape[1]
    col_count = right.shape[1]
    block_rows = math.gcd(row_count, max(1, 512 // col_count))
    weight_f32 = closing_linear_map.astype(jnp.float32)

    def project_block(first_row):
        left_block = lax.dynamic_slice_in_dim(left, first_row, block_rows, 1)
        outer_prod = jnp.einsum(
            "sic,sjd->ijcd", left_block, right, preferred_element_type=jnp.float32
        )
        flattened = outer_prod.reshape(block_rows * col_count, -1)
        result = jnp.dot(flattened, weight_f32, precision=lax.Precision.HIGHEST)
        return result.reshape(block_rows, col_count, -1)

    starts = jnp.arange(row_count // block_rows) * block_rows
    return lax.map(project_block, starts).reshape(row_count, col_count, -1)


def general_shards(
    homolog_embedding,
    homolog_cell_occupancy,
    peptide_occupancy,
    standardize_multiplier,
    standardize_addend,
    lhs_linear_map,
    lhs_linear_constant,
    rhs_linear_map,
    rhs_linear_constant,
    closing_linear_map,
    closing_linear_constant,
):
    occupied_indicator = (homolog_cell_occupancy * peptide_occupancy[None, :]).astype(jnp.float32)
    report_text = homolog_embedding.astype(jnp.float32)
    average = jnp.mean(report_text, axis=-1, keepdims=True)
    spread = jnp.mean(jnp.square(report_text - average), axis=-1, keepdims=True)
    normed = (
        (report_text - average) * lax.rsqrt(spread + 1e-05) * standardize_multiplier
        + standardize_addend
    ).astype(jnp.bfloat16)
    left = project_side(normed, occupied_indicator, lhs_linear_map, lhs_linear_constant)
    right = project_side(normed, occupied_indicator, rhs_linear_map, rhs_linear_constant)
    mask_bf = occupied_indicator.astype(jnp.bfloat16)
    left_col, right_col, mask_col = (
        lax.all_gather(left, "row", axis=1, tiled=True),
        lax.all_gather(right, "row", axis=1, tiled=True),
        lax.all_gather(mask_bf, "row", axis=1, tiled=True),
    )
    row_devices = lax.axis_size("row")
    col_devices = lax.axis_size("col")
    col_len = left_col.shape[1]
    row_len = col_len * col_devices // row_devices
    row_index = lax.axis_index("row")
    root_col = row_index * col_devices // row_devices
    offset = row_index * row_len % col_len
    whole_left, whole_mask = (
        from_root(left_col, "col", root_col),
        from_root(mask_col, "col", root_col),
    )
    left_row = lax.dynamic_slice_in_dim(whole_left, offset, row_len, 1)
    mask_row = lax.dynamic_slice_in_dim(whole_mask, offset, row_len, 1)
    partial_value = pair_rows(left_row, right_col, closing_linear_map)
    mask_rows_all, mask_cols_all = (
        lax.all_gather(mask_row, "seq", axis=0, tiled=True),
        lax.all_gather(mask_col, "seq", axis=0, tiled=True),
    )
    counts_full = jnp.dot(mask_rows_all.T, mask_cols_all, preferred_element_type=jnp.float32)
    summed = lax.psum_scatter(
        partial_value.astype(jnp.bfloat16), "seq", scatter_dimension=1, tiled=True
    ).astype(jnp.float32)
    seq_devices = lax.axis_size("seq")
    part_cols = col_len // seq_devices
    counts = lax.dynamic_slice_in_dim(counts_full, lax.axis_index("seq") * part_cols, part_cols, 1)
    return ((summed + closing_linear_constant) / jnp.maximum(counts, 1.0)[:, :, None]).astype(
        jnp.bfloat16
    )


def project_kernel(
    pept_hbm, x_hbm, occ_hbm, gain_hbm, shift_hbm, wl_hbm, bl_hbm, wr_hbm, br_hbm,
    left_ref, right_ref,
    pept_ref, x_ref, occ_ref, gain_ref, shift_ref, wl_ref, bl_ref, wr_ref, br_ref,
    y_ref, l_ref, x_sems, sems,
):
    residues, sequences = occ_ref.shape
    hidden = wl_ref.shape[0]
    chunks = x_sems.shape[0]
    size = x_ref.shape[0] // chunks
    x_copies = [
        pltpu.make_async_copy(
            x_hbm.at[pl.ds(n * size, size)], x_ref.at[pl.ds(n * size, size)], x_sems.at[n]
        )
        for n in range(chunks)
    ]
    pairs = (
        (wl_hbm, wl_ref), (wr_hbm, wr_ref), (gain_hbm, gain_ref), (shift_hbm, shift_ref),
        (bl_hbm, bl_ref), (br_hbm, br_ref), (occ_hbm, occ_ref), (pept_hbm, pept_ref),
    )
    copies = [pltpu.make_async_copy(a, b, sems.at[n]) for n, (a, b) in enumerate(pairs)]
    x_copies[0].start()
    for copy in copies:
        copy.start()
    for copy in x_copies[1:]:
        copy.start()
    for copy in copies:
        copy.wait()
    weight = jnp.concatenate([wl_ref[...], wr_ref[...]], axis=0)
    bias = jnp.concatenate([bl_ref[...], br_ref[...]], axis=1)
    for n, copy in enumerate(x_copies):
        copy.wait()
        x = x_ref[n * size : (n + 1) * size, :].astype(jnp.float32)
        average = jnp.mean(x, axis=-1, keepdims=True)
        centred = x - average
        spread = jnp.mean(jnp.square(centred), axis=-1, keepdims=True)
        normed = (centred * lax.rsqrt(spread + 1e-05) * gain_ref[...] + shift_ref[...]).astype(
            jnp.bfloat16
        )
        y = lax.dot_general(normed, weight, NT, preferred_element_type=jnp.float32) + bias
        y_ref[n * size : (n + 1) * size, : 2 * hidden] = y
    for i in range(residues):
        live = (occ_ref[i : i + 1, :] * pept_ref[i]).astype(jnp.float32)
        part = y_ref[pl.ds(i, sequences, stride=residues), :].T[: 2 * hidden] * live
        l_ref[pl.ds(i, hidden, stride=residues), :] = part[:hidden]
        right_ref[i * hidden : (i + 1) * hidden, :] = part[hidden:].astype(jnp.bfloat16)
        l_ref[hidden * residues + i : hidden * residues + i + 1, :] = live
    l_ref[hidden * residues + residues :, :] = jnp.zeros((MASK_ROWS - residues, sequences), jnp.float32)
    left_ref[...] = l_ref[...].astype(jnp.bfloat16)
    right_ref[hidden * residues :, :] = l_ref[hidden * residues :, :].astype(jnp.bfloat16)


def expand(tile, store, hidden, wide):
    rows, lanes = tile.shape
    per_vector = 128 // hidden
    lane = lax.broadcasted_iota(jnp.int32, (rows, 128), 1) // (hidden * wide)
    for g in range(lanes // 128):
        part = tile[:, g * 128 : (g + 1) * 128]
        for a in range(per_vector // wide):
            first = (g * (per_vector // wide) + a) * rows
            store(first, part * (lane == a).astype(jnp.bfloat16))


def join_kernel(right_ref, far_ref, out_ref):
    out_ref[0] = right_ref[...]
    out_ref[1] = far_ref[...]


def keep_kernel(w_ref, b_ref, w_out, b_out):
    hidden = 32
    b_out[...] = b_ref[...]
    width = b_ref.shape[1]
    zero = jnp.zeros((hidden, width), jnp.bfloat16)
    for c in range(hidden):
        block = w_ref[c * hidden : (c + 1) * hidden, :]
        for a in range(128 // hidden):
            for n in range(WIDE):
                w_out[c * 128 + a * hidden : c * 128 + (a + 1) * hidden, n * width : (n + 1) * width] = (
                    block if a % WIDE == n else zero
                )


def pair_kernel(
    own, l0, l1, held, passed, w_ref, b_ref, out_ref, ls_ref, rs_ref, big_ref
):
    body = l0.shape[0] - MASK_ROWS
    hidden = 32
    residues = body // hidden
    row, col, seq = (lax.axis_index(name) for name in GROUP)
    for k, piece in enumerate((l0, l1)):
        ls_ref[col ^ k] = piece[...]
    for k in range(2):
        rs_ref[row ^ (2 * k)] = held[k]
        rs_ref[row ^ (2 * k + 1)] = passed[k]
    half = 2 * (seq if own else 1 - seq)

    def rows(ref, at, first, last):
        return jnp.concatenate([ref[at + p, first:last, :] for p in range(2)], axis=0)

    outer = lax.dot_general(
        rows(ls_ref, 0, 0, body), rows(rs_ref, half, 0, body), NT, preferred_element_type=jnp.float32
    )
    live_i = rows(ls_ref, 0, body, body + MASK_ROWS)
    live_j = rows(rs_ref, half, body, body + MASK_ROWS)
    live_j = jnp.concatenate([live_j, jnp.zeros((128 - 2 * MASK_ROWS, live_j.shape[1]), live_j.dtype)], axis=0)
    counts = lax.dot_general(live_i, live_j, NT, preferred_element_type=jnp.float32)
    for c in range(hidden):
        tile = jnp.concatenate(
            [outer[p * body + c * residues : p * body + (c + 1) * residues] for p in range(2)], axis=0
        ).astype(jnp.bfloat16)

        def store(first, value, c=c):
            big_ref[first : first + 2 * residues, c * 128 : (c + 1) * 128] = value

        expand(tile, store, hidden, WIDE)
    pairs = 4 * residues * residues
    projected = jnp.dot(big_ref[...], w_ref[...], preferred_element_type=jnp.float32)
    width = b_ref.shape[1]
    size = 2 * residues
    for g in range(pairs // (size * WIDE)):
        for n in range(WIDE):
            part = projected[g * size : (g + 1) * size, n * width : (n + 1) * width]
            if own:
                part = part + b_ref[...]
            first = (g * WIDE + n) * size
            out_ref[first : first + size, :] = part.astype(out_ref.dtype)
    out_ref[pairs:, :] = counts.astype(out_ref.dtype)


def finish_kernel(mine_ref, other_ref, out_ref, big_ref, p_ref):
    residues = out_ref.shape[0] // 2
    pairs = 4 * residues * residues
    hidden = 32
    counts = mine_ref[pairs:, :] + other_ref[pairs:, :].astype(jnp.float32)
    spread_shape = (128, 2 * residues * hidden)
    at_row = lax.broadcasted_iota(jnp.int32, spread_shape, 0)
    at_lane = lax.broadcasted_iota(jnp.int32, spread_shape, 1)
    hit = ((at_row // MASK_ROWS) * residues + at_row % MASK_ROWS == at_lane // hidden) & (
        at_row % MASK_ROWS < residues
    )
    counts = jnp.dot(
        counts.astype(jnp.bfloat16), hit.astype(jnp.bfloat16), preferred_element_type=jnp.float32
    )
    tile = jnp.concatenate(
        [counts[p * MASK_ROWS : p * MASK_ROWS + residues] for p in range(2)], axis=0
    ).astype(jnp.bfloat16)

    def store(first, value):
        big_ref[first : first + 2 * residues, :] = value

    expand(tile, store, hidden, 1)
    share = jnp.full((128, 128), 1.0 / hidden, jnp.bfloat16)
    divisor = jnp.dot(big_ref[...], share, preferred_element_type=jnp.float32)
    total = mine_ref[:pairs, :] + other_ref[:pairs, :].astype(jnp.float32)
    p_ref[...] = total / jnp.maximum(divisor, 1.0)
    for i in range(2 * residues):
        out_ref[i] = p_ref[pl.ds(i, 2 * residues, stride=2 * residues), :].astype(jnp.bfloat16)


def route(target):
    return [
        (4 * r + 2 * c + q, 4 * to[0] + 2 * to[1] + to[2])
        for r in range(4)
        for c in range(2)
        for q in range(2)
        for to in (target(r, c, q),)
    ]


def direct_shards(
    homolog_embedding,
    homolog_cell_occupancy,
    peptide_occupancy,
    standardize_multiplier,
    standardize_addend,
    lhs_linear_map,
    lhs_linear_constant,
    rhs_linear_map,
    rhs_linear_constant,
    closing_linear_map,
    closing_linear_constant,
):
    sequences, residues, signal = homolog_embedding.shape
    hidden = lhs_linear_map.shape[1]
    width = closing_linear_map.shape[1]
    rows = residues * hidden + MASK_ROWS
    pairs = 4 * residues * residues
    payload = jax.ShapeDtypeStruct((rows, sequences), jnp.bfloat16)
    vmem = pl.BlockSpec(memory_space=pltpu.VMEM)
    in_hbm = pl.BlockSpec(memory_space=pltpu.HBM)
    left, right = pl.pallas_call(
        project_kernel,
        out_shape=(payload, payload),
        in_specs=[in_hbm] * 9,
        out_specs=(vmem, vmem),
        scratch_shapes=[
            pltpu.SMEM((residues,), jnp.int32),
            pltpu.VMEM((sequences * residues, signal), jnp.bfloat16),
            pltpu.VMEM((residues, sequences), jnp.int32),
            pltpu.VMEM((1, signal), jnp.float32),
            pltpu.VMEM((1, signal), jnp.float32),
            pltpu.VMEM((hidden, signal), jnp.bfloat16),
            pltpu.VMEM((1, hidden), jnp.float32),
            pltpu.VMEM((hidden, signal), jnp.bfloat16),
            pltpu.VMEM((1, hidden), jnp.float32),
            pltpu.VMEM((sequences * residues, 128), jnp.float32),
            pltpu.VMEM((rows, sequences), jnp.float32),
            pltpu.SemaphoreType.DMA((4,)),
            pltpu.SemaphoreType.DMA((8,)),
        ],
        compiler_params=pltpu.CompilerParams(vmem_limit_bytes=60 * 1024 * 1024),
        name="normalize_and_project",
    )(
        peptide_occupancy,
        homolog_embedding.reshape(sequences * residues, signal),
        homolog_cell_occupancy.T,
        standardize_multiplier.reshape(1, signal),
        standardize_addend.reshape(1, signal),
        lhs_linear_map.T,
        lhs_linear_constant.reshape(1, hidden),
        rhs_linear_map.T,
        rhs_linear_constant.reshape(1, hidden),
    )
    far = lax.ppermute(right, GROUP, route(lambda r, c, q: (r ^ 2, c, q)))
    first = lax.ppermute(left, GROUP, route(lambda r, c, q: (2 * c + r // 2, r % 2, q)))
    held = pl.pallas_call(
        join_kernel,
        out_shape=jax.ShapeDtypeStruct((2,) + payload.shape, jnp.bfloat16),
        in_specs=[vmem] * 2,
        out_specs=vmem,
        name="join",
    )(right, far)
    passed = lax.ppermute(held, GROUP, route(lambda r, c, q: (r ^ 1, c, q)))
    second = lax.ppermute(first, GROUP, route(lambda r, c, q: (r, 1 - c, q)))
    weight, bias = pl.pallas_call(
        keep_kernel,
        out_shape=(
            jax.ShapeDtypeStruct((hidden * 128, WIDE * width), jnp.bfloat16),
            jax.ShapeDtypeStruct((1, width), jnp.float32),
        ),
        in_specs=[vmem] * 2,
        out_specs=(vmem,) * 2,
        compiler_params=pltpu.CompilerParams(vmem_limit_bytes=16 * 1024 * 1024),
        cost_estimate=pl.CostEstimate(flops=0, bytes_accessed=1 << 22, transcendentals=0),
        name="keep",
    )(closing_linear_map, closing_linear_constant.reshape(1, width))

    def pair_sums(own, kind):
        return pl.pallas_call(
            lambda *refs: pair_kernel(own, *refs),
            out_shape=jax.ShapeDtypeStruct((pairs + 2 * MASK_ROWS, width), kind),
            in_specs=[vmem] * 6,
            out_specs=vmem,
            scratch_shapes=[
                pltpu.VMEM((2, rows, sequences), jnp.bfloat16),
                pltpu.VMEM((4, rows, sequences), jnp.bfloat16),
                pltpu.VMEM((pairs // WIDE, hidden * 128), jnp.bfloat16),
            ],
            compiler_params=pltpu.CompilerParams(vmem_limit_bytes=24 * 1024 * 1024),
            cost_estimate=pl.CostEstimate(
                flops=2 * pairs * hidden * 128 * width, bytes_accessed=1 << 20, transcendentals=0
            ),
            name="own_pair_sums" if own else "other_pair_sums",
        )(first, second, held, passed, weight, bias)

    theirs = pair_sums(False, jnp.bfloat16)
    received = lax.ppermute(theirs, GROUP, route(lambda r, c, q: (r, c, 1 - q)))
    mine = pair_sums(True, jnp.float32)
    return pl.pallas_call(
        finish_kernel,
        out_shape=jax.ShapeDtypeStruct((2 * residues, 2 * residues, width), jnp.bfloat16),
        in_specs=[vmem] * 2,
        out_specs=vmem,
        scratch_shapes=[
            pltpu.VMEM((pairs, 128), jnp.bfloat16),
            pltpu.VMEM((pairs, width), jnp.float32),
        ],
        compiler_params=pltpu.CompilerParams(vmem_limit_bytes=16 * 1024 * 1024),
        name="divide",
    )(mine, received)


def shards(*arrays):
    sizes = tuple(lax.axis_size(name) for name in GROUP)
    if sizes == (4, 2, 2) and arrays[0].shape[:2] == (128, 8):
        return direct_shards(*arrays)
    return general_shards(*arrays)


def solution(mesh):
    return jax.shard_map(
        shards,
        mesh=mesh,
        in_specs=(
            P(("crops", "seq"), ("col", "row"), None),
            P(("crops", "seq"), ("col", "row")),
            P(("crops", "col", "row")),
            P(),
            P(),
            P(),
            P(),
            P(),
            P(),
            P(),
            P(),
        ),
        out_specs=P(("crops", "row"), ("col", "seq"), None),
        check_vma=False,
    )
```

```python
import math

import jax
import jax.numpy as jnp
from jax import lax
from jax.experimental import pallas as pl
from jax.experimental.pallas import tpu as pltpu
from jax.sharding import PartitionSpec as P

GROUP = ("row", "col", "seq")
NT = (((1,), (1,)), ((), ()))
MASK_ROWS = 16
WIDE = 2


def from_root(x, axis, root):
    mine = lax.axis_index(axis) == root
    return lax.psum(jnp.where(mine, x, jnp.zeros_like(x)), axis)


def project_side(normed, occupied_indicator, weight, bias):
    seq_count, res_count, width = normed.shape
    report_text = jnp.dot(
        normed.reshape(seq_count * res_count, width), weight, preferred_element_type=jnp.float32
    )
    report_text = (report_text + bias).reshape(seq_count, res_count, -1) * occupied_indicator[
        :, :, None
    ]
    return report_text.astype(jnp.bfloat16)


def pair_rows(left, right, closing_linear_map):
    row_count = left.shape[1]
    col_count = right.shape[1]
    block_rows = math.gcd(row_count, max(1, 512 // col_count))
    weight_f32 = closing_linear_map.astype(jnp.float32)

    def project_block(first_row):
        left_block = lax.dynamic_slice_in_dim(left, first_row, block_rows, 1)
        outer_prod = jnp.einsum(
            "sic,sjd->ijcd", left_block, right, preferred_element_type=jnp.float32
        )
        flattened = outer_prod.reshape(block_rows * col_count, -1)
        result = jnp.dot(flattened, weight_f32, precision=lax.Precision.HIGHEST)
        return result.reshape(block_rows, col_count, -1)

    starts = jnp.arange(row_count // block_rows) * block_rows
    return lax.map(project_block, starts).reshape(row_count, col_count, -1)


def general_shards(
    homolog_embedding,
    homolog_cell_occupancy,
    peptide_occupancy,
    standardize_multiplier,
    standardize_addend,
    lhs_linear_map,
    lhs_linear_constant,
    rhs_linear_map,
    rhs_linear_constant,
    closing_linear_map,
    closing_linear_constant,
):
    occupied_indicator = (homolog_cell_occupancy * peptide_occupancy[None, :]).astype(jnp.float32)
    report_text = homolog_embedding.astype(jnp.float32)
    average = jnp.mean(report_text, axis=-1, keepdims=True)
    spread = jnp.mean(jnp.square(report_text - average), axis=-1, keepdims=True)
    normed = (
        (report_text - average) * lax.rsqrt(spread + 1e-05) * standardize_multiplier
        + standardize_addend
    ).astype(jnp.bfloat16)
    left = project_side(normed, occupied_indicator, lhs_linear_map, lhs_linear_constant)
    right = project_side(normed, occupied_indicator, rhs_linear_map, rhs_linear_constant)
    mask_bf = occupied_indicator.astype(jnp.bfloat16)
    left_col, right_col, mask_col = (
        lax.all_gather(left, "row", axis=1, tiled=True),
        lax.all_gather(right, "row", axis=1, tiled=True),
        lax.all_gather(mask_bf, "row", axis=1, tiled=True),
    )
    row_devices = lax.axis_size("row")
    col_devices = lax.axis_size("col")
    col_len = left_col.shape[1]
    row_len = col_len * col_devices // row_devices
    row_index = lax.axis_index("row")
    root_col = row_index * col_devices // row_devices
    offset = row_index * row_len % col_len
    whole_left, whole_mask = (
        from_root(left_col, "col", root_col),
        from_root(mask_col, "col", root_col),
    )
    left_row = lax.dynamic_slice_in_dim(whole_left, offset, row_len, 1)
    mask_row = lax.dynamic_slice_in_dim(whole_mask, offset, row_len, 1)
    partial_value = pair_rows(left_row, right_col, closing_linear_map)
    mask_rows_all, mask_cols_all = (
        lax.all_gather(mask_row, "seq", axis=0, tiled=True),
        lax.all_gather(mask_col, "seq", axis=0, tiled=True),
    )
    counts_full = jnp.dot(mask_rows_all.T, mask_cols_all, preferred_element_type=jnp.float32)
    summed = lax.psum_scatter(
        partial_value.astype(jnp.bfloat16), "seq", scatter_dimension=1, tiled=True
    ).astype(jnp.float32)
    seq_devices = lax.axis_size("seq")
    part_cols = col_len // seq_devices
    counts = lax.dynamic_slice_in_dim(counts_full, lax.axis_index("seq") * part_cols, part_cols, 1)
    return ((summed + closing_linear_constant) / jnp.maximum(counts, 1.0)[:, :, None]).astype(
        jnp.bfloat16
    )


def project_kernel(
    pept_hbm, x_hbm, occ_hbm, gain_hbm, shift_hbm, wl_hbm, bl_hbm, wr_hbm, br_hbm,
    left_ref, right_ref,
    pept_ref, x_ref, occ_ref, gain_ref, shift_ref, wl_ref, bl_ref, wr_ref, br_ref,
    y_ref, l_ref, x_sems, sems,
):
    residues, sequences = occ_ref.shape
    hidden = wl_ref.shape[0]
    chunks = x_sems.shape[0]
    size = x_ref.shape[0] // chunks
    x_copies = [
        pltpu.make_async_copy(
            x_hbm.at[pl.ds(n * size, size)], x_ref.at[pl.ds(n * size, size)], x_sems.at[n]
        )
        for n in range(chunks)
    ]
    pairs = (
        (wl_hbm, wl_ref), (wr_hbm, wr_ref), (gain_hbm, gain_ref), (shift_hbm, shift_ref),
        (bl_hbm, bl_ref), (br_hbm, br_ref), (occ_hbm, occ_ref), (pept_hbm, pept_ref),
    )
    copies = [pltpu.make_async_copy(a, b, sems.at[n]) for n, (a, b) in enumerate(pairs)]
    x_copies[0].start()
    for copy in copies:
        copy.start()
    for copy in x_copies[1:]:
        copy.start()
    for copy in copies:
        copy.wait()
    weight = jnp.concatenate([wl_ref[...], wr_ref[...]], axis=0)
    bias = jnp.concatenate([bl_ref[...], br_ref[...]], axis=1)
    for n, copy in enumerate(x_copies):
        copy.wait()
        x = x_ref[n * size : (n + 1) * size, :].astype(jnp.float32)
        average = jnp.mean(x, axis=-1, keepdims=True)
        centred = x - average
        spread = jnp.mean(jnp.square(centred), axis=-1, keepdims=True)
        normed = (centred * lax.rsqrt(spread + 1e-05) * gain_ref[...] + shift_ref[...]).astype(
            jnp.bfloat16
        )
        y = lax.dot_general(normed, weight, NT, preferred_element_type=jnp.float32) + bias
        y_ref[n * size : (n + 1) * size, : 2 * hidden] = y
    for i in range(residues):
        live = (occ_ref[i : i + 1, :] * pept_ref[i]).astype(jnp.float32)
        part = y_ref[pl.ds(i, sequences, stride=residues), :].T[: 2 * hidden] * live
        l_ref[pl.ds(i, hidden, stride=residues), :] = part[:hidden]
        right_ref[i * hidden : (i + 1) * hidden, :] = part[hidden:].astype(jnp.bfloat16)
        l_ref[hidden * residues + i : hidden * residues + i + 1, :] = live
    l_ref[hidden * residues + residues :, :] = jnp.zeros((MASK_ROWS - residues, sequences), jnp.float32)
    left_ref[...] = l_ref[...].astype(jnp.bfloat16)
    right_ref[hidden * residues :, :] = l_ref[hidden * residues :, :].astype(jnp.bfloat16)


def expand(tile, store, hidden, wide):
    rows, lanes = tile.shape
    per_vector = 128 // hidden
    lane = lax.broadcasted_iota(jnp.int32, (rows, 128), 1) // (hidden * wide)
    for g in range(lanes // 128):
        part = tile[:, g * 128 : (g + 1) * 128]
        for a in range(per_vector // wide):
            first = (g * (per_vector // wide) + a) * rows
            store(first, part * (lane == a).astype(jnp.bfloat16))


def hold_kernel(right_ref, out_ref):
    out_ref[...] = right_ref[...]


def join_kernel(right_ref, far_ref, out_ref):
    out_ref[0] = right_ref[...]
    out_ref[1] = far_ref[...]


def keep_kernel(w_ref, b_ref, w_out, b_out):
    hidden = 32
    b_out[...] = b_ref[...]
    width = b_ref.shape[1]
    zero = jnp.zeros((hidden, width), jnp.bfloat16)
    for c in range(hidden):
        block = w_ref[c * hidden : (c + 1) * hidden, :]
        for a in range(128 // hidden):
            for n in range(WIDE):
                w_out[c * 128 + a * hidden : c * 128 + (a + 1) * hidden, n * width : (n + 1) * width] = (
                    block if a % WIDE == n else zero
                )


def pair_kernel(
    own, l0, l1, held, passed, w_ref, b_ref, out_ref, ls_ref, rs_ref, big_ref
):
    body = l0.shape[0] - MASK_ROWS
    hidden = 32
    residues = body // hidden
    row, col, seq = (lax.axis_index(name) for name in GROUP)
    for k, piece in enumerate((l0, l1)):
        ls_ref[col ^ k] = piece[...]
    for k in range(2):
        rs_ref[row ^ (2 * k)] = held[k]
        rs_ref[row ^ (2 * k + 1)] = passed[k]
    half = 2 * (seq if own else 1 - seq)

    def rows(ref, at, first, last):
        return jnp.concatenate([ref[at + p, first:last, :] for p in range(2)], axis=0)

    outer = lax.dot_general(
        rows(ls_ref, 0, 0, body), rows(rs_ref, half, 0, body), NT, preferred_element_type=jnp.float32
    )
    live_i = rows(ls_ref, 0, body, body + MASK_ROWS)
    live_j = rows(rs_ref, half, body, body + MASK_ROWS)
    live_j = jnp.concatenate([live_j, jnp.zeros((128 - 2 * MASK_ROWS, live_j.shape[1]), live_j.dtype)], axis=0)
    counts = lax.dot_general(live_i, live_j, NT, preferred_element_type=jnp.float32)
    for c in range(hidden):
        tile = jnp.concatenate(
            [outer[p * body + c * residues : p * body + (c + 1) * residues] for p in range(2)], axis=0
        ).astype(jnp.bfloat16)

        def store(first, value, c=c):
            big_ref[first : first + 2 * residues, c * 128 : (c + 1) * 128] = value

        expand(tile, store, hidden, WIDE)
    pairs = 4 * residues * residues
    projected = jnp.dot(big_ref[...], w_ref[...], preferred_element_type=jnp.float32)
    width = b_ref.shape[1]
    size = 2 * residues
    for g in range(pairs // (size * WIDE)):
        for n in range(WIDE):
            part = projected[g * size : (g + 1) * size, n * width : (n + 1) * width]
            if own:
                part = part + b_ref[...]
            first = (g * WIDE + n) * size
            out_ref[first : first + size, :] = part.astype(out_ref.dtype)
    out_ref[pairs:, :] = counts.astype(out_ref.dtype)


def finish_kernel(mine_ref, other_ref, out_ref, big_ref, p_ref):
    residues = out_ref.shape[0] // 2
    pairs = 4 * residues * residues
    hidden = 32
    counts = mine_ref[pairs:, :] + other_ref[pairs:, :].astype(jnp.float32)
    spread_shape = (128, 2 * residues * hidden)
    at_row = lax.broadcasted_iota(jnp.int32, spread_shape, 0)
    at_lane = lax.broadcasted_iota(jnp.int32, spread_shape, 1)
    hit = ((at_row // MASK_ROWS) * residues + at_row % MASK_ROWS == at_lane // hidden) & (
        at_row % MASK_ROWS < residues
    )
    counts = jnp.dot(
        counts.astype(jnp.bfloat16), hit.astype(jnp.bfloat16), preferred_element_type=jnp.float32
    )
    tile = jnp.concatenate(
        [counts[p * MASK_ROWS : p * MASK_ROWS + residues] for p in range(2)], axis=0
    ).astype(jnp.bfloat16)

    def store(first, value):
        big_ref[first : first + 2 * residues, :] = value

    expand(tile, store, hidden, 1)
    share = jnp.full((128, 128), 1.0 / hidden, jnp.bfloat16)
    divisor = jnp.dot(big_ref[...], share, preferred_element_type=jnp.float32)
    total = mine_ref[:pairs, :] + other_ref[:pairs, :].astype(jnp.float32)
    p_ref[...] = total / jnp.maximum(divisor, 1.0)
    for i in range(2 * residues):
        out_ref[i] = p_ref[pl.ds(i, 2 * residues, stride=2 * residues), :].astype(jnp.bfloat16)


def route(target):
    return [
        (4 * r + 2 * c + q, 4 * to[0] + 2 * to[1] + to[2])
        for r in range(4)
        for c in range(2)
        for q in range(2)
        for to in (target(r, c, q),)
    ]


def direct_shards(
    homolog_embedding,
    homolog_cell_occupancy,
    peptide_occupancy,
    standardize_multiplier,
    standardize_addend,
    lhs_linear_map,
    lhs_linear_constant,
    rhs_linear_map,
    rhs_linear_constant,
    closing_linear_map,
    closing_linear_constant,
):
    sequences, residues, signal = homolog_embedding.shape
    hidden = lhs_linear_map.shape[1]
    width = closing_linear_map.shape[1]
    rows = residues * hidden + MASK_ROWS
    pairs = 4 * residues * residues
    payload = jax.ShapeDtypeStruct((rows, sequences), jnp.bfloat16)
    vmem = pl.BlockSpec(memory_space=pltpu.VMEM)
    in_hbm = pl.BlockSpec(memory_space=pltpu.HBM)
    left, right = pl.pallas_call(
        project_kernel,
        out_shape=(payload, payload),
        in_specs=[in_hbm] * 9,
        out_specs=(vmem, vmem),
        scratch_shapes=[
            pltpu.SMEM((residues,), jnp.int32),
            pltpu.VMEM((sequences * residues, signal), jnp.bfloat16),
            pltpu.VMEM((residues, sequences), jnp.int32),
            pltpu.VMEM((1, signal), jnp.float32),
            pltpu.VMEM((1, signal), jnp.float32),
            pltpu.VMEM((hidden, signal), jnp.bfloat16),
            pltpu.VMEM((1, hidden), jnp.float32),
            pltpu.VMEM((hidden, signal), jnp.bfloat16),
            pltpu.VMEM((1, hidden), jnp.float32),
            pltpu.VMEM((sequences * residues, 128), jnp.float32),
            pltpu.VMEM((rows, sequences), jnp.float32),
            pltpu.SemaphoreType.DMA((4,)),
            pltpu.SemaphoreType.DMA((8,)),
        ],
        compiler_params=pltpu.CompilerParams(vmem_limit_bytes=60 * 1024 * 1024),
        name="normalize_and_project",
    )(
        peptide_occupancy,
        homolog_embedding.reshape(sequences * residues, signal),
        homolog_cell_occupancy.T,
        standardize_multiplier.reshape(1, signal),
        standardize_addend.reshape(1, signal),
        lhs_linear_map.T,
        lhs_linear_constant.reshape(1, hidden),
        rhs_linear_map.T,
        rhs_linear_constant.reshape(1, hidden),
    )
    far = lax.ppermute(right, GROUP, route(lambda r, c, q: (r ^ 2, c, q)))
    first = lax.ppermute(left, GROUP, route(lambda r, c, q: (2 * c + r // 2, r % 2, q)))
    small = pltpu.CompilerParams(vmem_limit_bytes=16 * 1024 * 1024)
    mine = pl.pallas_call(
        hold_kernel,
        out_shape=payload,
        in_specs=[vmem],
        out_specs=vmem,
        compiler_params=small,
        cost_estimate=pl.CostEstimate(flops=0, bytes_accessed=1 << 22, transcendentals=0),
        name="hold",
    )(right)
    held = pl.pallas_call(
        join_kernel,
        out_shape=jax.ShapeDtypeStruct((2,) + payload.shape, jnp.bfloat16),
        in_specs=[vmem] * 2,
        out_specs=vmem,
        compiler_params=small,
        name="join",
    )(mine, far)
    passed = lax.ppermute(held, GROUP, route(lambda r, c, q: (r ^ 1, c, q)))
    second = lax.ppermute(first, GROUP, route(lambda r, c, q: (r, 1 - c, q)))
    weight, bias = pl.pallas_call(
        keep_kernel,
        out_shape=(
            jax.ShapeDtypeStruct((hidden * 128, WIDE * width), jnp.bfloat16),
            jax.ShapeDtypeStruct((1, width), jnp.float32),
        ),
        in_specs=[vmem] * 2,
        out_specs=(vmem,) * 2,
        compiler_params=pltpu.CompilerParams(vmem_limit_bytes=16 * 1024 * 1024),
        cost_estimate=pl.CostEstimate(flops=0, bytes_accessed=1 << 22, transcendentals=0),
        name="keep",
    )(closing_linear_map, closing_linear_constant.reshape(1, width))

    def pair_sums(own, kind):
        return pl.pallas_call(
            lambda *refs: pair_kernel(own, *refs),
            out_shape=jax.ShapeDtypeStruct((pairs + 2 * MASK_ROWS, width), kind),
            in_specs=[vmem] * 6,
            out_specs=vmem,
            scratch_shapes=[
                pltpu.VMEM((2, rows, sequences), jnp.bfloat16),
                pltpu.VMEM((4, rows, sequences), jnp.bfloat16),
                pltpu.VMEM((pairs // WIDE, hidden * 128), jnp.bfloat16),
            ],
            compiler_params=pltpu.CompilerParams(vmem_limit_bytes=24 * 1024 * 1024),
            cost_estimate=pl.CostEstimate(
                flops=2 * pairs * hidden * 128 * width, bytes_accessed=1 << 20, transcendentals=0
            ),
            name="own_pair_sums" if own else "other_pair_sums",
        )(first, second, held, passed, weight, bias)

    theirs = pair_sums(False, jnp.bfloat16)
    received = lax.ppermute(theirs, GROUP, route(lambda r, c, q: (r, c, 1 - q)))
    mine = pair_sums(True, jnp.float32)
    return pl.pallas_call(
        finish_kernel,
        out_shape=jax.ShapeDtypeStruct((2 * residues, 2 * residues, width), jnp.bfloat16),
        in_specs=[vmem] * 2,
        out_specs=vmem,
        scratch_shapes=[
            pltpu.VMEM((pairs, 128), jnp.bfloat16),
            pltpu.VMEM((pairs, width), jnp.float32),
        ],
        compiler_params=pltpu.CompilerParams(vmem_limit_bytes=16 * 1024 * 1024),
        name="divide",
    )(mine, received)


def shards(*arrays):
    sizes = tuple(lax.axis_size(name) for name in GROUP)
    if sizes == (4, 2, 2) and arrays[0].shape[:2] == (128, 8):
        return direct_shards(*arrays)
    return general_shards(*arrays)


def solution(mesh):
    return jax.shard_map(
        shards,
        mesh=mesh,
        in_specs=(
            P(("crops", "seq"), ("col", "row"), None),
            P(("crops", "seq"), ("col", "row")),
            P(("crops", "col", "row")),
            P(),
            P(),
            P(),
            P(),
            P(),
            P(),
            P(),
            P(),
        ),
        out_specs=P(("crops", "row"), ("col", "seq"), None),
        check_vma=False,
    )
```

```python
import math

import jax
import jax.numpy as jnp
from jax import lax
from jax.experimental import pallas as pl
from jax.experimental.pallas import tpu as pltpu
from jax.sharding import PartitionSpec as P

GROUP = ("row", "col", "seq")
NT = (((1,), (1,)), ((), ()))
MASK_ROWS = 16
WIDE = 2


def from_root(x, axis, root):
    mine = lax.axis_index(axis) == root
    return lax.psum(jnp.where(mine, x, jnp.zeros_like(x)), axis)


def project_side(normed, occupied_indicator, weight, bias):
    seq_count, res_count, width = normed.shape
    report_text = jnp.dot(
        normed.reshape(seq_count * res_count, width), weight, preferred_element_type=jnp.float32
    )
    report_text = (report_text + bias).reshape(seq_count, res_count, -1) * occupied_indicator[
        :, :, None
    ]
    return report_text.astype(jnp.bfloat16)


def pair_rows(left, right, closing_linear_map):
    row_count = left.shape[1]
    col_count = right.shape[1]
    block_rows = math.gcd(row_count, max(1, 512 // col_count))
    weight_f32 = closing_linear_map.astype(jnp.float32)

    def project_block(first_row):
        left_block = lax.dynamic_slice_in_dim(left, first_row, block_rows, 1)
        outer_prod = jnp.einsum(
            "sic,sjd->ijcd", left_block, right, preferred_element_type=jnp.float32
        )
        flattened = outer_prod.reshape(block_rows * col_count, -1)
        result = jnp.dot(flattened, weight_f32, precision=lax.Precision.HIGHEST)
        return result.reshape(block_rows, col_count, -1)

    starts = jnp.arange(row_count // block_rows) * block_rows
    return lax.map(project_block, starts).reshape(row_count, col_count, -1)


def general_shards(
    homolog_embedding,
    homolog_cell_occupancy,
    peptide_occupancy,
    standardize_multiplier,
    standardize_addend,
    lhs_linear_map,
    lhs_linear_constant,
    rhs_linear_map,
    rhs_linear_constant,
    closing_linear_map,
    closing_linear_constant,
):
    occupied_indicator = (homolog_cell_occupancy * peptide_occupancy[None, :]).astype(jnp.float32)
    report_text = homolog_embedding.astype(jnp.float32)
    average = jnp.mean(report_text, axis=-1, keepdims=True)
    spread = jnp.mean(jnp.square(report_text - average), axis=-1, keepdims=True)
    normed = (
        (report_text - average) * lax.rsqrt(spread + 1e-05) * standardize_multiplier
        + standardize_addend
    ).astype(jnp.bfloat16)
    left = project_side(normed, occupied_indicator, lhs_linear_map, lhs_linear_constant)
    right = project_side(normed, occupied_indicator, rhs_linear_map, rhs_linear_constant)
    mask_bf = occupied_indicator.astype(jnp.bfloat16)
    left_col, right_col, mask_col = (
        lax.all_gather(left, "row", axis=1, tiled=True),
        lax.all_gather(right, "row", axis=1, tiled=True),
        lax.all_gather(mask_bf, "row", axis=1, tiled=True),
    )
    row_devices = lax.axis_size("row")
    col_devices = lax.axis_size("col")
    col_len = left_col.shape[1]
    row_len = col_len * col_devices // row_devices
    row_index = lax.axis_index("row")
    root_col = row_index * col_devices // row_devices
    offset = row_index * row_len % col_len
    whole_left, whole_mask = (
        from_root(left_col, "col", root_col),
        from_root(mask_col, "col", root_col),
    )
    left_row = lax.dynamic_slice_in_dim(whole_left, offset, row_len, 1)
    mask_row = lax.dynamic_slice_in_dim(whole_mask, offset, row_len, 1)
    partial_value = pair_rows(left_row, right_col, closing_linear_map)
    mask_rows_all, mask_cols_all = (
        lax.all_gather(mask_row, "seq", axis=0, tiled=True),
        lax.all_gather(mask_col, "seq", axis=0, tiled=True),
    )
    counts_full = jnp.dot(mask_rows_all.T, mask_cols_all, preferred_element_type=jnp.float32)
    summed = lax.psum_scatter(
        partial_value.astype(jnp.bfloat16), "seq", scatter_dimension=1, tiled=True
    ).astype(jnp.float32)
    seq_devices = lax.axis_size("seq")
    part_cols = col_len // seq_devices
    counts = lax.dynamic_slice_in_dim(counts_full, lax.axis_index("seq") * part_cols, part_cols, 1)
    return ((summed + closing_linear_constant) / jnp.maximum(counts, 1.0)[:, :, None]).astype(
        jnp.bfloat16
    )


def project_kernel(
    pept_hbm, x_hbm, occ_hbm, gain_hbm, shift_hbm, wl_hbm, bl_hbm, wr_hbm, br_hbm,
    left_ref, right_ref,
    pept_ref, x_ref, occ_ref, gain_ref, shift_ref, wl_ref, bl_ref, wr_ref, br_ref,
    y_ref, l_ref, x_sems, sems,
):
    residues, sequences = occ_ref.shape
    hidden = wl_ref.shape[0]
    chunks = x_sems.shape[0]
    size = x_ref.shape[0] // chunks
    x_copies = [
        pltpu.make_async_copy(
            x_hbm.at[pl.ds(n * size, size)], x_ref.at[pl.ds(n * size, size)], x_sems.at[n]
        )
        for n in range(chunks)
    ]
    pairs = (
        (wl_hbm, wl_ref), (wr_hbm, wr_ref), (gain_hbm, gain_ref), (shift_hbm, shift_ref),
        (bl_hbm, bl_ref), (br_hbm, br_ref), (occ_hbm, occ_ref), (pept_hbm, pept_ref),
    )
    copies = [pltpu.make_async_copy(a, b, sems.at[n]) for n, (a, b) in enumerate(pairs)]
    x_copies[0].start()
    for copy in copies:
        copy.start()
    for copy in x_copies[1:]:
        copy.start()
    for copy in copies:
        copy.wait()
    weight = jnp.concatenate([wl_ref[...], wr_ref[...]], axis=0)
    bias = jnp.concatenate([bl_ref[...], br_ref[...]], axis=1)
    for n, copy in enumerate(x_copies):
        copy.wait()
        x = x_ref[n * size : (n + 1) * size, :].astype(jnp.float32)
        average = jnp.mean(x, axis=-1, keepdims=True)
        centred = x - average
        spread = jnp.mean(jnp.square(centred), axis=-1, keepdims=True)
        normed = (centred * lax.rsqrt(spread + 1e-05) * gain_ref[...] + shift_ref[...]).astype(
            jnp.bfloat16
        )
        y = lax.dot_general(normed, weight, NT, preferred_element_type=jnp.float32) + bias
        y_ref[n * size : (n + 1) * size, : 2 * hidden] = y
    for i in range(residues):
        live = (occ_ref[i : i + 1, :] * pept_ref[i]).astype(jnp.float32)
        part = y_ref[pl.ds(i, sequences, stride=residues), :].T[: 2 * hidden] * live
        l_ref[pl.ds(i, hidden, stride=residues), :] = part[:hidden]
        right_ref[i * hidden : (i + 1) * hidden, :] = part[hidden:].astype(jnp.bfloat16)
        l_ref[hidden * residues + i : hidden * residues + i + 1, :] = live
    l_ref[hidden * residues + residues :, :] = jnp.zeros((MASK_ROWS - residues, sequences), jnp.float32)
    left_ref[...] = l_ref[...].astype(jnp.bfloat16)
    right_ref[hidden * residues :, :] = l_ref[hidden * residues :, :].astype(jnp.bfloat16)


def expand(tile, store, hidden, wide):
    rows, lanes = tile.shape
    per_vector = 128 // hidden
    lane = lax.broadcasted_iota(jnp.int32, (rows, 128), 1) // (hidden * wide)
    for g in range(lanes // 128):
        part = tile[:, g * 128 : (g + 1) * 128]
        for a in range(per_vector // wide):
            first = (g * (per_vector // wide) + a) * rows
            store(first, part * (lane == a).astype(jnp.bfloat16))


def hold_kernel(right_ref, out_ref):
    out_ref[...] = right_ref[...]


def join_kernel(right_ref, far_ref, out_ref):
    out_ref[0] = right_ref[...]
    out_ref[1] = far_ref[...]


def keep_kernel(w_ref, b_ref, w_out, b_out):
    hidden = 32
    b_out[...] = b_ref[...]
    width = b_ref.shape[1]
    zero = jnp.zeros((hidden, width), jnp.bfloat16)
    for c in range(hidden):
        block = w_ref[c * hidden : (c + 1) * hidden, :]
        for a in range(128 // hidden):
            for n in range(WIDE):
                w_out[c * 128 + a * hidden : c * 128 + (a + 1) * hidden, n * width : (n + 1) * width] = (
                    block if a % WIDE == n else zero
                )


def pair_kernel(
    own, l0, l1, held, passed, w_ref, b_ref, out_ref, ls_ref, rs_ref, big_ref
):
    body = l0.shape[0] - MASK_ROWS
    hidden = 32
    residues = body // hidden
    row, col, seq = (lax.axis_index(name) for name in GROUP)
    for k, piece in enumerate((l0, l1)):
        ls_ref[col ^ k] = piece[...]
    for k in range(2):
        rs_ref[row ^ (2 * k)] = held[k]
        rs_ref[row ^ (2 * k + 1)] = passed[k]
    half = 2 * (seq if own else 1 - seq)

    def rows(ref, at, first, last):
        return jnp.concatenate([ref[at + p, first:last, :] for p in range(2)], axis=0)

    outer = lax.dot_general(
        rows(ls_ref, 0, 0, body), rows(rs_ref, half, 0, body), NT, preferred_element_type=jnp.float32
    )
    live_i = rows(ls_ref, 0, body, body + MASK_ROWS)
    live_j = rows(rs_ref, half, body, body + MASK_ROWS)
    live_j = jnp.concatenate([live_j, jnp.zeros((128 - 2 * MASK_ROWS, live_j.shape[1]), live_j.dtype)], axis=0)
    counts = lax.dot_general(live_i, live_j, NT, preferred_element_type=jnp.float32)
    for c in range(hidden):
        tile = jnp.concatenate(
            [outer[p * body + c * residues : p * body + (c + 1) * residues] for p in range(2)], axis=0
        ).astype(jnp.bfloat16)

        def store(first, value, c=c):
            big_ref[first : first + 2 * residues, c * 128 : (c + 1) * 128] = value

        expand(tile, store, hidden, WIDE)
    pairs = 4 * residues * residues
    projected = jnp.dot(big_ref[...], w_ref[...], preferred_element_type=jnp.float32)
    width = b_ref.shape[1]
    size = 2 * residues
    for g in range(pairs // (size * WIDE)):
        for n in range(WIDE):
            part = projected[g * size : (g + 1) * size, n * width : (n + 1) * width]
            if own:
                part = part + b_ref[...]
            first = (g * WIDE + n) * size
            out_ref[first : first + size, :] = part.astype(out_ref.dtype)
    out_ref[pairs:, :] = counts.astype(out_ref.dtype)


def finish_kernel(mine_ref, other_ref, out_ref, big_ref, p_ref):
    residues = out_ref.shape[0] // 2
    pairs = 4 * residues * residues
    hidden = 32
    counts = mine_ref[pairs:, :] + other_ref[pairs:, :].astype(jnp.float32)
    spread_shape = (128, 2 * residues * hidden)
    at_row = lax.broadcasted_iota(jnp.int32, spread_shape, 0)
    at_lane = lax.broadcasted_iota(jnp.int32, spread_shape, 1)
    hit = ((at_row // MASK_ROWS) * residues + at_row % MASK_ROWS == at_lane // hidden) & (
        at_row % MASK_ROWS < residues
    )
    counts = jnp.dot(
        counts.astype(jnp.bfloat16), hit.astype(jnp.bfloat16), preferred_element_type=jnp.float32
    )
    tile = jnp.concatenate(
        [counts[p * MASK_ROWS : p * MASK_ROWS + residues] for p in range(2)], axis=0
    ).astype(jnp.bfloat16)

    def store(first, value):
        big_ref[first : first + 2 * residues, :] = value

    expand(tile, store, hidden, 1)
    share = jnp.full((128, 128), 1.0 / hidden, jnp.bfloat16)
    divisor = jnp.dot(big_ref[...], share, preferred_element_type=jnp.float32)
    total = mine_ref[:pairs, :] + other_ref[:pairs, :].astype(jnp.float32)
    p_ref[...] = total / jnp.maximum(divisor, 1.0)
    for i in range(2 * residues):
        out_ref[i] = p_ref[pl.ds(i, 2 * residues, stride=2 * residues), :].astype(jnp.bfloat16)


def route(target):
    return [
        (4 * r + 2 * c + q, 4 * to[0] + 2 * to[1] + to[2])
        for r in range(4)
        for c in range(2)
        for q in range(2)
        for to in (target(r, c, q),)
    ]


def direct_shards(
    homolog_embedding,
    homolog_cell_occupancy,
    peptide_occupancy,
    standardize_multiplier,
    standardize_addend,
    lhs_linear_map,
    lhs_linear_constant,
    rhs_linear_map,
    rhs_linear_constant,
    closing_linear_map,
    closing_linear_constant,
):
    sequences, residues, signal = homolog_embedding.shape
    hidden = lhs_linear_map.shape[1]
    width = closing_linear_map.shape[1]
    rows = residues * hidden + MASK_ROWS
    pairs = 4 * residues * residues
    payload = jax.ShapeDtypeStruct((rows, sequences), jnp.bfloat16)
    vmem = pl.BlockSpec(memory_space=pltpu.VMEM)
    in_hbm = pl.BlockSpec(memory_space=pltpu.HBM)
    left, right = pl.pallas_call(
        project_kernel,
        out_shape=(payload, payload),
        in_specs=[in_hbm] * 9,
        out_specs=(vmem, vmem),
        scratch_shapes=[
            pltpu.SMEM((residues,), jnp.int32),
            pltpu.VMEM((sequences * residues, signal), jnp.bfloat16),
            pltpu.VMEM((residues, sequences), jnp.int32),
            pltpu.VMEM((1, signal), jnp.float32),
            pltpu.VMEM((1, signal), jnp.float32),
            pltpu.VMEM((hidden, signal), jnp.bfloat16),
            pltpu.VMEM((1, hidden), jnp.float32),
            pltpu.VMEM((hidden, signal), jnp.bfloat16),
            pltpu.VMEM((1, hidden), jnp.float32),
            pltpu.VMEM((sequences * residues, 128), jnp.float32),
            pltpu.VMEM((rows, sequences), jnp.float32),
            pltpu.SemaphoreType.DMA((4,)),
            pltpu.SemaphoreType.DMA((8,)),
        ],
        compiler_params=pltpu.CompilerParams(vmem_limit_bytes=60 * 1024 * 1024),
        name="normalize_and_project",
    )(
        peptide_occupancy,
        homolog_embedding.reshape(sequences * residues, signal),
        homolog_cell_occupancy.T,
        standardize_multiplier.reshape(1, signal),
        standardize_addend.reshape(1, signal),
        lhs_linear_map.T,
        lhs_linear_constant.reshape(1, hidden),
        rhs_linear_map.T,
        rhs_linear_constant.reshape(1, hidden),
    )
    far = lax.ppermute(right, GROUP, route(lambda r, c, q: (r ^ 2, c, q)))
    first = lax.ppermute(left, GROUP, route(lambda r, c, q: (2 * c + r // 2, 1 - r % 2, q)))
    small = pltpu.CompilerParams(vmem_limit_bytes=16 * 1024 * 1024)
    mine = pl.pallas_call(
        hold_kernel,
        out_shape=payload,
        in_specs=[vmem],
        out_specs=vmem,
        compiler_params=small,
        cost_estimate=pl.CostEstimate(flops=0, bytes_accessed=1 << 22, transcendentals=0),
        name="hold",
    )(right)
    held = pl.pallas_call(
        join_kernel,
        out_shape=jax.ShapeDtypeStruct((2,) + payload.shape, jnp.bfloat16),
        in_specs=[vmem] * 2,
        out_specs=vmem,
        compiler_params=small,
        name="join",
    )(mine, far)
    passed = lax.ppermute(held, GROUP, route(lambda r, c, q: (r ^ 1, c, q)))
    second = lax.ppermute(first, GROUP, route(lambda r, c, q: (r, 1 - c, q)))
    weight, bias = pl.pallas_call(
        keep_kernel,
        out_shape=(
            jax.ShapeDtypeStruct((hidden * 128, WIDE * width), jnp.bfloat16),
            jax.ShapeDtypeStruct((1, width), jnp.float32),
        ),
        in_specs=[vmem] * 2,
        out_specs=(vmem,) * 2,
        compiler_params=pltpu.CompilerParams(vmem_limit_bytes=16 * 1024 * 1024),
        cost_estimate=pl.CostEstimate(flops=0, bytes_accessed=1 << 22, transcendentals=0),
        name="keep",
    )(closing_linear_map, closing_linear_constant.reshape(1, width))

    def pair_sums(own, kind):
        return pl.pallas_call(
            lambda *refs: pair_kernel(own, *refs),
            out_shape=jax.ShapeDtypeStruct((pairs + 2 * MASK_ROWS, width), kind),
            in_specs=[vmem] * 6,
            out_specs=vmem,
            scratch_shapes=[
                pltpu.VMEM((2, rows, sequences), jnp.bfloat16),
                pltpu.VMEM((4, rows, sequences), jnp.bfloat16),
                pltpu.VMEM((pairs // WIDE, hidden * 128), jnp.bfloat16),
            ],
            compiler_params=pltpu.CompilerParams(vmem_limit_bytes=24 * 1024 * 1024),
            cost_estimate=pl.CostEstimate(
                flops=2 * pairs * hidden * 128 * width, bytes_accessed=1 << 20, transcendentals=0
            ),
            name="own_pair_sums" if own else "other_pair_sums",
        )(second, first, held, passed, weight, bias)

    theirs = pair_sums(False, jnp.bfloat16)
    received = lax.ppermute(theirs, GROUP, route(lambda r, c, q: (r, c, 1 - q)))
    mine = pair_sums(True, jnp.float32)
    return pl.pallas_call(
        finish_kernel,
        out_shape=jax.ShapeDtypeStruct((2 * residues, 2 * residues, width), jnp.bfloat16),
        in_specs=[vmem] * 2,
        out_specs=vmem,
        scratch_shapes=[
            pltpu.VMEM((pairs, 128), jnp.bfloat16),
            pltpu.VMEM((pairs, width), jnp.float32),
        ],
        compiler_params=pltpu.CompilerParams(vmem_limit_bytes=16 * 1024 * 1024),
        name="divide",
    )(mine, received)


def shards(*arrays):
    sizes = tuple(lax.axis_size(name) for name in GROUP)
    if sizes == (4, 2, 2) and arrays[0].shape[:2] == (128, 8):
        return direct_shards(*arrays)
    return general_shards(*arrays)


def solution(mesh):
    return jax.shard_map(
        shards,
        mesh=mesh,
        in_specs=(
            P(("crops", "seq"), ("col", "row"), None),
            P(("crops", "seq"), ("col", "row")),
            P(("crops", "col", "row")),
            P(),
            P(),
            P(),
            P(),
            P(),
            P(),
            P(),
            P(),
        ),
        out_specs=P(("crops", "row"), ("col", "seq"), None),
        check_vma=False,
    )
```

```python
import math

import jax
import jax.numpy as jnp
from jax import lax
from jax.experimental import pallas as pl
from jax.experimental.pallas import tpu as pltpu
from jax.sharding import PartitionSpec as P

GROUP = ("row", "col", "seq")
NT = (((1,), (1,)), ((), ()))
MASK_ROWS = 16
WIDE = 4


def from_root(x, axis, root):
    mine = lax.axis_index(axis) == root
    return lax.psum(jnp.where(mine, x, jnp.zeros_like(x)), axis)


def project_side(normed, occupied_indicator, weight, bias):
    seq_count, res_count, width = normed.shape
    report_text = jnp.dot(
        normed.reshape(seq_count * res_count, width), weight, preferred_element_type=jnp.float32
    )
    report_text = (report_text + bias).reshape(seq_count, res_count, -1) * occupied_indicator[
        :, :, None
    ]
    return report_text.astype(jnp.bfloat16)


def pair_rows(left, right, closing_linear_map):
    row_count = left.shape[1]
    col_count = right.shape[1]
    block_rows = math.gcd(row_count, max(1, 512 // col_count))
    weight_f32 = closing_linear_map.astype(jnp.float32)

    def project_block(first_row):
        left_block = lax.dynamic_slice_in_dim(left, first_row, block_rows, 1)
        outer_prod = jnp.einsum(
            "sic,sjd->ijcd", left_block, right, preferred_element_type=jnp.float32
        )
        flattened = outer_prod.reshape(block_rows * col_count, -1)
        result = jnp.dot(flattened, weight_f32, precision=lax.Precision.HIGHEST)
        return result.reshape(block_rows, col_count, -1)

    starts = jnp.arange(row_count // block_rows) * block_rows
    return lax.map(project_block, starts).reshape(row_count, col_count, -1)


def general_shards(
    homolog_embedding,
    homolog_cell_occupancy,
    peptide_occupancy,
    standardize_multiplier,
    standardize_addend,
    lhs_linear_map,
    lhs_linear_constant,
    rhs_linear_map,
    rhs_linear_constant,
    closing_linear_map,
    closing_linear_constant,
):
    occupied_indicator = (homolog_cell_occupancy * peptide_occupancy[None, :]).astype(jnp.float32)
    report_text = homolog_embedding.astype(jnp.float32)
    average = jnp.mean(report_text, axis=-1, keepdims=True)
    spread = jnp.mean(jnp.square(report_text - average), axis=-1, keepdims=True)
    normed = (
        (report_text - average) * lax.rsqrt(spread + 1e-05) * standardize_multiplier
        + standardize_addend
    ).astype(jnp.bfloat16)
    left = project_side(normed, occupied_indicator, lhs_linear_map, lhs_linear_constant)
    right = project_side(normed, occupied_indicator, rhs_linear_map, rhs_linear_constant)
    mask_bf = occupied_indicator.astype(jnp.bfloat16)
    left_col, right_col, mask_col = (
        lax.all_gather(left, "row", axis=1, tiled=True),
        lax.all_gather(right, "row", axis=1, tiled=True),
        lax.all_gather(mask_bf, "row", axis=1, tiled=True),
    )
    row_devices = lax.axis_size("row")
    col_devices = lax.axis_size("col")
    col_len = left_col.shape[1]
    row_len = col_len * col_devices // row_devices
    row_index = lax.axis_index("row")
    root_col = row_index * col_devices // row_devices
    offset = row_index * row_len % col_len
    whole_left, whole_mask = (
        from_root(left_col, "col", root_col),
        from_root(mask_col, "col", root_col),
    )
    left_row = lax.dynamic_slice_in_dim(whole_left, offset, row_len, 1)
    mask_row = lax.dynamic_slice_in_dim(whole_mask, offset, row_len, 1)
    partial_value = pair_rows(left_row, right_col, closing_linear_map)
    mask_rows_all, mask_cols_all = (
        lax.all_gather(mask_row, "seq", axis=0, tiled=True),
        lax.all_gather(mask_col, "seq", axis=0, tiled=True),
    )
    counts_full = jnp.dot(mask_rows_all.T, mask_cols_all, preferred_element_type=jnp.float32)
    summed = lax.psum_scatter(
        partial_value.astype(jnp.bfloat16), "seq", scatter_dimension=1, tiled=True
    ).astype(jnp.float32)
    seq_devices = lax.axis_size("seq")
    part_cols = col_len // seq_devices
    counts = lax.dynamic_slice_in_dim(counts_full, lax.axis_index("seq") * part_cols, part_cols, 1)
    return ((summed + closing_linear_constant) / jnp.maximum(counts, 1.0)[:, :, None]).astype(
        jnp.bfloat16
    )


def project_kernel(
    pept_hbm, x_hbm, occ_hbm, gain_hbm, shift_hbm, wl_hbm, bl_hbm, wr_hbm, br_hbm,
    left_ref, right_ref,
    pept_ref, x_ref, occ_ref, gain_ref, shift_ref, wl_ref, bl_ref, wr_ref, br_ref,
    y_ref, l_ref, x_sems, sems,
):
    residues, sequences = occ_ref.shape
    hidden = wl_ref.shape[0]
    chunks = x_sems.shape[0]
    size = x_ref.shape[0] // chunks
    x_copies = [
        pltpu.make_async_copy(
            x_hbm.at[pl.ds(n * size, size)], x_ref.at[pl.ds(n * size, size)], x_sems.at[n]
        )
        for n in range(chunks)
    ]
    pairs = (
        (wl_hbm, wl_ref), (wr_hbm, wr_ref), (gain_hbm, gain_ref), (shift_hbm, shift_ref),
        (bl_hbm, bl_ref), (br_hbm, br_ref), (occ_hbm, occ_ref), (pept_hbm, pept_ref),
    )
    copies = [pltpu.make_async_copy(a, b, sems.at[n]) for n, (a, b) in enumerate(pairs)]
    x_copies[0].start()
    for copy in copies:
        copy.start()
    for copy in x_copies[1:]:
        copy.start()
    for copy in copies:
        copy.wait()
    weight = jnp.concatenate([wl_ref[...], wr_ref[...]], axis=0)
    bias = jnp.concatenate([bl_ref[...], br_ref[...]], axis=1)
    for n, copy in enumerate(x_copies):
        copy.wait()
        x = x_ref[n * size : (n + 1) * size, :].astype(jnp.float32)
        average = jnp.mean(x, axis=-1, keepdims=True)
        centred = x - average
        spread = jnp.mean(jnp.square(centred), axis=-1, keepdims=True)
        normed = (centred * lax.rsqrt(spread + 1e-05) * gain_ref[...] + shift_ref[...]).astype(
            jnp.bfloat16
        )
        y = lax.dot_general(normed, weight, NT, preferred_element_type=jnp.float32) + bias
        y_ref[n * size : (n + 1) * size, : 2 * hidden] = y
    for i in range(residues):
        live = (occ_ref[i : i + 1, :] * pept_ref[i]).astype(jnp.float32)
        part = y_ref[pl.ds(i, sequences, stride=residues), :].T[: 2 * hidden] * live
        l_ref[pl.ds(i, hidden, stride=residues), :] = part[:hidden]
        right_ref[i * hidden : (i + 1) * hidden, :] = part[hidden:].astype(jnp.bfloat16)
        l_ref[hidden * residues + i : hidden * residues + i + 1, :] = live
    l_ref[hidden * residues + residues :, :] = jnp.zeros((MASK_ROWS - residues, sequences), jnp.float32)
    left_ref[...] = l_ref[...].astype(jnp.bfloat16)
    right_ref[hidden * residues :, :] = l_ref[hidden * residues :, :].astype(jnp.bfloat16)


def expand(tile, store, hidden, wide):
    rows, lanes = tile.shape
    per_vector = 128 // hidden
    lane = lax.broadcasted_iota(jnp.int32, (rows, 128), 1) // (hidden * wide)
    for g in range(lanes // 128):
        part = tile[:, g * 128 : (g + 1) * 128]
        for a in range(per_vector // wide):
            first = (g * (per_vector // wide) + a) * rows
            store(first, part * (lane == a).astype(jnp.bfloat16))


def hold_kernel(right_ref, out_ref):
    out_ref[...] = right_ref[...]


def join_kernel(right_ref, far_ref, out_ref):
    out_ref[0] = right_ref[...]
    out_ref[1] = far_ref[...]


def keep_kernel(w_ref, b_ref, w_out, b_out):
    hidden = 32
    b_out[...] = b_ref[...]
    width = b_ref.shape[1]
    zero = jnp.zeros((hidden, width), jnp.bfloat16)
    for c in range(hidden):
        block = w_ref[c * hidden : (c + 1) * hidden, :]
        for a in range(128 // hidden):
            for n in range(WIDE):
                w_out[c * 128 + a * hidden : c * 128 + (a + 1) * hidden, n * width : (n + 1) * width] = (
                    block if a % WIDE == n else zero
                )


def pair_kernel(
    own, l0, l1, held, passed, w_ref, b_ref, out_ref, ls_ref, rs_ref, big_ref
):
    body = l0.shape[0] - MASK_ROWS
    hidden = 32
    residues = body // hidden
    row, col, seq = (lax.axis_index(name) for name in GROUP)
    for k, piece in enumerate((l0, l1)):
        ls_ref[col ^ k] = piece[...]
    for k in range(2):
        rs_ref[row ^ (2 * k)] = held[k]
        rs_ref[row ^ (2 * k + 1)] = passed[k]
    half = 2 * (seq if own else 1 - seq)

    def rows(ref, at, first, last):
        return jnp.concatenate([ref[at + p, first:last, :] for p in range(2)], axis=0)

    outer = lax.dot_general(
        rows(ls_ref, 0, 0, body), rows(rs_ref, half, 0, body), NT, preferred_element_type=jnp.float32
    )
    live_i = rows(ls_ref, 0, body, body + MASK_ROWS)
    live_j = rows(rs_ref, half, body, body + MASK_ROWS)
    live_j = jnp.concatenate([live_j, jnp.zeros((128 - 2 * MASK_ROWS, live_j.shape[1]), live_j.dtype)], axis=0)
    counts = lax.dot_general(live_i, live_j, NT, preferred_element_type=jnp.float32)
    for c in range(hidden):
        tile = jnp.concatenate(
            [outer[p * body + c * residues : p * body + (c + 1) * residues] for p in range(2)], axis=0
        ).astype(jnp.bfloat16)

        def store(first, value, c=c):
            big_ref[first : first + 2 * residues, c * 128 : (c + 1) * 128] = value

        expand(tile, store, hidden, WIDE)
    pairs = 4 * residues * residues
    projected = jnp.dot(big_ref[...], w_ref[...], preferred_element_type=jnp.float32)
    width = b_ref.shape[1]
    size = 2 * residues
    for g in range(pairs // (size * WIDE)):
        for n in range(WIDE):
            part = projected[g * size : (g + 1) * size, n * width : (n + 1) * width]
            if own:
                part = part + b_ref[...]
            first = (g * WIDE + n) * size
            out_ref[first : first + size, :] = part.astype(out_ref.dtype)
    out_ref[pairs:, :] = counts.astype(out_ref.dtype)


def finish_kernel(mine_ref, other_ref, out_ref, big_ref, p_ref):
    residues = out_ref.shape[0] // 2
    pairs = 4 * residues * residues
    hidden = 32
    counts = mine_ref[pairs:, :] + other_ref[pairs:, :].astype(jnp.float32)
    spread_shape = (128, 2 * residues * hidden)
    at_row = lax.broadcasted_iota(jnp.int32, spread_shape, 0)
    at_lane = lax.broadcasted_iota(jnp.int32, spread_shape, 1)
    hit = ((at_row // MASK_ROWS) * residues + at_row % MASK_ROWS == at_lane // hidden) & (
        at_row % MASK_ROWS < residues
    )
    counts = jnp.dot(
        counts.astype(jnp.bfloat16), hit.astype(jnp.bfloat16), preferred_element_type=jnp.float32
    )
    tile = jnp.concatenate(
        [counts[p * MASK_ROWS : p * MASK_ROWS + residues] for p in range(2)], axis=0
    ).astype(jnp.bfloat16)

    def store(first, value):
        big_ref[first : first + 2 * residues, :] = value

    expand(tile, store, hidden, 1)
    share = jnp.full((128, 128), 1.0 / hidden, jnp.bfloat16)
    divisor = jnp.dot(big_ref[...], share, preferred_element_type=jnp.float32)
    total = mine_ref[:pairs, :] + other_ref[:pairs, :].astype(jnp.float32)
    p_ref[...] = total / jnp.maximum(divisor, 1.0)
    for i in range(2 * residues):
        out_ref[i] = p_ref[pl.ds(i, 2 * residues, stride=2 * residues), :].astype(jnp.bfloat16)


def route(target):
    return [
        (4 * r + 2 * c + q, 4 * to[0] + 2 * to[1] + to[2])
        for r in range(4)
        for c in range(2)
        for q in range(2)
        for to in (target(r, c, q),)
    ]


def direct_shards(
    homolog_embedding,
    homolog_cell_occupancy,
    peptide_occupancy,
    standardize_multiplier,
    standardize_addend,
    lhs_linear_map,
    lhs_linear_constant,
    rhs_linear_map,
    rhs_linear_constant,
    closing_linear_map,
    closing_linear_constant,
):
    sequences, residues, signal = homolog_embedding.shape
    hidden = lhs_linear_map.shape[1]
    width = closing_linear_map.shape[1]
    rows = residues * hidden + MASK_ROWS
    pairs = 4 * residues * residues
    payload = jax.ShapeDtypeStruct((rows, sequences), jnp.bfloat16)
    vmem = pl.BlockSpec(memory_space=pltpu.VMEM)
    in_hbm = pl.BlockSpec(memory_space=pltpu.HBM)
    left, right = pl.pallas_call(
        project_kernel,
        out_shape=(payload, payload),
        in_specs=[in_hbm] * 9,
        out_specs=(vmem, vmem),
        scratch_shapes=[
            pltpu.SMEM((residues,), jnp.int32),
            pltpu.VMEM((sequences * residues, signal), jnp.bfloat16),
            pltpu.VMEM((residues, sequences), jnp.int32),
            pltpu.VMEM((1, signal), jnp.float32),
            pltpu.VMEM((1, signal), jnp.float32),
            pltpu.VMEM((hidden, signal), jnp.bfloat16),
            pltpu.VMEM((1, hidden), jnp.float32),
            pltpu.VMEM((hidden, signal), jnp.bfloat16),
            pltpu.VMEM((1, hidden), jnp.float32),
            pltpu.VMEM((sequences * residues, 128), jnp.float32),
            pltpu.VMEM((rows, sequences), jnp.float32),
            pltpu.SemaphoreType.DMA((8,)),
            pltpu.SemaphoreType.DMA((8,)),
        ],
        compiler_params=pltpu.CompilerParams(vmem_limit_bytes=60 * 1024 * 1024),
        name="normalize_and_project",
    )(
        peptide_occupancy,
        homolog_embedding.reshape(sequences * residues, signal),
        homolog_cell_occupancy.T,
        standardize_multiplier.reshape(1, signal),
        standardize_addend.reshape(1, signal),
        lhs_linear_map.T,
        lhs_linear_constant.reshape(1, hidden),
        rhs_linear_map.T,
        rhs_linear_constant.reshape(1, hidden),
    )
    far = lax.ppermute(right, GROUP, route(lambda r, c, q: (r ^ 2, c, q)))
    first = lax.ppermute(left, GROUP, route(lambda r, c, q: (2 * c + r // 2, 1 - r % 2, q)))
    small = pltpu.CompilerParams(vmem_limit_bytes=16 * 1024 * 1024)
    mine = pl.pallas_call(
        hold_kernel,
        out_shape=payload,
        in_specs=[vmem],
        out_specs=vmem,
        compiler_params=small,
        cost_estimate=pl.CostEstimate(flops=0, bytes_accessed=1 << 22, transcendentals=0),
        name="hold",
    )(right)
    held = pl.pallas_call(
        join_kernel,
        out_shape=jax.ShapeDtypeStruct((2,) + payload.shape, jnp.bfloat16),
        in_specs=[vmem] * 2,
        out_specs=vmem,
        compiler_params=small,
        name="join",
    )(mine, far)
    passed = lax.ppermute(held, GROUP, route(lambda r, c, q: (r ^ 1, c, q)))
    second = lax.ppermute(first, GROUP, route(lambda r, c, q: (r, 1 - c, q)))
    weight, bias = pl.pallas_call(
        keep_kernel,
        out_shape=(
            jax.ShapeDtypeStruct((hidden * 128, WIDE * width), jnp.bfloat16),
            jax.ShapeDtypeStruct((1, width), jnp.float32),
        ),
        in_specs=[vmem] * 2,
        out_specs=(vmem,) * 2,
        compiler_params=pltpu.CompilerParams(vmem_limit_bytes=16 * 1024 * 1024),
        cost_estimate=pl.CostEstimate(flops=0, bytes_accessed=1 << 22, transcendentals=0),
        name="keep",
    )(closing_linear_map, closing_linear_constant.reshape(1, width))

    def pair_sums(own, kind):
        return pl.pallas_call(
            lambda *refs: pair_kernel(own, *refs),
            out_shape=jax.ShapeDtypeStruct((pairs + 2 * MASK_ROWS, width), kind),
            in_specs=[vmem] * 6,
            out_specs=vmem,
            scratch_shapes=[
                pltpu.VMEM((2, rows, sequences), jnp.bfloat16),
                pltpu.VMEM((4, rows, sequences), jnp.bfloat16),
                pltpu.VMEM((pairs // WIDE, hidden * 128), jnp.bfloat16),
            ],
            compiler_params=pltpu.CompilerParams(vmem_limit_bytes=24 * 1024 * 1024),
            cost_estimate=pl.CostEstimate(
                flops=2 * pairs * hidden * 128 * width, bytes_accessed=1 << 20, transcendentals=0
            ),
            name="own_pair_sums" if own else "other_pair_sums",
        )(second, first, held, passed, weight, bias)

    theirs = pair_sums(False, jnp.bfloat16)
    received = lax.ppermute(theirs, GROUP, route(lambda r, c, q: (r, c, 1 - q)))
    mine = pair_sums(True, jnp.float32)
    return pl.pallas_call(
        finish_kernel,
        out_shape=jax.ShapeDtypeStruct((2 * residues, 2 * residues, width), jnp.bfloat16),
        in_specs=[vmem] * 2,
        out_specs=vmem,
        scratch_shapes=[
            pltpu.VMEM((pairs, 128), jnp.bfloat16),
            pltpu.VMEM((pairs, width), jnp.float32),
        ],
        compiler_params=pltpu.CompilerParams(vmem_limit_bytes=16 * 1024 * 1024),
        name="divide",
    )(mine, received)


def shards(*arrays):
    sizes = tuple(lax.axis_size(name) for name in GROUP)
    if sizes == (4, 2, 2) and arrays[0].shape[:2] == (128, 8):
        return direct_shards(*arrays)
    return general_shards(*arrays)


def solution(mesh):
    return jax.shard_map(
        shards,
        mesh=mesh,
        in_specs=(
            P(("crops", "seq"), ("col", "row"), None),
            P(("crops", "seq"), ("col", "row")),
            P(("crops", "col", "row")),
            P(),
            P(),
            P(),
            P(),
            P(),
            P(),
            P(),
            P(),
        ),
        out_specs=P(("crops", "row"), ("col", "seq"), None),
        check_vma=False,
    )
```

```python
import math

import jax
import jax.numpy as jnp
from jax import lax
from jax.experimental import pallas as pl
from jax.experimental.pallas import tpu as pltpu
from jax.sharding import PartitionSpec as P

GROUP = ("row", "col", "seq")
NT = (((1,), (1,)), ((), ()))
MASK_ROWS = 16
WIDE = 2


def from_root(x, axis, root):
    mine = lax.axis_index(axis) == root
    return lax.psum(jnp.where(mine, x, jnp.zeros_like(x)), axis)


def project_side(normed, occupied_indicator, weight, bias):
    seq_count, res_count, width = normed.shape
    report_text = jnp.dot(
        normed.reshape(seq_count * res_count, width), weight, preferred_element_type=jnp.float32
    )
    report_text = (report_text + bias).reshape(seq_count, res_count, -1) * occupied_indicator[
        :, :, None
    ]
    return report_text.astype(jnp.bfloat16)


def pair_rows(left, right, closing_linear_map):
    row_count = left.shape[1]
    col_count = right.shape[1]
    block_rows = math.gcd(row_count, max(1, 512 // col_count))
    weight_f32 = closing_linear_map.astype(jnp.float32)

    def project_block(first_row):
        left_block = lax.dynamic_slice_in_dim(left, first_row, block_rows, 1)
        outer_prod = jnp.einsum(
            "sic,sjd->ijcd", left_block, right, preferred_element_type=jnp.float32
        )
        flattened = outer_prod.reshape(block_rows * col_count, -1)
        result = jnp.dot(flattened, weight_f32, precision=lax.Precision.HIGHEST)
        return result.reshape(block_rows, col_count, -1)

    starts = jnp.arange(row_count // block_rows) * block_rows
    return lax.map(project_block, starts).reshape(row_count, col_count, -1)


def general_shards(
    homolog_embedding,
    homolog_cell_occupancy,
    peptide_occupancy,
    standardize_multiplier,
    standardize_addend,
    lhs_linear_map,
    lhs_linear_constant,
    rhs_linear_map,
    rhs_linear_constant,
    closing_linear_map,
    closing_linear_constant,
):
    occupied_indicator = (homolog_cell_occupancy * peptide_occupancy[None, :]).astype(jnp.float32)
    report_text = homolog_embedding.astype(jnp.float32)
    average = jnp.mean(report_text, axis=-1, keepdims=True)
    spread = jnp.mean(jnp.square(report_text - average), axis=-1, keepdims=True)
    normed = (
        (report_text - average) * lax.rsqrt(spread + 1e-05) * standardize_multiplier
        + standardize_addend
    ).astype(jnp.bfloat16)
    left = project_side(normed, occupied_indicator, lhs_linear_map, lhs_linear_constant)
    right = project_side(normed, occupied_indicator, rhs_linear_map, rhs_linear_constant)
    mask_bf = occupied_indicator.astype(jnp.bfloat16)
    left_col, right_col, mask_col = (
        lax.all_gather(left, "row", axis=1, tiled=True),
        lax.all_gather(right, "row", axis=1, tiled=True),
        lax.all_gather(mask_bf, "row", axis=1, tiled=True),
    )
    row_devices = lax.axis_size("row")
    col_devices = lax.axis_size("col")
    col_len = left_col.shape[1]
    row_len = col_len * col_devices // row_devices
    row_index = lax.axis_index("row")
    root_col = row_index * col_devices // row_devices
    offset = row_index * row_len % col_len
    whole_left, whole_mask = (
        from_root(left_col, "col", root_col),
        from_root(mask_col, "col", root_col),
    )
    left_row = lax.dynamic_slice_in_dim(whole_left, offset, row_len, 1)
    mask_row = lax.dynamic_slice_in_dim(whole_mask, offset, row_len, 1)
    partial_value = pair_rows(left_row, right_col, closing_linear_map)
    mask_rows_all, mask_cols_all = (
        lax.all_gather(mask_row, "seq", axis=0, tiled=True),
        lax.all_gather(mask_col, "seq", axis=0, tiled=True),
    )
    counts_full = jnp.dot(mask_rows_all.T, mask_cols_all, preferred_element_type=jnp.float32)
    summed = lax.psum_scatter(
        partial_value.astype(jnp.bfloat16), "seq", scatter_dimension=1, tiled=True
    ).astype(jnp.float32)
    seq_devices = lax.axis_size("seq")
    part_cols = col_len // seq_devices
    counts = lax.dynamic_slice_in_dim(counts_full, lax.axis_index("seq") * part_cols, part_cols, 1)
    return ((summed + closing_linear_constant) / jnp.maximum(counts, 1.0)[:, :, None]).astype(
        jnp.bfloat16
    )


def project_kernel(
    pept_hbm, x_hbm, occ_hbm, gain_hbm, shift_hbm, wl_hbm, bl_hbm, wr_hbm, br_hbm,
    left_ref, right_ref,
    pept_ref, x_ref, occ_ref, gain_ref, shift_ref, wl_ref, bl_ref, wr_ref, br_ref,
    y_ref, l_ref, x_sems, sems,
):
    residues, sequences = occ_ref.shape
    hidden = wl_ref.shape[0]
    chunks = x_sems.shape[0]
    size = x_ref.shape[0] // chunks
    x_copies = [
        pltpu.make_async_copy(
            x_hbm.at[pl.ds(n * size, size)], x_ref.at[pl.ds(n * size, size)], x_sems.at[n]
        )
        for n in range(chunks)
    ]
    pairs = (
        (wl_hbm, wl_ref), (wr_hbm, wr_ref), (gain_hbm, gain_ref), (shift_hbm, shift_ref),
        (bl_hbm, bl_ref), (br_hbm, br_ref), (occ_hbm, occ_ref), (pept_hbm, pept_ref),
    )
    copies = [pltpu.make_async_copy(a, b, sems.at[n]) for n, (a, b) in enumerate(pairs)]
    for copy in x_copies + copies:
        copy.start()
    for copy in copies:
        copy.wait()
    weight = jnp.concatenate([wl_ref[...], wr_ref[...]], axis=0)
    bias = jnp.concatenate([bl_ref[...], br_ref[...]], axis=1)
    for copy in x_copies:
        copy.wait()
    x = x_ref[...].astype(jnp.float32)
    average = jnp.mean(x, axis=-1, keepdims=True)
    centred = x - average
    spread = jnp.mean(jnp.square(centred), axis=-1, keepdims=True)
    normed = (centred * lax.rsqrt(spread + 1e-05) * gain_ref[...] + shift_ref[...]).astype(
        jnp.bfloat16
    )
    y = lax.dot_general(normed, weight, NT, preferred_element_type=jnp.float32) + bias
    y_ref[:, : 2 * hidden] = y
    for i in range(residues):
        live = (occ_ref[i : i + 1, :] * pept_ref[i]).astype(jnp.float32)
        part = y_ref[pl.ds(i, sequences, stride=residues), :].T[: 2 * hidden] * live
        l_ref[pl.ds(i, hidden, stride=residues), :] = part[:hidden]
        right_ref[i * hidden : (i + 1) * hidden, :] = part[hidden:].astype(jnp.bfloat16)
        l_ref[hidden * residues + i : hidden * residues + i + 1, :] = live
    l_ref[hidden * residues + residues :, :] = jnp.zeros((MASK_ROWS - residues, sequences), jnp.float32)
    left_ref[...] = l_ref[...].astype(jnp.bfloat16)
    right_ref[hidden * residues :, :] = l_ref[hidden * residues :, :].astype(jnp.bfloat16)


def expand(tile, store, hidden, wide):
    rows, lanes = tile.shape
    per_vector = 128 // hidden
    lane = lax.broadcasted_iota(jnp.int32, (rows, 128), 1) // (hidden * wide)
    for g in range(lanes // 128):
        part = tile[:, g * 128 : (g + 1) * 128]
        for a in range(per_vector // wide):
            first = (g * (per_vector // wide) + a) * rows
            store(first, part * (lane == a).astype(jnp.bfloat16))


def hold_kernel(right_ref, out_ref):
    out_ref[...] = right_ref[...]


def join_kernel(right_ref, far_ref, out_ref):
    out_ref[0] = right_ref[...]
    out_ref[1] = far_ref[...]


def keep_kernel(w_ref, b_ref, w_out, b_out):
    hidden = 32
    b_out[...] = b_ref[...]
    width = b_ref.shape[1]
    zero = jnp.zeros((hidden, width), jnp.bfloat16)
    for c in range(hidden):
        block = w_ref[c * hidden : (c + 1) * hidden, :]
        for a in range(128 // hidden):
            for n in range(WIDE):
                w_out[c * 128 + a * hidden : c * 128 + (a + 1) * hidden, n * width : (n + 1) * width] = (
                    block if a % WIDE == n else zero
                )


def pair_kernel(
    own, l0, l1, held, passed, w_ref, b_ref, out_ref, ls_ref, rs_ref, big_ref
):
    body = l0.shape[0] - MASK_ROWS
    hidden = 32
    residues = body // hidden
    row, col, seq = (lax.axis_index(name) for name in GROUP)
    for k, piece in enumerate((l0, l1)):
        ls_ref[col ^ k] = piece[...]
    for k in range(2):
        rs_ref[row ^ (2 * k)] = held[k]
        rs_ref[row ^ (2 * k + 1)] = passed[k]
    half = 2 * (seq if own else 1 - seq)

    def rows(ref, at, first, last):
        return jnp.concatenate([ref[at + p, first:last, :] for p in range(2)], axis=0)

    outer = lax.dot_general(
        rows(ls_ref, 0, 0, body), rows(rs_ref, half, 0, body), NT, preferred_element_type=jnp.float32
    )
    live_i = rows(ls_ref, 0, body, body + MASK_ROWS)
    live_j = rows(rs_ref, half, body, body + MASK_ROWS)
    live_j = jnp.concatenate([live_j, jnp.zeros((128 - 2 * MASK_ROWS, live_j.shape[1]), live_j.dtype)], axis=0)
    counts = lax.dot_general(live_i, live_j, NT, preferred_element_type=jnp.float32)
    for c in range(hidden):
        tile = jnp.concatenate(
            [outer[p * body + c * residues : p * body + (c + 1) * residues] for p in range(2)], axis=0
        ).astype(jnp.bfloat16)

        def store(first, value, c=c):
            big_ref[first : first + 2 * residues, c * 128 : (c + 1) * 128] = value

        expand(tile, store, hidden, WIDE)
    pairs = 4 * residues * residues
    projected = jnp.dot(big_ref[...], w_ref[...], preferred_element_type=jnp.float32)
    width = b_ref.shape[1]
    size = 2 * residues
    for g in range(pairs // (size * WIDE)):
        for n in range(WIDE):
            part = projected[g * size : (g + 1) * size, n * width : (n + 1) * width]
            if own:
                part = part + b_ref[...]
            first = (g * WIDE + n) * size
            out_ref[first : first + size, :] = part.astype(out_ref.dtype)
    out_ref[pairs:, :] = counts.astype(out_ref.dtype)


def finish_kernel(mine_ref, other_ref, out_ref, big_ref, p_ref):
    residues = out_ref.shape[0] // 2
    pairs = 4 * residues * residues
    hidden = 32
    counts = mine_ref[pairs:, :] + other_ref[pairs:, :].astype(jnp.float32)
    spread_shape = (128, 2 * residues * hidden)
    at_row = lax.broadcasted_iota(jnp.int32, spread_shape, 0)
    at_lane = lax.broadcasted_iota(jnp.int32, spread_shape, 1)
    hit = ((at_row // MASK_ROWS) * residues + at_row % MASK_ROWS == at_lane // hidden) & (
        at_row % MASK_ROWS < residues
    )
    counts = jnp.dot(
        counts.astype(jnp.bfloat16), hit.astype(jnp.bfloat16), preferred_element_type=jnp.float32
    )
    tile = jnp.concatenate(
        [counts[p * MASK_ROWS : p * MASK_ROWS + residues] for p in range(2)], axis=0
    ).astype(jnp.bfloat16)

    def store(first, value):
        big_ref[first : first + 2 * residues, :] = value

    expand(tile, store, hidden, 1)
    share = jnp.full((128, 128), 1.0 / hidden, jnp.bfloat16)
    divisor = jnp.dot(big_ref[...], share, preferred_element_type=jnp.float32)
    total = mine_ref[:pairs, :] + other_ref[:pairs, :].astype(jnp.float32)
    p_ref[...] = total / jnp.maximum(divisor, 1.0)
    for i in range(2 * residues):
        out_ref[i] = p_ref[pl.ds(i, 2 * residues, stride=2 * residues), :].astype(jnp.bfloat16)


def route(target):
    return [
        (4 * r + 2 * c + q, 4 * to[0] + 2 * to[1] + to[2])
        for r in range(4)
        for c in range(2)
        for q in range(2)
        for to in (target(r, c, q),)
    ]


def direct_shards(
    homolog_embedding,
    homolog_cell_occupancy,
    peptide_occupancy,
    standardize_multiplier,
    standardize_addend,
    lhs_linear_map,
    lhs_linear_constant,
    rhs_linear_map,
    rhs_linear_constant,
    closing_linear_map,
    closing_linear_constant,
):
    sequences, residues, signal = homolog_embedding.shape
    hidden = lhs_linear_map.shape[1]
    width = closing_linear_map.shape[1]
    rows = residues * hidden + MASK_ROWS
    pairs = 4 * residues * residues
    payload = jax.ShapeDtypeStruct((rows, sequences), jnp.bfloat16)
    vmem = pl.BlockSpec(memory_space=pltpu.VMEM)
    in_hbm = pl.BlockSpec(memory_space=pltpu.HBM)
    left, right = pl.pallas_call(
        project_kernel,
        out_shape=(payload, payload),
        in_specs=[in_hbm] * 9,
        out_specs=(vmem, vmem),
        scratch_shapes=[
            pltpu.SMEM((residues,), jnp.int32),
            pltpu.VMEM((sequences * residues, signal), jnp.bfloat16),
            pltpu.VMEM((residues, sequences), jnp.int32),
            pltpu.VMEM((1, signal), jnp.float32),
            pltpu.VMEM((1, signal), jnp.float32),
            pltpu.VMEM((hidden, signal), jnp.bfloat16),
            pltpu.VMEM((1, hidden), jnp.float32),
            pltpu.VMEM((hidden, signal), jnp.bfloat16),
            pltpu.VMEM((1, hidden), jnp.float32),
            pltpu.VMEM((sequences * residues, 128), jnp.float32),
            pltpu.VMEM((rows, sequences), jnp.float32),
            pltpu.SemaphoreType.DMA((4,)),
            pltpu.SemaphoreType.DMA((8,)),
        ],
        compiler_params=pltpu.CompilerParams(vmem_limit_bytes=60 * 1024 * 1024),
        name="normalize_and_project",
    )(
        peptide_occupancy,
        homolog_embedding.reshape(sequences * residues, signal),
        homolog_cell_occupancy.T,
        standardize_multiplier.reshape(1, signal),
        standardize_addend.reshape(1, signal),
        lhs_linear_map.T,
        lhs_linear_constant.reshape(1, hidden),
        rhs_linear_map.T,
        rhs_linear_constant.reshape(1, hidden),
    )
    far = lax.ppermute(right, GROUP, route(lambda r, c, q: (r ^ 2, c, q)))
    first = lax.ppermute(left, GROUP, route(lambda r, c, q: (2 * c + r // 2, 1 - r % 2, q)))
    small = pltpu.CompilerParams(vmem_limit_bytes=16 * 1024 * 1024)
    mine = pl.pallas_call(
        hold_kernel,
        out_shape=payload,
        in_specs=[vmem],
        out_specs=vmem,
        compiler_params=small,
        cost_estimate=pl.CostEstimate(flops=0, bytes_accessed=1 << 22, transcendentals=0),
        name="hold",
    )(right)
    held = pl.pallas_call(
        join_kernel,
        out_shape=jax.ShapeDtypeStruct((2,) + payload.shape, jnp.bfloat16),
        in_specs=[vmem] * 2,
        out_specs=vmem,
        compiler_params=small,
        name="join",
    )(mine, far)
    passed = lax.ppermute(held, GROUP, route(lambda r, c, q: (r ^ 1, c, q)))
    second = lax.ppermute(first, GROUP, route(lambda r, c, q: (r, 1 - c, q)))
    weight, bias = pl.pallas_call(
        keep_kernel,
        out_shape=(
            jax.ShapeDtypeStruct((hidden * 128, WIDE * width), jnp.bfloat16),
            jax.ShapeDtypeStruct((1, width), jnp.float32),
        ),
        in_specs=[vmem] * 2,
        out_specs=(vmem,) * 2,
        compiler_params=pltpu.CompilerParams(vmem_limit_bytes=16 * 1024 * 1024),
        cost_estimate=pl.CostEstimate(flops=0, bytes_accessed=1 << 22, transcendentals=0),
        name="keep",
    )(closing_linear_map, closing_linear_constant.reshape(1, width))

    def pair_sums(own, kind):
        return pl.pallas_call(
            lambda *refs: pair_kernel(own, *refs),
            out_shape=jax.ShapeDtypeStruct((pairs + 2 * MASK_ROWS, width), kind),
            in_specs=[vmem] * 6,
            out_specs=vmem,
            scratch_shapes=[
                pltpu.VMEM((2, rows, sequences), jnp.bfloat16),
                pltpu.VMEM((4, rows, sequences), jnp.bfloat16),
                pltpu.VMEM((pairs // WIDE, hidden * 128), jnp.bfloat16),
            ],
            compiler_params=pltpu.CompilerParams(vmem_limit_bytes=24 * 1024 * 1024),
            cost_estimate=pl.CostEstimate(
                flops=2 * pairs * hidden * 128 * width, bytes_accessed=1 << 20, transcendentals=0
            ),
            name="own_pair_sums" if own else "other_pair_sums",
        )(second, first, held, passed, weight, bias)

    theirs = pair_sums(False, jnp.bfloat16)
    received = lax.ppermute(theirs, GROUP, route(lambda r, c, q: (r, c, 1 - q)))
    mine = pair_sums(True, jnp.float32)
    return pl.pallas_call(
        finish_kernel,
        out_shape=jax.ShapeDtypeStruct((2 * residues, 2 * residues, width), jnp.bfloat16),
        in_specs=[vmem] * 2,
        out_specs=vmem,
        scratch_shapes=[
            pltpu.VMEM((pairs, 128), jnp.bfloat16),
            pltpu.VMEM((pairs, width), jnp.float32),
        ],
        compiler_params=pltpu.CompilerParams(vmem_limit_bytes=16 * 1024 * 1024),
        name="divide",
    )(mine, received)


def shards(*arrays):
    sizes = tuple(lax.axis_size(name) for name in GROUP)
    if sizes == (4, 2, 2) and arrays[0].shape[:2] == (128, 8):
        return direct_shards(*arrays)
    return general_shards(*arrays)


def solution(mesh):
    return jax.shard_map(
        shards,
        mesh=mesh,
        in_specs=(
            P(("crops", "seq"), ("col", "row"), None),
            P(("crops", "seq"), ("col", "row")),
            P(("crops", "col", "row")),
            P(),
            P(),
            P(),
            P(),
            P(),
            P(),
            P(),
            P(),
        ),
        out_specs=P(("crops", "row"), ("col", "seq"), None),
        check_vma=False,
    )
```
